32 devices in a mesh: img: 4 (over z), txt: 8 (over y, x, core).
Axes of the slice: x: 2, y: 2, z: 4, core: 2. Of those that a mesh axis runs over, the one named last changes fastest.
Arguments:
- teacher_image: bfloat16 [4096, 1280], P(('img', 'txt')), may hold values from -24 to 24
- teacher_text: bfloat16 [4096, 1280], P(('txt', 'img')), may hold values from -24 to 24
- student_image: bfloat16 [4096, 512], P(('img', 'txt')), may hold values from -24 to 24
- student_text: bfloat16 [4096, 512], P(('txt', 'img')), may hold values from -24 to 24
Outputs:
- loss: float32 [], replicated
- image_grad: float32 [4096, 512], P(('img', 'txt'))
- text_grad: float32 [4096, 512], P(('txt', 'img'))
The draws below stay inside these ranges and needn't reach their ends.
All inputs are finite; a program needn't handle non-finite values.
Results may differ from the reference program's by a relative error of at most 0.0012.
Values may be sent and summed in bfloat16 or wider, within the bound.
No kernel may reach another device: no remote copies, remote signals or barrier semaphores. Data moves between devices by JAX's collectives and lax.ppermute only.
A program may use at most 128 MiB of HBM per device.

```python
import math
import jax
import jax.numpy as jnp
from jax import lax

TWIDTH = 1280
SWIDTH = 512
PAIRS = 4096


def pair_rows(key, side, ramp):
    key = jax.random.fold_in(key, 11 + side)
    key_normal = jax.random.fold_in(key, 0)
    key_scale = jax.random.fold_in(key, 2)
    key_extra = jax.random.fold_in(key, 3)
    normal_part = jax.random.truncated_normal(key_normal, -4.0, 4.0, (PAIRS, TWIDTH), jnp.float32)
    field = normal_part
    position = jnp.arange(PAIRS, dtype=jnp.float32) / PAIRS
    spread = jnp.exp(jax.random.uniform(key_scale, (PAIRS, 1), jnp.float32, math.log(0.5), math.log(1.6)))
    scales = spread * (1.0 + ramp * position)[:, None]
    extra = jax.random.truncated_normal(key_extra, -4.0, 4.0, (PAIRS, SWIDTH), jnp.float32)
    return (field * scales, scales * (0.8 * field[:, :SWIDTH] + 0.6 * extra))


def draw_teacher_image(key, part):
    teacher_rows, student_rows = pair_rows(key, 0, 0.5)
    return teacher_rows.astype(jnp.bfloat16)


def draw_student_image(key, part):
    teacher_rows, student_rows = pair_rows(key, 0, 0.5)
    return student_rows.astype(jnp.bfloat16)


def draw_teacher_text(key, part):
    teacher_rows, student_rows = pair_rows(key, 1, 0.5)
    return teacher_rows.astype(jnp.bfloat16)


def draw_student_text(key, part):
    teacher_rows, student_rows = pair_rows(key, 1, 0.5)
    return student_rows.astype(jnp.bfloat16)


def setup_inputs(seed: int = 0) -> dict:
    splits = jax.random.split(jax.random.key(seed), 5)
    teacher_image = draw_teacher_image(jax.random.fold_in(splits[4], 71), 0)
    teacher_text = draw_teacher_text(jax.random.fold_in(splits[4], 71), 0)
    student_image = draw_student_image(jax.random.fold_in(splits[4], 71), 0)
    student_text = draw_student_text(jax.random.fold_in(splits[4], 71), 0)
    return dict(teacher_image=teacher_image, teacher_text=teacher_text, student_image=student_image, student_text=student_text)


def both_logits(image_teacher, image_student, text_teacher, text_student):
    teacher_logit = jnp.dot(image_teacher, text_teacher.T, preferred_element_type=jnp.float32) * (TWIDTH ** -0.5)
    student_logit = jnp.dot(image_student, text_student.T, preferred_element_type=jnp.float32) * (SWIDTH ** -0.5)
    return teacher_logit, student_logit


def row_logsumexp(logit):
    highest = jnp.max(logit, axis=1)
    return highest + jnp.log(jnp.sum(jnp.exp(logit - highest[:, None]), axis=1))


def fold_columns(column_peak, column_total, logit):
    new_peak = jnp.maximum(column_peak, jnp.max(logit, axis=0))
    new_total = column_total * jnp.exp(column_peak - new_peak) + jnp.sum(jnp.exp(logit - new_peak[None, :]), axis=0)
    return new_peak, new_total


def split_delta(delta):
    delta_high = delta.astype(jnp.bfloat16)
    widened = lax.optimization_barrier(delta_high).astype(jnp.float32)
    delta_low = (delta - widened).astype(jnp.bfloat16)
    return delta_high, delta_low


def reference(teacher_image, teacher_text, student_image, student_text):
    block_rows = min(1024, PAIRS)
    blocks = PAIRS // block_rows
    image_teacher = teacher_image.reshape(blocks, block_rows, TWIDTH)
    image_student = student_image.reshape(blocks, block_rows, SWIDTH)

    def gather_stats(running, pieces):
        peak_teacher, total_teacher, peak_student, total_student = running
        teacher_logit, student_logit = both_logits(pieces[0], pieces[1], teacher_text, student_text)
        peak_teacher, total_teacher = fold_columns(peak_teacher, total_teacher, teacher_logit)
        peak_student, total_student = fold_columns(peak_student, total_student, student_logit)
        return (peak_teacher, total_teacher, peak_student, total_student), (row_logsumexp(teacher_logit), row_logsumexp(student_logit))

    empty_peak = jnp.full((PAIRS,), -jnp.inf, jnp.float32)
    empty_total = jnp.zeros((PAIRS,), jnp.float32)
    running, row_parts = lax.scan(gather_stats, (empty_peak, empty_total, empty_peak, empty_total), (image_teacher, image_student))
    teacher_column_lse = running[0] + jnp.log(running[1])
    student_column_lse = running[2] + jnp.log(running[3])
    teacher_row_lse = row_parts[0].reshape(PAIRS)
    student_row_lse = row_parts[1].reshape(PAIRS)

    def gradient_pass(running, pieces):
        text_total, divergence = running
        block_teacher, block_student, lse_teacher, lse_student = pieces
        teacher_logit, student_logit = both_logits(block_teacher, block_student, teacher_text, student_text)
        teacher_row_prob = jnp.exp(teacher_logit - lse_teacher[:, None])
        student_row_prob = jnp.exp(student_logit - lse_student[:, None])
        teacher_column_prob = jnp.exp(teacher_logit - teacher_column_lse[None, :])
        student_column_prob = jnp.exp(student_logit - student_column_lse[None, :])
        difference = teacher_logit - student_logit
        divergence = divergence + jnp.sum(teacher_row_prob * difference) + jnp.sum(teacher_column_prob * difference)
        delta = (student_row_prob - teacher_row_prob) + (student_column_prob - teacher_column_prob)
        delta_high, delta_low = split_delta(delta)
        image_part = jnp.dot(delta_high, student_text, preferred_element_type=jnp.float32) + jnp.dot(delta_low, student_text, preferred_element_type=jnp.float32)
        text_total = text_total + jnp.dot(delta_high.T, block_student, preferred_element_type=jnp.float32) + jnp.dot(delta_low.T, block_student, preferred_element_type=jnp.float32)
        return (text_total, divergence), image_part

    start = (jnp.zeros((PAIRS, SWIDTH), jnp.float32), jnp.zeros((), jnp.float32))
    finished, image_parts = lax.scan(gradient_pass, start, (image_teacher, image_student, teacher_row_lse.reshape(blocks, block_rows), student_row_lse.reshape(blocks, block_rows)))
    text_total, divergence = finished
    total = divergence + jnp.sum(student_row_lse - teacher_row_lse) + jnp.sum(student_column_lse - teacher_column_lse)
    loss = total / (2.0 * PAIRS)
    image_grad = image_parts.reshape(PAIRS, SWIDTH) * (SWIDTH ** -0.5)
    text_grad = text_total * (SWIDTH ** -0.5)
    return loss, image_grad, text_grad
```

```python
import functools

import jax
import jax.numpy as jnp
import numpy as np
from jax import lax
from jax.experimental import pallas as pl
from jax.experimental.pallas import tpu as pltpu
from jax.sharding import Mesh, PartitionSpec as P

F32 = jnp.float32
BF16 = jnp.bfloat16
LINES = 8
EXTRA = 8
PARAMS = pltpu.CompilerParams(vmem_limit_bytes=56 * 2**20)
VMEM = pl.BlockSpec(memory_space=pltpu.VMEM)
SMEM = pl.BlockSpec(memory_space=pltpu.SMEM)


def matmul(a, b, da, db):
    return lax.dot_general(a, b, (((da,), (db,)), ((), ())), preferred_element_type=F32)


def pack_lines(values, shape, axis):
    index = lax.broadcasted_iota(jnp.int32, shape, axis)
    out = jnp.zeros(shape, F32)
    for k, value in enumerate(values):
        out = jnp.where(index == k, value, out)
    return out


def stats_kernel(cfg, rank, *refs):
    nr, nc, b, tw, scale_t, scale_s = cfg
    images, texts = refs[:nr], refs[nr : nr + nc]
    tl_ref, sl_ref, row_ref, col_ref, text = refs[nr + nc :]
    for p in range(nc):
        text[p * b : (p + 1) * b, :] = texts[p][...]
    step = 2 if nr % 2 == 0 else 1
    count = step * b
    peak_t = peak_s = None
    for p in range(0, nr, step):
        block = jnp.concatenate([images[p + k][...] for k in range(step)], 0)
        tl = matmul(block[:, :tw], text[:, :tw], 1, 1) * scale_t
        sl = matmul(block[:, tw:], text[:, tw:], 1, 1) * scale_s
        tl_ref[p * b : p * b + count, :] = tl
        sl_ref[p * b : p * b + count, :] = sl
        top_t, top_s = jnp.max(tl, 0, keepdims=True), jnp.max(sl, 0, keepdims=True)
        peak_t = top_t if peak_t is None else jnp.maximum(peak_t, top_t)
        peak_s = top_s if peak_s is None else jnp.maximum(peak_s, top_s)
        mt, ms = jnp.max(tl, 1, keepdims=True), jnp.max(sl, 1, keepdims=True)
        et = jnp.exp(tl - mt)
        sum_t = jnp.sum(et, 1, keepdims=True)
        gap = jnp.sum(et * (tl - sl), 1, keepdims=True)
        sum_s = jnp.sum(jnp.exp(sl - ms), 1, keepdims=True)
        lines = pack_lines((mt + jnp.log(sum_t), ms + jnp.log(sum_s), gap / sum_t), (count, 128), 1)
        for k in range(step):
            place = pl.ds(pl.multiple_of((rank[0] ^ (p + k)) * b, b), b)
            flat = jnp.transpose(lines[k * b : (k + 1) * b])[:LINES]
            for q in range(nr):
                row_ref[q * LINES : (q + 1) * LINES, place] = flat
    sum_t = sum_s = gap = None
    for p in range(0, nr, step):
        tl, sl = tl_ref[p * b : p * b + count, :], sl_ref[p * b : p * b + count, :]
        et = jnp.exp(tl - peak_t)
        parts = [
            jnp.sum(et, 0, keepdims=True),
            jnp.sum(jnp.exp(sl - peak_s), 0, keepdims=True),
            jnp.sum(et * (tl - sl), 0, keepdims=True),
        ]
        sum_t, sum_s, gap = parts if p == 0 else [x + y for x, y in zip((sum_t, sum_s, gap), parts)]
    lines = (peak_t + jnp.log(sum_t), peak_s + jnp.log(sum_s), gap / sum_t)
    for p in range(nc):
        place = pl.ds(pl.multiple_of((rank[1] ^ p) * b, b), b)
        flat = pack_lines([x[:, p * b : (p + 1) * b] for x in lines], (LINES, b), 0)
        for q in range(nc):
            col_ref[q * LINES : (q + 1) * LINES, place] = flat


def combine(parts, n):
    tiles = [parts[k * LINES : (k + 1) * LINES, :] for k in range(n)]
    peak = functools.reduce(jnp.maximum, tiles)
    weights = [jnp.exp(x - peak) for x in tiles]
    total = functools.reduce(jnp.add, weights)
    lse = peak + jnp.log(total)
    gap = functools.reduce(jnp.add, [w[0:1] * x[2:3] for w, x in zip(weights, tiles)])
    return lse, jnp.sum(gap / total[0:1] + lse[1:2] - lse[0:1], axis=(0, 1), keepdims=True)


def gradient_kernel(cfg, rank, *refs):
    nr, nc, b, tw, scale = cfg
    images, texts = refs[:nr], refs[nr : nr + nc]
    tl_ref, sl_ref, row_parts, col_parts = refs[nr + nc : nr + nc + 4]
    image_keep, image_send, text_keep, text_send, lse_ref, text, image, high_ref, low_ref = refs[nr + nc + 4 :]
    row_lse, row_share = combine(row_parts, nr)
    col_lse, col_share = combine(col_parts, nc)
    lse_ref[...] = row_lse
    for p in range(nc):
        text[p * b : (p + 1) * b, :] = texts[p][:, tw:]
    for p in range(nr):
        image[p * b : (p + 1) * b, :] = images[p][:, tw:]
    columns = [[None, None] for _ in range(nc)]
    for p in range(nc):
        place = rank[1] ^ p
        for k in range(2):
            piece = col_lse[k : k + 1, :b]
            for q in range(1, nc):
                piece = jnp.where(place == q, col_lse[k : k + 1, q * b : (q + 1) * b], piece)
            columns[p][k] = piece
    col_t = jnp.concatenate([c[0] for c in columns], 1)
    col_s = jnp.concatenate([c[1] for c in columns], 1)
    half = nr // 2
    for p in range(nr):
        place = pl.ds(pl.multiple_of((rank[0] ^ p) * b, b), b)
        row = jnp.transpose(lse_ref[:, place])
        tl, sl = tl_ref[p * b : (p + 1) * b, :], sl_ref[p * b : (p + 1) * b, :]
        delta = (jnp.exp(sl - row[:, 1:2]) - jnp.exp(tl - row[:, 0:1])) + (jnp.exp(sl - col_s) - jnp.exp(tl - col_t))
        high = delta.astype(BF16)
        high_ref[p * b : (p + 1) * b, :] = high
        low_ref[p * b : (p + 1) * b, :] = (delta - high.astype(F32)).astype(BF16)
    for p in range(nr):
        rows = slice(p * b, (p + 1) * b)
        part = (matmul(high_ref[rows, :], text[...], 1, 0) + matmul(low_ref[rows, :], text[...], 1, 0)) * scale
        if p < half:
            image_keep[rows, :] = part
        else:
            image_send[(p - half) * b : (p - half + 1) * b, :] = part
    half = nc // 2
    for p in range(nc):
        cols = slice(p * b, (p + 1) * b)
        part = (matmul(high_ref[:, cols], image[...], 0, 0) + matmul(low_ref[:, cols], image[...], 0, 0)) * scale
        if p < half:
            text_keep[cols, :] = part
        else:
            text_send[(p - half) * b : (p - half + 1) * b, :] = part
    for ref, share in ((image_keep, col_share), (image_send, col_share), (text_keep, row_share), (text_send, row_share)):
        ref[ref.shape[0] - EXTRA :, :] = jnp.broadcast_to(share, (EXTRA, ref.shape[1]))


def swap(bit, x):
    return lax.ppermute(x, bit, [(0, 1), (1, 0)])


def gather(bits, x):
    blocks = [x]
    for bit in bits:
        blocks = blocks + [swap(bit, y) for y in blocks]
    return blocks


def scatter_sum(bits, keep, send, b):
    for k in reversed(range(len(bits))):
        total = keep + swap(bits[k], send)
        if k:
            rows = total.shape[0] - EXTRA
            send = total[rows // 2 :]
            keep = jnp.concatenate([total[: rows // 2], total[rows:]])
    return total[:b], total[b, 0]


def local(image_bits, text_bits, teacher_image, teacher_text, student_image, student_text):
    b, tw = teacher_image.shape
    sw = student_image.shape[1]
    nr, nc = 1 << len(image_bits), 1 << len(text_bits)
    r, c = nr * b, nc * b
    images = gather(image_bits, jnp.concatenate([teacher_image, student_image], 1))
    texts = gather(text_bits, jnp.concatenate([teacher_text, student_text], 1))
    row_axes, col_axes = image_bits[::-1], text_bits[::-1]
    rank = jnp.stack([lax.axis_index(row_axes), lax.axis_index(col_axes)]).astype(jnp.int32)
    blocks = images + texts
    specs = [SMEM] + [VMEM] * len(blocks)
    out = lambda *shape: jax.ShapeDtypeStruct(shape, F32)
    flops = 2 * r * c * (tw + sw)
    tl, sl, row_lines, col_lines = pl.pallas_call(
        functools.partial(stats_kernel, (nr, nc, b, tw, tw**-0.5, sw**-0.5)),
        out_shape=[out(r, c), out(r, c), out(nr * LINES, r), out(nc * LINES, c)],
        in_specs=specs,
        out_specs=[VMEM] * 4,
        scratch_shapes=[pltpu.VMEM((c, tw + sw), BF16)],
        compiler_params=PARAMS,
        cost_estimate=pl.CostEstimate(flops=flops, bytes_accessed=8 * r * c, transcendentals=4 * r * c),
    )(rank, *blocks)
    row_lines = lax.all_to_all(row_lines, row_axes, 0, 0, tiled=True)
    col_lines = lax.all_to_all(col_lines, col_axes, 0, 0, tiled=True)
    ir, ic = r // 2 + EXTRA, c // 2 + EXTRA
    image_keep, image_send, text_keep, text_send = pl.pallas_call(
        functools.partial(gradient_kernel, (nr, nc, b, tw, sw**-0.5)),
        out_shape=[out(ir, sw), out(ir, sw), out(ic, sw), out(ic, sw)],
        in_specs=specs + [VMEM] * 4,
        out_specs=[VMEM] * 4,
        scratch_shapes=[
            pltpu.VMEM((LINES, r), F32),
            pltpu.VMEM((c, sw), BF16),
            pltpu.VMEM((r, sw), BF16),
            pltpu.VMEM((r, c), BF16),
            pltpu.VMEM((r, c), BF16),
        ],
        compiler_params=PARAMS,
        cost_estimate=pl.CostEstimate(flops=8 * r * c * sw, bytes_accessed=8 * r * c, transcendentals=4 * r * c),
    )(rank, *blocks, tl, sl, row_lines, col_lines)
    image_grad, col_share = scatter_sum(image_bits, image_keep, image_send, b)
    text_grad, row_share = scatter_sum(text_bits, text_keep, text_send, b)
    pairs = b << (len(image_bits) + len(text_bits))
    return ((row_share + col_share) / (2.0 * pairs), image_grad, text_grad)


def solution(mesh):
    bits = {axis: [f"{axis}{k}" for k in reversed(range(mesh.shape[axis].bit_length() - 1))] for axis in ("img", "txt")}
    names = bits["img"] + bits["txt"]
    cube = Mesh(np.asarray(mesh.devices).reshape((2,) * len(names)), names)
    text_bits = [x for x in bits["img"] if int(x[3:]) >= 1] + [x for x in bits["txt"] if int(x[3:]) % 2 == 1]
    image_bits = [x for x in names if x not in text_bits]
    image, text = P(tuple(names), None), P(tuple(bits["txt"] + bits["img"]), None)
    return jax.shard_map(
        functools.partial(local, tuple(image_bits), tuple(text_bits)),
        mesh=cube,
        in_specs=(image, text, image, text),
        out_specs=(P(), image, text),
        check_vma=False,
    )
```

```python
import functools

import jax
import jax.numpy as jnp
import numpy as np
from jax import lax
from jax.experimental import pallas as pl
from jax.experimental.pallas import tpu as pltpu
from jax.sharding import Mesh, PartitionSpec as P

F32 = jnp.float32
BF16 = jnp.bfloat16
F16 = jnp.float16
LINES = 8
EXTRA = 16
PARAMS = pltpu.CompilerParams(vmem_limit_bytes=56 * 2**20)
VMEM = pl.BlockSpec(memory_space=pltpu.VMEM)


def matmul(a, b, da, db):
    return lax.dot_general(a, b, (((da,), (db,)), ((), ())), preferred_element_type=F32)


def block(k, b):
    return slice(k * b, (k + 1) * b)


def only(k, value, shape, axis):
    return jnp.where(lax.broadcasted_iota(jnp.int32, shape, axis) == k, value, 0.0)


def row_lse(logit):
    peak = jnp.max(logit, 1, keepdims=True)
    return peak + jnp.log(jnp.sum(jnp.exp(logit - peak), 1, keepdims=True))


def logit_kernel(nr, nc, b, scale, line, *refs):
    images, texts, refs = refs[:nr], refs[nr : nr + nc], refs[nr + nc :]
    before, refs = (refs[0], refs[1:]) if line else (None, refs)
    logit_ref, row_ref, text = refs
    for p in range(nc):
        text[block(p, b), :] = texts[p][...]
    step = 2 if nr % 2 == 0 else 1
    for p in range(0, nr, step):
        image = jnp.concatenate([x[...] for x in images[p : p + step]], 0)
        logit = matmul(image, text[...], 1, 1) * scale
        logit_ref[p * b : (p + step) * b, :] = logit
        lse = only(line, row_lse(logit), (step * b, 128), 1)
        for k in range(step):
            flat = jnp.transpose(lse[block(k, b)])[:LINES]
            row_ref[:, block(p + k, b)] = flat + before[:, block(p + k, b)] if line else flat


def column_kernel(line, *refs):
    logit_ref, refs = refs[0], refs[1:]
    before, refs = (refs[0], refs[1:]) if line else (None, refs)
    col_ref = refs[0]
    step = min(256, logit_ref.shape[0])
    chunks = [slice(k, k + step) for k in range(0, logit_ref.shape[0], step)]
    peak = functools.reduce(jnp.maximum, [jnp.max(logit_ref[x, :], 0, keepdims=True) for x in chunks])
    total = functools.reduce(
        jnp.add, [jnp.sum(jnp.exp(logit_ref[x, :] - peak), 0, keepdims=True) for x in chunks]
    )
    lse = only(line, peak + jnp.log(total), col_ref.shape, 0)
    col_ref[...] = lse + before[...] if line else lse


def merge(x, y):
    peak = jnp.maximum(x, y)
    return peak + jnp.log(jnp.exp(x - peak) + jnp.exp(y - peak))


def merge_kernel(b, flips, *refs):
    n = len(flips)
    for k, flip in enumerate(flips):
        own, come, out = refs[2 * k], refs[2 * k + 1], refs[2 * n + k]
        for p in range(own.shape[1] // b):
            out[:, block(p, b)] = merge(own[:, block(p, b)], come[:, block(p ^ flip, b)])


def image_kernel(nr, nc, b, scale, *refs):
    texts, refs = refs[:nc], refs[nc:]
    tl_ref, sl_ref, row_own, row_come, col_own, col_come, keep, send, high_ref, low_ref, share, top, text = refs
    for p in range(nc):
        text[block(p, b), :] = texts[p][...]
    cols = [merge(col_own[:, block(p, b)], col_come[:, block(p ^ 1, b)]) for p in range(nc)]
    col_t = jnp.concatenate([x[0:1] for x in cols], 1)
    col_s = jnp.concatenate([x[1:2] for x in cols], 1)
    gap = cols[0][1:2] - cols[0][0:1]
    half = nr // 2
    total = high_end = None
    for p in range(nr):
        rows = merge(row_own[:, block(p, b)], row_come[:, block(p ^ 1, b)])
        if p == 0:
            gap = gap + (rows[1:2] - rows[0:1])
        row = jnp.transpose(rows)
        tl, sl = tl_ref[block(p, b), :], sl_ref[block(p, b), :]
        row_t, col_prob_t = jnp.exp(tl - row[:, 0:1]), jnp.exp(tl - col_t)
        delta = (jnp.exp(sl - row[:, 1:2]) - row_t) + (jnp.exp(sl - col_s) - col_prob_t)
        part = jnp.sum((row_t + col_prob_t) * (tl - sl), 0, keepdims=True)
        total = part if total is None else total + part
        high = delta.astype(BF16)
        low = (delta - high.astype(F32)).astype(BF16)
        high_ref[block(p, b), :] = high
        low_ref[block(p, b), :] = low
        part = (matmul(high, text[...], 1, 0) + matmul(low, text[...], 1, 0)) * scale
        peak = jnp.max(jnp.abs(part), 0, keepdims=True)
        high_end = peak if high_end is None else jnp.maximum(high_end, peak)
        if p < half:
            keep[block(p, b), :] = part
        else:
            send[block(p - half, b), :] = part
    share[...] = jnp.broadcast_to(jnp.sum(total, 1, keepdims=True) + jnp.sum(gap, 1, keepdims=True), share.shape)
    high_end = jnp.max(high_end, 1, keepdims=True)
    top[...] = jnp.broadcast_to(high_end, top.shape)
    send[half * b :, :] = jnp.broadcast_to(high_end, (send.shape[0] - half * b, send.shape[1]))


def text_kernel(nr, nc, b, scale, *refs):
    images, refs = refs[:nr], refs[nr:]
    high_ref, low_ref, keep, send, top, image = refs
    for p in range(nr):
        image[block(p, b), :] = images[p][...]
    half = nc // 2
    high_end = None
    for p in range(nc):
        high, low = high_ref[:, block(p, b)], low_ref[:, block(p, b)]
        part = (matmul(high, image[...], 0, 0) + matmul(low, image[...], 0, 0)) * scale
        peak = jnp.max(jnp.abs(part), axis=(0, 1), keepdims=True)
        high_end = peak if high_end is None else jnp.maximum(high_end, peak)
        if p < half:
            keep[block(p, b), :] = part
        else:
            send[block(p - half, b), :] = part
    top[...] = jnp.broadcast_to(high_end, top.shape)


def call(kernel, outs, args, scratch=(), flops=0, transcendentals=0):
    shapes = [jax.ShapeDtypeStruct(s, d) for s, d in outs]
    size = sum(x.size * x.dtype.itemsize for x in list(args) + shapes)
    return pl.pallas_call(
        kernel,
        out_shape=shapes,
        in_specs=[VMEM] * len(args),
        out_specs=[VMEM] * len(shapes),
        scratch_shapes=[pltpu.VMEM(s, d) for s, d in scratch],
        compiler_params=PARAMS,
        cost_estimate=pl.CostEstimate(flops=flops, bytes_accessed=size, transcendentals=transcendentals),
    )(*args)


def swap(bit, x):
    return lax.ppermute(x, bit, [(0, 1), (1, 0)])


def after(x, done):
    return lax.optimization_barrier((x, done))[0]


def gather(bits, teacher, student):
    teachers, students = [teacher], [student]
    for bit in bits:
        first = swap(bit, teacher)
        second = swap(bit, after(student, first))
        teachers = teachers + [first] + [swap(bit, after(x, second)) for x in teachers[1:]]
        students = students + [second] + [swap(bit, x) for x in students[1:]]
    return teachers, students


def message(x, bound):
    power = jnp.ceil(jnp.log2(jnp.maximum(bound, 1e-30)))
    return jnp.concatenate([(x * jnp.exp2(14.0 - power)).astype(F16), jnp.full((EXTRA, x.shape[1]), power, F16)])


def add_message(keep, come, bound):
    rows = come.shape[0] - EXTRA
    power = come[rows, 0].astype(F32)
    return keep + come[:rows].astype(F32) * jnp.exp2(power - 14.0), bound + jnp.exp2(power)


def halves(x):
    return x[: x.shape[0] // 2], x[x.shape[0] // 2 :]


def local(image_bits, text_bits, teacher_image, teacher_text, student_image, student_text):
    b, tw = teacher_image.shape
    sw = student_image.shape[1]
    nr, nc = 1 << len(image_bits), 1 << len(text_bits)
    r, c = nr * b, nc * b
    ti, si = gather(image_bits, teacher_image, student_image)
    tt, st = gather(text_bits, teacher_text, student_text)
    tl, rows = call(
        functools.partial(logit_kernel, nr, nc, b, tw**-0.5, 0),
        [((r, c), F32), ((LINES, r), F32)], ti + tt, [((c, tw), BF16)], 2 * r * c * tw, r * c,
    )
    (cols,) = call(functools.partial(column_kernel, 0), [((LINES, c), F32)], [tl], (), 4 * r * c, r * c)
    sl, rows = call(
        functools.partial(logit_kernel, nr, nc, b, sw**-0.5, 1),
        [((r, c), F32), ((LINES, r), F32)], si + st + [rows], [((c, sw), BF16)], 2 * r * c * sw, r * c,
    )
    (cols,) = call(functools.partial(column_kernel, 1), [((LINES, c), F32)], [sl, cols], (), 4 * r * c, r * c)
    rounds = max(len(image_bits), len(text_bits))
    row_come = col_come = None
    for k in reversed(range(rounds)):
        todo = []
        if k < len(image_bits):
            row_come = swap(image_bits[k], rows)
            todo.append((rows, row_come))
        if k < len(text_bits):
            col_come = swap(text_bits[k], cols)
            todo.append((cols, col_come))
        if k:
            args = [x for pair in todo for x in pair]
            outs = list(call(
                functools.partial(merge_kernel, b, [1 << k] * len(todo)), [(x.shape, F32) for x, _ in todo], args)
            )
            if k < len(text_bits):
                cols = outs.pop()
            if k < len(image_bits):
                rows = outs.pop()
    lanes = ((8, 128), F32)
    keep, send, high, low, share, top = call(
        functools.partial(image_kernel, nr, nc, b, sw**-0.5),
        [((r // 2, sw), F32), ((r // 2 + 8, sw), F32), ((r, c), BF16), ((r, c), BF16), lanes, lanes],
        st + [tl, sl, rows, row_come, cols, col_come], [((c, sw), BF16)], 4 * r * c * sw, 4 * r * c,
    )
    come = swap(image_bits[-1], send)
    share_bits = list(text_bits[:1] + image_bits[:1] + text_bits[1:] + image_bits[1:])
    share = share + swap(share_bits.pop(), share)
    text_keep, text_send, text_top = call(
        functools.partial(text_kernel, nr, nc, b, sw**-0.5),
        [((c // 2, sw), F32), ((c // 2, sw), F32), lanes], si + [high, low], [((r, sw), BF16)], 4 * r * c * sw,
    )
    text_bound, image_bound = text_top[0, 0], top[0, 0] + come[r // 2, 0]
    text_note = message(text_send, text_bound)
    text_come = swap(text_bits[-1], text_note)
    image_keep, image_send = halves(keep + come[: r // 2])
    image_note = message(image_send, image_bound)
    image_come = swap(image_bits[-2], image_note)
    share = after(share, image_note)
    share = share + swap(share_bits.pop(), share)
    text_total, text_bound = add_message(text_keep, after(text_come, image_note), text_bound)
    image_total, image_bound = add_message(image_keep, image_come, image_bound)
    for k in reversed(range(max(len(text_bits) - 1, len(image_bits) - 2))):
        if k < len(text_bits) - 1:
            text_keep, text_send = halves(text_total)
            text_note = message(text_send, text_bound)
            text_come = swap(text_bits[k], text_note)
        if k < len(image_bits) - 2:
            image_keep, image_send = halves(image_total)
            image_note = message(image_send, image_bound)
            image_come = swap(image_bits[k], image_note)
        if k < len(text_bits) - 1:
            text_total, text_bound = add_message(text_keep, after(text_come, image_note), text_bound)
        if k < len(image_bits) - 2:
            image_total, image_bound = add_message(image_keep, after(image_come, text_note), image_bound)
    share = after(share, (text_note, image_note))
    while share_bits:
        share = share + swap(share_bits.pop(), share)
    image_grad, text_grad = image_total, text_total
    pairs = b << (len(image_bits) + len(text_bits))
    return (share[0, 0] / (2.0 * pairs), image_grad, text_grad)


def solution(mesh):
    bits = {axis: [f"{axis}{k}" for k in reversed(range(mesh.shape[axis].bit_length() - 1))] for axis in ("img", "txt")}
    names = bits["img"] + bits["txt"]
    cube = Mesh(np.asarray(mesh.devices).reshape((2,) * len(names)), names)
    text_bits = [x for x in bits["img"] if int(x[3:]) >= 1] + [x for x in bits["txt"] if int(x[3:]) % 2 == 1]
    image_bits = [x for x in names if x not in text_bits]
    image, text = P(tuple(names), None), P(tuple(bits["txt"] + bits["img"]), None)
    return jax.shard_map(
        functools.partial(local, tuple(image_bits), tuple(text_bits)),
        mesh=cube,
        in_specs=(image, text, image, text),
        out_specs=(P(), image, text),
        check_vma=False,
    )
```

```python
import functools

import jax
import jax.numpy as jnp
import numpy as np
from jax import lax
from jax.experimental import pallas as pl
from jax.experimental.pallas import tpu as pltpu
from jax.sharding import Mesh, PartitionSpec as P

F32 = jnp.float32
BF16 = jnp.bfloat16
F16 = jnp.float16
LOG2E = 1.4426950408889634
LN2 = 0.6931471805599453
LINES = 8
KINDS = 3
PARAMS = pltpu.CompilerParams(vmem_limit_bytes=56 * 2**20)
VMEM = pl.BlockSpec(memory_space=pltpu.VMEM)
SMEM = pl.BlockSpec(memory_space=pltpu.SMEM)


def matmul(a, b, da, db):
    return lax.dot_general(a, b, (((da,), (db,)), ((), ())), preferred_element_type=F32)


def block(k, b):
    return slice(k * b, (k + 1) * b)


def stack_rows(values, shape, axis, first=0):
    index = lax.broadcasted_iota(jnp.int32, shape, axis) - first
    out = jnp.zeros(shape, F32)
    for k, value in enumerate(values):
        out = jnp.where(index == k, value, out)
    return out


def tree(op, items):
    while len(items) > 1:
        items = [op(x, y) for x, y in zip(items[::2], items[1::2])]
    return items[0]


def stats_kernel(image_forms, text_forms, b, tw, scale_t, scale_s, core, *refs):
    nr, nc = len(image_forms), len(text_forms)
    ti, si, refs = views(refs, image_forms, tw)
    tt, st, refs = views(refs, text_forms, tw)
    tl_ref, sl_ref, row_ref, swap_ref, col_ref, text_t, text_s = refs
    for p in range(nc):
        text_t[block(p, b), :] = tt[p][...]
        text_s[block(p, b), :] = st[p][...]
    step = 2 if nr % 2 == 0 else 1
    count = step * b
    peak_t = peak_s = None
    for p in range(0, nr, step):
        rows = slice(p * b, p * b + count)
        tl = matmul(jnp.concatenate([x[...] for x in ti[p : p + step]], 0), text_t[...], 1, 1) * (scale_t * LOG2E)
        sl = matmul(jnp.concatenate([x[...] for x in si[p : p + step]], 0), text_s[...], 1, 1) * (scale_s * LOG2E)
        tl_ref[rows, :] = tl
        sl_ref[rows, :] = sl
        top_t, top_s = jnp.max(tl, 0, keepdims=True), jnp.max(sl, 0, keepdims=True)
        peak_t = top_t if peak_t is None else jnp.maximum(peak_t, top_t)
        peak_s = top_s if peak_s is None else jnp.maximum(peak_s, top_s)
        mt, ms = jnp.max(tl, 1, keepdims=True), jnp.max(sl, 1, keepdims=True)
        et = jnp.exp2(tl - mt)
        sum_t = jnp.sum(et, 1, keepdims=True)
        gap = jnp.sum(et * (tl - sl), 1, keepdims=True)
        sum_s = jnp.sum(jnp.exp2(sl - ms), 1, keepdims=True)
        lines = (mt + jnp.log2(sum_t), ms + jnp.log2(sum_s), gap / sum_t)
        lines = stack_rows(lines, (count, 128), 1, core[0] * KINDS)
        for k in range(step):
            flat = jnp.transpose(lines[block(k, b)])[:LINES]
            row_ref[:, block(p + k, b)] = flat
            swap_ref[:, block((p + k) ^ (nr // 2), b)] = flat
    sum_t = sum_s = gap = None
    for p in range(0, nr, step):
        tl, sl = tl_ref[p * b : p * b + count, :], sl_ref[p * b : p * b + count, :]
        et = jnp.exp2(tl - peak_t)
        parts = [
            jnp.sum(et, 0, keepdims=True),
            jnp.sum(jnp.exp2(sl - peak_s), 0, keepdims=True),
            jnp.sum(et * (tl - sl), 0, keepdims=True),
        ]
        sum_t, sum_s, gap = parts if p == 0 else [x + y for x, y in zip((sum_t, sum_s, gap), parts)]
    lines = (peak_t + jnp.log2(sum_t), peak_s + jnp.log2(sum_s), gap / sum_t)
    col_ref[...] = stack_rows(lines, col_ref.shape, 0)


def combine(tiles, terms):
    lses = []
    for kind in (1, 0):
        peak = tree(jnp.maximum, [x[kind] for x in tiles])
        weights = [jnp.exp2(x[kind] - peak) for x in tiles]
        total = tree(jnp.add, weights)
        lses.append(peak + jnp.log2(total))
    for k, (w, x) in enumerate(zip(weights, tiles)):
        terms[k : k + 1, :] = w * x[2]
    gap = tree(jnp.add, [terms[k : k + 1, :] for k in range(len(tiles))])
    return lses[1], lses[0], gap / total + (lses[0] - lses[1])


def sum_blocks(x, b):
    parts = [jnp.sum(x[:, block(p, b)], axis=(0, 1), keepdims=True) for p in range(x.shape[1] // b)]
    return tree(jnp.add, parts) * LN2


def gradient_kernel(image_forms, text_forms, b, tw, scale, *refs):
    nr, nc = len(image_forms), len(text_forms)
    si, refs = refs[:nr], refs[nr:]
    st, refs = refs[:nc], refs[nc:]
    tl_ref, sl_ref, refs = refs[0], refs[1], refs[2:]
    row_parts, refs = refs[: nr // 2], refs[nr // 2 :]
    col_parts, refs = refs[:nc], refs[nc:]
    image_keep, image_send, text_keep, text_send, image_extra, text_extra, refs = *refs[:6], refs[6:]
    text, image, high_ref, low_ref, row_terms, col_terms = refs
    for p in range(nc):
        text[block(p, b), :] = st[p][...] if text_forms[p] == 2 else st[p][:, tw:]
    for p in range(nr):
        image[block(p, b), :] = si[p][...] if image_forms[p] == 2 else si[p][:, tw:]
    tiles = []
    for q in range(nr // 2):
        x = jnp.concatenate([row_parts[q][:, block(p ^ q, b)] for p in range(nr)], 1)
        for core in range(2):
            tiles.append([x[core * KINDS + k : core * KINDS + k + 1, :] for k in range(KINDS)])
    row_t, row_s, terms = combine(tiles, row_terms)
    row_share = sum_blocks(terms, b)
    rows = stack_rows((row_t, row_s), (LINES, nr * b), 0)
    tiles = []
    for q in range(nc):
        x = jnp.concatenate([col_parts[q][:, block(p ^ q, b)] for p in range(nc)], 1)
        tiles.append([x[k : k + 1, :] for k in range(KINDS)])
    col_t, col_s, terms = combine(tiles, col_terms)
    col_share = sum_blocks(terms, b)
    half = nr // 2
    for p in range(nr):
        row = jnp.transpose(rows[:, block(p, b)])
        tl, sl = tl_ref[block(p, b), :], sl_ref[block(p, b), :]
        delta = (jnp.exp2(sl - row[:, 1:2]) - jnp.exp2(tl - row[:, 0:1])) + (
            jnp.exp2(sl - col_s) - jnp.exp2(tl - col_t)
        )
        high = delta.astype(BF16)
        high_ref[block(p, b), :] = high
        low_ref[block(p, b), :] = (delta - high.astype(F32)).astype(BF16)
    step = 2 if half % 2 == 0 else 1
    bound = None
    for p in range(0, nr, step):
        rows = slice(p * b, (p + step) * b)
        part = (matmul(high_ref[rows, :], text[...], 1, 0) + matmul(low_ref[rows, :], text[...], 1, 0)) * scale
        peak = jnp.max(jnp.abs(part), 0, keepdims=True)
        bound = peak if bound is None else jnp.maximum(bound, peak)
        if p < half:
            image_keep[rows, :] = part
        else:
            image_send[(p - half) * b : (p - half + step) * b, :] = part
    extra = stack_rows((bound, col_share), image_extra.shape, 0)
    image_extra[...] = extra
    image_send[half * b :, :] = extra
    half = nc // 2
    step = 2 if half % 2 == 0 else 1
    bound = None
    for p in range(0, nc, step):
        cols = slice(p * b, (p + step) * b)
        part = (matmul(high_ref[:, cols], image[...], 0, 0) + matmul(low_ref[:, cols], image[...], 0, 0)) * scale
        peak = jnp.max(jnp.abs(part), 0, keepdims=True)
        bound = peak if bound is None else jnp.maximum(bound, peak)
        if p < half:
            text_keep[cols, :] = part
        else:
            text_send[(p - half) * b : (p - half + step) * b, :] = part
    text_extra[...] = stack_rows((bound, row_share), text_extra.shape, 0)


def call(kernel, outs, args, scratch=(), flops=0, transcendentals=0):
    shapes = [jax.ShapeDtypeStruct(s, d) for s, d in outs]
    size = sum(x.size * x.dtype.itemsize for x in list(args) + shapes)
    return pl.pallas_call(
        kernel,
        out_shape=shapes,
        in_specs=[SMEM if x.dtype == jnp.int32 else VMEM for x in args],
        out_specs=[VMEM] * len(shapes),
        scratch_shapes=[pltpu.VMEM(s, d) for s, d in scratch],
        compiler_params=PARAMS,
        cost_estimate=pl.CostEstimate(flops=flops, bytes_accessed=size, transcendentals=transcendentals),
    )(*args)


def swap(bits, x):
    perm = [(i, i ^ ((1 << len(bits)) - 1)) for i in range(1 << len(bits))]
    return lax.ppermute(x, bits, perm)


def subset(bits, q):
    return tuple(b for k, b in enumerate(bits) if q >> k & 1)


def after(x, done):
    return lax.optimization_barrier((x, done))[0]


def together(*groups):
    return lax.optimization_barrier(groups)


def gather(image_bits, text_bits, image, text):
    groups = []
    for bits, (teacher, student) in ((image_bits, image), (text_bits, text)):
        both = jnp.concatenate([teacher, student], 1)
        groups.append((bits, teacher, student, both))
    come = [{0: [swap(bits[:1], teacher)]} for bits, teacher, _, _ in groups]
    for (bits, _, _, both), got in zip(groups, come):
        for k in range(1, len(bits)):
            got[1 << k] = [swap(bits[k : k + 1], both)]
    come = [{1 if p == 0 else p: x for p, x in got.items()} for got in come]
    students = [group[2] for group in groups]
    for stage in range(1, max(len(image_bits), len(text_bits)) + 1):
        come, students = together(come, students)
        new = [{p: list(x) for p, x in got.items()} for got in come]
        for n, (bits, _, _, _) in enumerate(groups):
            if stage == 1:
                new[n][1].append(swap(bits[:1], students[n]))
            for k in range(1, len(bits)):
                for p in range(1, 1 << k):
                    have, sent = come[n].get(p, []), new[n].setdefault(p | 1 << k, [])
                    sent.extend(swap(bits[k : k + 1], x) for x in have[len(sent) :])
        come = new
    blocks = []
    for (bits, teacher, student, _), got in zip(groups, come):
        blocks.append([(teacher, student)] + [tuple(got[p]) for p in range(1, 1 << len(bits))])
    return blocks


def flatten(blocks):
    return [x for parts in blocks for x in parts]


def views(refs, forms, tw):
    teachers, students = [], []
    for form in forms:
        if form == 1:
            teachers.append(refs[0].at[:, :tw])
            students.append(refs[0].at[:, tw:])
        else:
            teachers.append(refs[0])
            students.append(refs[1])
        refs = refs[form:]
    return teachers, students, refs


def power_of(extra):
    return jnp.ceil(jnp.log2(jnp.maximum(extra[0:1], 1e-30)))


def narrow(x, extra):
    return (x * jnp.exp2(14.0 - power_of(extra))).astype(F16)


def add_sum(keep, come, extra):
    body, other = come
    return keep + body.astype(F32) * jnp.exp2(power_of(other) - 14.0), extra + other


def halves(x):
    return x[: x.shape[0] // 2], x[x.shape[0] // 2 :]


def local(image_bits, text_bits, teacher_image, teacher_text, student_image, student_text):
    b, tw = teacher_image.shape
    sw = student_image.shape[1]
    nr, nc = 1 << len(image_bits), 1 << len(text_bits)
    r, c = nr * b, nc * b
    pair, others = image_bits[-1:], image_bits[:-1]
    images, texts = gather(image_bits, text_bits, (teacher_image, student_image), (teacher_text, student_text))
    forms = [len(x) for x in images], [len(x) for x in texts]
    core = lax.axis_index(pair).astype(jnp.int32).reshape(1)
    tl, sl, rows, rows_swapped, cols = call(
        functools.partial(stats_kernel, *forms, b, tw, tw**-0.5, sw**-0.5),
        [((r, c), F32), ((r, c), F32), ((LINES, r), F32), ((LINES, r), F32), ((LINES, c), F32)],
        [core] + flatten(images + texts), [((c, tw), BF16), ((c, sw), BF16)], 2 * r * c * (tw + sw), 4 * r * c,
    )
    other = swap(pair, rows_swapped)
    col_parts = [cols] + [swap(subset(text_bits, q), cols) for q in range(1, nc)]
    rows = rows + other
    row_parts = [rows] + [swap(subset(others, q), rows) for q in range(1, nr // 2)]
    lines = ((LINES, sw), F32)
    image_keep, image_send, text_keep, text_send, image_extra, text_extra = call(
        functools.partial(gradient_kernel, *forms, b, tw, sw**-0.5),
        [((r // 2, sw), F32), ((r // 2 + LINES, sw), F32), ((c // 2, sw), F32), ((c // 2, sw), F32), lines, lines],
        [x[-1] for x in images + texts] + [tl, sl] + row_parts + col_parts,
        [((c, sw), BF16), ((r, sw), BF16), ((r, c), BF16), ((r, c), BF16), ((nr, r), F32), ((max(nc, 8), c), F32)],
        8 * r * c * sw, 4 * r * c,
    )
    come = swap(pair, image_send)
    image_keep, image_send = halves(image_keep + come[: r // 2])
    image_extra = image_extra + come[r // 2 :]
    for k in reversed(range(max(len(text_bits), len(others)))):
        todo = {}
        if k < len(text_bits):
            todo["text"] = [narrow(text_send, text_extra), text_extra]
        if k < len(others):
            todo["image"] = [narrow(image_send, image_extra), image_extra]
        (todo,) = together(todo)
        if k < len(text_bits):
            text_come = [swap(text_bits[k : k + 1], x) for x in todo["text"]]
        if k < len(others):
            image_come = [swap(others[k : k + 1], x) for x in todo["image"]]
        if k < len(text_bits):
            text_total, text_extra = add_sum(text_keep, text_come, text_extra)
            text_keep, text_send = halves(text_total)
        if k < len(others):
            image_total, image_extra = add_sum(image_keep, image_come, image_extra)
            image_keep, image_send = halves(image_total)
    pairs = b << (len(image_bits) + len(text_bits))
    loss = (image_extra[1, 0] + text_extra[1, 0]) / (2.0 * pairs)
    return (loss, image_total, text_total)


def solution(mesh):
    bits = {axis: [f"{axis}{k}" for k in reversed(range(mesh.shape[axis].bit_length() - 1))] for axis in ("img", "txt")}
    names = bits["img"] + bits["txt"]
    cube = Mesh(np.asarray(mesh.devices).reshape((2,) * len(names)), names)
    text_bits = [x for x in bits["img"] if int(x[3:]) >= 1] + [x for x in bits["txt"] if int(x[3:]) % 2 == 1]
    image_bits = [x for x in names if x not in text_bits]
    image, text = P(tuple(names), None), P(tuple(bits["txt"] + bits["img"]), None)
    return jax.shard_map(
        functools.partial(local, tuple(image_bits), tuple(text_bits)),
        mesh=cube,
        in_specs=(image, text, image, text),
        out_specs=(P(), image, text),
        check_vma=False,
    )
```

```python
import functools

import jax
import jax.numpy as jnp
import numpy as np
from jax import lax
from jax.experimental import pallas as pl
from jax.experimental.pallas import tpu as pltpu
from jax.sharding import Mesh, PartitionSpec as P

F32 = jnp.float32
BF16 = jnp.bfloat16
F16 = jnp.float16
LOG2E = 1.4426950408889634
LN2 = 0.6931471805599453
LINES = 8
KINDS = 3
PARAMS = pltpu.CompilerParams(vmem_limit_bytes=56 * 2**20)
VMEM = pl.BlockSpec(memory_space=pltpu.VMEM)
SMEM = pl.BlockSpec(memory_space=pltpu.SMEM)


def matmul(a, b, da, db):
    return lax.dot_general(a, b, (((da,), (db,)), ((), ())), preferred_element_type=F32)


def block(k, b):
    return slice(k * b, (k + 1) * b)


def stack_rows(values, shape, axis, first=0):
    index = lax.broadcasted_iota(jnp.int32, shape, axis) - first
    out = jnp.zeros(shape, F32)
    for k, value in enumerate(values):
        out = jnp.where(index == k, value, out)
    return out


def tree(op, items):
    while len(items) > 1:
        items = [op(x, y) for x, y in zip(items[::2], items[1::2])]
    return items[0]


def stats_kernel(nr, nc, b, scale_t, scale_s, core, *refs):
    ti, si, refs = refs[:nr], refs[nr : 2 * nr], refs[2 * nr :]
    tt, st, refs = refs[:nc], refs[nc : 2 * nc], refs[2 * nc :]
    tl_ref, sl_ref, row_ref, swap_ref, col_ref, text_t, text_s = refs
    for p in range(nc):
        text_t[block(p, b), :] = tt[p][...]
        text_s[block(p, b), :] = st[p][...]
    largest = [
        functools.reduce(jnp.maximum, [jnp.max(jnp.abs(x[...].astype(F32)), 0, keepdims=True) for x in xs])
        for xs in (si, st)
    ]
    width = largest[0].shape[1]

    def with_largest(flat, k):
        if (k + 1) * b > width:
            return flat
        return flat + stack_rows((largest[1][:, block(k, b)],), flat.shape, 0, 2 * KINDS + core[0])

    step = 2 if nr % 2 == 0 else 1
    count = step * b
    peak_t = peak_s = None
    for p in range(0, nr, step):
        rows = slice(p * b, p * b + count)
        tl = matmul(jnp.concatenate([x[...] for x in ti[p : p + step]], 0), text_t[...], 1, 1) * (scale_t * LOG2E)
        sl = matmul(jnp.concatenate([x[...] for x in si[p : p + step]], 0), text_s[...], 1, 1) * (scale_s * LOG2E)
        tl_ref[rows, :] = tl
        sl_ref[rows, :] = sl
        top_t, top_s = jnp.max(tl, 0, keepdims=True), jnp.max(sl, 0, keepdims=True)
        peak_t = top_t if peak_t is None else jnp.maximum(peak_t, top_t)
        peak_s = top_s if peak_s is None else jnp.maximum(peak_s, top_s)
        mt, ms = jnp.max(tl, 1, keepdims=True), jnp.max(sl, 1, keepdims=True)
        et = jnp.exp2(tl - mt)
        sum_t = jnp.sum(et, 1, keepdims=True)
        gap = jnp.sum(et * (tl - sl), 1, keepdims=True)
        sum_s = jnp.sum(jnp.exp2(sl - ms), 1, keepdims=True)
        lines = (mt + jnp.log2(sum_t), ms + jnp.log2(sum_s), gap / sum_t)
        lines = stack_rows(lines, (count, 128), 1, core[0] * KINDS)
        for k in range(step):
            flat = jnp.transpose(lines[block(k, b)])[:LINES]
            other = (p + k) ^ (nr // 2)
            row_ref[:, block(p + k, b)] = with_largest(flat, p + k)
            swap_ref[:, block(other, b)] = with_largest(flat, other)
    sum_t = sum_s = gap = None
    for p in range(0, nr, step):
        tl, sl = tl_ref[p * b : p * b + count, :], sl_ref[p * b : p * b + count, :]
        et = jnp.exp2(tl - peak_t)
        parts = [
            jnp.sum(et, 0, keepdims=True),
            jnp.sum(jnp.exp2(sl - peak_s), 0, keepdims=True),
            jnp.sum(et * (tl - sl), 0, keepdims=True),
        ]
        sum_t, sum_s, gap = parts if p == 0 else [x + y for x, y in zip((sum_t, sum_s, gap), parts)]
    lines = (peak_t + jnp.log2(sum_t), peak_s + jnp.log2(sum_s), gap / sum_t)
    images = largest[0]
    if col_ref.shape[1] > width:
        images = jnp.concatenate([images, jnp.zeros((1, col_ref.shape[1] - width), F32)], 1)
    col_ref[...] = stack_rows(lines + (images,), col_ref.shape, 0)


def combine(tiles, terms):
    lses = []
    for kind in (1, 0):
        peak = tree(jnp.maximum, [x[kind] for x in tiles])
        weights = [jnp.exp2(x[kind] - peak) for x in tiles]
        total = tree(jnp.add, weights)
        lses.append(peak + jnp.log2(total))
    for k, (w, x) in enumerate(zip(weights, tiles)):
        terms[k : k + 1, :] = w * x[2]
    gap = tree(jnp.add, [terms[k : k + 1, :] for k in range(len(tiles))])
    return lses[1], lses[0], gap / total + (lses[0] - lses[1])


def sum_blocks(x, b):
    parts = [jnp.sum(x[:, block(p, b)], axis=(0, 1), keepdims=True) for p in range(x.shape[1] // b)]
    return tree(jnp.add, parts) * LN2


def powers(largest, pairs, scale):
    bound = functools.reduce(jnp.maximum, largest) * ((1 + pairs) * scale)
    power = jnp.ceil(jnp.log2(jnp.maximum(bound, 1e-30)))
    return jnp.exp2(15.0 - power) * scale, jnp.exp2(power - 15.0)


def gradient_kernel(nr, nc, b, pairs, scale, *refs):
    si, refs = refs[:nr], refs[nr:]
    st, refs = refs[:nc], refs[nc:]
    tl_ref, sl_ref, refs = refs[0], refs[1], refs[2:]
    row_parts, refs = refs[: nr // 2], refs[nr // 2 :]
    col_parts, refs = refs[:nc], refs[nc:]
    image_keep, image_send, text_keep, text_send, back, image_share, text_share, refs = *refs[:7], refs[7:]
    width = back.shape[1]
    lines = [x[2 * KINDS + core : 2 * KINDS + core + 1, :width] for x in row_parts for core in range(2)]
    image_scale, image_back = powers(lines, pairs, scale)
    text_scale, text_back = powers([x[KINDS : KINDS + 1, :width] for x in col_parts], pairs, scale)
    back[...] = stack_rows((image_back, text_back), back.shape, 0)
    text, image, high_ref, low_ref, row_terms, col_terms = refs
    for p in range(nc):
        text[block(p, b), :] = st[p][...]
    for p in range(nr):
        image[block(p, b), :] = si[p][...]
    tiles = []
    for q in range(nr // 2):
        x = jnp.concatenate([row_parts[q][:, block(p ^ q, b)] for p in range(nr)], 1)
        for core in range(2):
            tiles.append([x[core * KINDS + k : core * KINDS + k + 1, :] for k in range(KINDS)])
    row_t, row_s, terms = combine(tiles, row_terms)
    row_share = sum_blocks(terms, b)
    rows = stack_rows((row_t, row_s), (LINES, nr * b), 0)
    tiles = []
    for q in range(nc):
        x = jnp.concatenate([col_parts[q][:, block(p ^ q, b)] for p in range(nc)], 1)
        tiles.append([x[k : k + 1, :] for k in range(KINDS)])
    col_t, col_s, terms = combine(tiles, col_terms)
    col_share = sum_blocks(terms, b)
    half = nr // 2
    for p in range(nr):
        row = jnp.transpose(rows[:, block(p, b)])
        tl, sl = tl_ref[block(p, b), :], sl_ref[block(p, b), :]
        delta = (jnp.exp2(sl - row[:, 1:2]) - jnp.exp2(tl - row[:, 0:1])) + (
            jnp.exp2(sl - col_s) - jnp.exp2(tl - col_t)
        )
        high = delta.astype(BF16)
        high_ref[block(p, b), :] = high
        low_ref[block(p, b), :] = (delta - high.astype(F32)).astype(BF16)
    image_share[...] = jnp.broadcast_to(col_share, image_share.shape)
    text_share[...] = jnp.broadcast_to(row_share, text_share.shape)
    step = 2 if half % 2 == 0 else 1
    for p in range(0, nr, step):
        rows = slice(p * b, (p + step) * b)
        part = (matmul(high_ref[rows, :], text[...], 1, 0) + matmul(low_ref[rows, :], text[...], 1, 0)) * image_scale
        if p < half:
            image_keep[rows, :] = part
        else:
            image_send[(p - half) * b : (p - half + step) * b, :] = part
    half = nc // 2
    step = 2 if half % 2 == 0 else 1
    for p in range(0, nc, step):
        cols = slice(p * b, (p + step) * b)
        part = (matmul(high_ref[:, cols], image[...], 0, 0) + matmul(low_ref[:, cols], image[...], 0, 0)) * text_scale
        if p < half:
            text_keep[cols, :] = part
        else:
            text_send[(p - half) * b : (p - half + step) * b, :] = part


def call(kernel, outs, args, scratch=(), flops=0, transcendentals=0):
    shapes = [jax.ShapeDtypeStruct(s, d) for s, d in outs]
    size = sum(x.size * x.dtype.itemsize for x in list(args) + shapes)
    return pl.pallas_call(
        kernel,
        out_shape=shapes,
        in_specs=[SMEM if x.dtype == jnp.int32 else VMEM for x in args],
        out_specs=[VMEM] * len(shapes),
        scratch_shapes=[pltpu.VMEM(s, d) for s, d in scratch],
        compiler_params=PARAMS,
        cost_estimate=pl.CostEstimate(flops=flops, bytes_accessed=size, transcendentals=transcendentals),
    )(*args)


def swap(bits, x):
    perm = [(i, i ^ ((1 << len(bits)) - 1)) for i in range(1 << len(bits))]
    return lax.ppermute(x, bits, perm)


def subset(bits, q):
    return tuple(b for k, b in enumerate(bits) if q >> k & 1)


def together(*groups):
    return lax.optimization_barrier(groups)


def stage_of(bits, pair, part, p):
    count = bin(p).count("1")
    late = count == 2 and pair in subset(bits, p)
    if part == 0:
        return 0 if count == 1 else count + (late and p & 1)
    return 1 if count == 1 and p > 1 else count + 1 + late


def gather(image_bits, text_bits, image, text):
    groups = [(image_bits, image), (text_bits, text)]
    have = {(n, part, 0): x for n, (_, own) in enumerate(groups) for part, x in enumerate(own)}
    stages = {}
    for n, (bits, _) in enumerate(groups):
        for part in range(2):
            for p in range(1, 1 << len(bits)):
                stages.setdefault(stage_of(bits, image_bits[-1], part, p), []).append((n, part, p))
    for stage in sorted(stages):
        top = {key: 1 << key[2].bit_length() - 1 for key in stages[stage]}
        sources = {key: have[key[0], key[1], key[2] ^ top[key]] for key in stages[stage]}
        if stage:
            gates = [x for key, x in have.items() if key[2] and (stage > 1 or key[2] > 1)]
            sources, _ = together(sources, gates)
        for key, x in sources.items():
            have[key] = swap(subset(groups[key[0]][0], top[key]), x)
    return [[have[n, part, p] for p in range(1 << len(bits))] for n, (bits, _) in enumerate(groups) for part in range(2)]


def halves(x):
    return x[: x.shape[0] // 2], x[x.shape[0] // 2 :]


def local(image_bits, text_bits, teacher_image, teacher_text, student_image, student_text):
    b, tw = teacher_image.shape
    sw = student_image.shape[1]
    nr, nc = 1 << len(image_bits), 1 << len(text_bits)
    r, c = nr * b, nc * b
    pair, others = image_bits[-1:], image_bits[:-1]
    ti, si, tt, st = gather(image_bits, text_bits, (teacher_image, student_image), (teacher_text, student_text))
    core = lax.axis_index(pair).astype(jnp.int32).reshape(1)
    tl, sl, rows, rows_swapped, cols = call(
        functools.partial(stats_kernel, nr, nc, b, tw**-0.5, sw**-0.5),
        [((r, c), F32), ((r, c), F32), ((LINES, r), F32), ((LINES, r), F32), ((LINES, c), F32)],
        [core] + ti + si + tt + st, [((c, tw), BF16), ((c, sw), BF16)], 2 * r * c * (tw + sw), 4 * r * c,
    )
    other = swap(pair, rows_swapped)
    col_parts = [cols] + [swap(subset(text_bits, q), cols) for q in range(1, nc)]
    rows = rows + other
    row_parts = [rows] + [swap(subset(others, q), rows) for q in range(1, nr // 2)]
    pairs = b << (len(image_bits) + len(text_bits))
    lanes = ((8, 128), F32)
    image_keep, image_send, text_keep, text_send, back, image_share, text_share = call(
        functools.partial(gradient_kernel, nr, nc, b, pairs, sw**-0.5),
        [((n, sw), F32) for n in (r // 2, r // 2, c // 2, c // 2)] + [((8, sw), F32), lanes, lanes],
        si + st + [tl, sl] + row_parts + col_parts,
        [((c, sw), BF16), ((r, sw), BF16), ((r, c), BF16), ((r, c), BF16), ((nr, r), F32), ((max(nc, 8), c), F32)],
        8 * r * c * sw, 4 * r * c,
    )
    image_keep, image_send = halves(image_keep + swap(pair, image_send))
    image_share = image_share + swap(pair, image_share)
    for k in reversed(range(max(len(text_bits), len(others)))):
        todo = {}
        if k < len(text_bits):
            todo["text"] = [text_send.astype(F16), text_share]
        if k < len(others):
            todo["image"] = [image_send.astype(F16), image_share]
        (todo,) = together(todo)
        if k < len(text_bits):
            come, share = [swap(text_bits[k : k + 1], x) for x in todo["text"]]
            text_total, text_share = text_keep + come.astype(F32), text_share + share
            text_keep, text_send = halves(text_total)
        if k < len(others):
            come, share = [swap(others[k : k + 1], x) for x in todo["image"]]
            image_total, image_share = image_keep + come.astype(F32), image_share + share
            image_keep, image_send = halves(image_total)
    loss = (image_share[0, 0] + text_share[0, 0]) / (2.0 * pairs)
    return (loss, image_total * back[0:1], text_total * back[1:2])


def solution(mesh):
    bits = {axis: [f"{axis}{k}" for k in reversed(range(mesh.shape[axis].bit_length() - 1))] for axis in ("img", "txt")}
    names = bits["img"] + bits["txt"]
    cube = Mesh(np.asarray(mesh.devices).reshape((2,) * len(names)), names)
    text_bits = [x for x in bits["img"] if int(x[3:]) >= 1] + [x for x in bits["txt"] if int(x[3:]) % 2 == 1]
    image_bits = [x for x in names if x not in text_bits]
    image, text = P(tuple(names), None), P(tuple(bits["txt"] + bits["img"]), None)
    return jax.shard_map(
        functools.partial(local, tuple(image_bits), tuple(text_bits)),
        mesh=cube,
        in_specs=(image, text, image, text),
        out_specs=(P(), image, text),
        check_vma=False,
    )
```

```python
import functools

import jax
import jax.numpy as jnp
import numpy as np
from jax import lax
from jax.experimental import pallas as pl
from jax.experimental.pallas import tpu as pltpu
from jax.sharding import Mesh, PartitionSpec as P

F32 = jnp.float32
BF16 = jnp.bfloat16
F16 = jnp.float16
LOG2E = 1.4426950408889634
LN2 = 0.6931471805599453
LINES = 8
KINDS = 3
PARAMS = pltpu.CompilerParams(vmem_limit_bytes=56 * 2**20)
VMEM = pl.BlockSpec(memory_space=pltpu.VMEM)
SMEM = pl.BlockSpec(memory_space=pltpu.SMEM)


def matmul(a, b, da, db):
    return lax.dot_general(a, b, (((da,), (db,)), ((), ())), preferred_element_type=F32)


def block(k, b):
    return slice(k * b, (k + 1) * b)


def stack_rows(values, shape, axis, first=0):
    index = lax.broadcasted_iota(jnp.int32, shape, axis) - first
    out = jnp.zeros(shape, F32)
    for k, value in enumerate(values):
        out = jnp.where(index == k, value, out)
    return out


def tree(op, items):
    while len(items) > 1:
        items = [op(x, y) for x, y in zip(items[::2], items[1::2])]
    return items[0]


def stats_kernel(nr, nc, b, tw, scale_t, scale_s, core, *refs):
    images, texts, refs = refs[:nr], refs[nr : nr + nc], refs[nr + nc :]
    tl_ref, sl_ref, row_ref, swap_ref, col_ref, text_t, text_s = refs
    for p in range(nc):
        text_t[block(p, b), :] = texts[p][:, :tw]
        text_s[block(p, b), :] = texts[p][:, tw:]
    largest = [
        functools.reduce(jnp.maximum, [jnp.max(jnp.abs(x[:, tw:].astype(F32)), 0, keepdims=True) for x in xs])
        for xs in (images, texts)
    ]
    width = largest[0].shape[1]

    def with_largest(flat, k):
        if (k + 1) * b > width:
            return flat
        return flat + stack_rows((largest[1][:, block(k, b)],), flat.shape, 0, 2 * KINDS + core[0])

    step = 2 if nr % 2 == 0 else 1
    count = step * b
    peak_t = peak_s = None
    for p in range(0, nr, step):
        rows = slice(p * b, p * b + count)
        tl = matmul(jnp.concatenate([x[:, :tw] for x in images[p : p + step]], 0), text_t[...], 1, 1) * (scale_t * LOG2E)
        sl = matmul(jnp.concatenate([x[:, tw:] for x in images[p : p + step]], 0), text_s[...], 1, 1) * (scale_s * LOG2E)
        tl_ref[rows, :] = tl
        sl_ref[rows, :] = sl
        top_t, top_s = jnp.max(tl, 0, keepdims=True), jnp.max(sl, 0, keepdims=True)
        peak_t = top_t if peak_t is None else jnp.maximum(peak_t, top_t)
        peak_s = top_s if peak_s is None else jnp.maximum(peak_s, top_s)
        mt, ms = jnp.max(tl, 1, keepdims=True), jnp.max(sl, 1, keepdims=True)
        et = jnp.exp2(tl - mt)
        sum_t = jnp.sum(et, 1, keepdims=True)
        gap = jnp.sum(et * (tl - sl), 1, keepdims=True)
        sum_s = jnp.sum(jnp.exp2(sl - ms), 1, keepdims=True)
        lines = (mt + jnp.log2(sum_t), ms + jnp.log2(sum_s), gap / sum_t)
        lines = stack_rows(lines, (count, 128), 1, core[0] * KINDS)
        for k in range(step):
            flat = jnp.transpose(lines[block(k, b)])[:LINES]
            other = (p + k) ^ (nr // 2)
            row_ref[:, block(p + k, b)] = with_largest(flat, p + k)
            swap_ref[:, block(other, b)] = with_largest(flat, other)
    sum_t = sum_s = gap = None
    for p in range(0, nr, step):
        tl, sl = tl_ref[p * b : p * b + count, :], sl_ref[p * b : p * b + count, :]
        et = jnp.exp2(tl - peak_t)
        parts = [
            jnp.sum(et, 0, keepdims=True),
            jnp.sum(jnp.exp2(sl - peak_s), 0, keepdims=True),
            jnp.sum(et * (tl - sl), 0, keepdims=True),
        ]
        sum_t, sum_s, gap = parts if p == 0 else [x + y for x, y in zip((sum_t, sum_s, gap), parts)]
    lines = (peak_t + jnp.log2(sum_t), peak_s + jnp.log2(sum_s), gap / sum_t)
    most = largest[0]
    if col_ref.shape[1] > width:
        most = jnp.concatenate([most, jnp.zeros((1, col_ref.shape[1] - width), F32)], 1)
    col_ref[...] = stack_rows(lines + (most,), col_ref.shape, 0)


def combine(tiles, terms):
    lses = []
    for kind in (1, 0):
        peak = tree(jnp.maximum, [x[kind] for x in tiles])
        weights = [jnp.exp2(x[kind] - peak) for x in tiles]
        total = tree(jnp.add, weights)
        lses.append(peak + jnp.log2(total))
    for k, (w, x) in enumerate(zip(weights, tiles)):
        terms[k : k + 1, :] = w * x[2]
    gap = tree(jnp.add, [terms[k : k + 1, :] for k in range(len(tiles))])
    return lses[1], lses[0], gap / total + (lses[0] - lses[1])


def sum_blocks(x, b):
    parts = [jnp.sum(x[:, block(p, b)], axis=(0, 1), keepdims=True) for p in range(x.shape[1] // b)]
    return tree(jnp.add, parts) * LN2


def powers(largest, pairs, scale):
    bound = functools.reduce(jnp.maximum, largest) * ((1 + pairs) * scale)
    power = jnp.ceil(jnp.log2(jnp.maximum(bound, 1e-30)))
    return jnp.exp2(15.0 - power) * scale, jnp.exp2(power - 15.0)


def gradient_kernel(nr, nc, b, tw, pairs, scale, *refs):
    images, texts, refs = refs[:nr], refs[nr : nr + nc], refs[nr + nc :]
    tl_ref, sl_ref, refs = refs[0], refs[1], refs[2:]
    row_parts, refs = refs[: nr // 2], refs[nr // 2 :]
    col_parts, refs = refs[:nc], refs[nc:]
    image_parts, text_parts, refs = refs[:4], refs[4:6], refs[6:]
    back, image_share, text_share, refs = *refs[:3], refs[3:]
    width = back.shape[1]
    lines = [x[2 * KINDS + core : 2 * KINDS + core + 1, :width] for x in row_parts for core in range(2)]
    image_scale, image_back = powers(lines, pairs, scale)
    text_scale, text_back = powers([x[KINDS : KINDS + 1, :width] for x in col_parts], pairs, scale)
    back[...] = stack_rows((image_back, text_back), back.shape, 0)
    text, image, high_ref, low_ref, row_terms, col_terms = refs
    for p in range(nc):
        text[block(p, b), :] = texts[p][:, tw:]
    for p in range(nr):
        image[block(p, b), :] = images[p][:, tw:]
    tiles = []
    for q in range(nr // 2):
        x = jnp.concatenate([row_parts[q][:, block(p ^ q, b)] for p in range(nr)], 1)
        for core in range(2):
            tiles.append([x[core * KINDS + k : core * KINDS + k + 1, :] for k in range(KINDS)])
    row_t, row_s, terms = combine(tiles, row_terms)
    row_share = sum_blocks(terms, b)
    rows = stack_rows((row_t, row_s), (LINES, nr * b), 0)
    tiles = []
    for q in range(nc):
        x = jnp.concatenate([col_parts[q][:, block(p ^ q, b)] for p in range(nc)], 1)
        tiles.append([x[k : k + 1, :] for k in range(KINDS)])
    col_t, col_s, terms = combine(tiles, col_terms)
    col_share = sum_blocks(terms, b)
    for p in range(nr):
        row = jnp.transpose(rows[:, block(p, b)])
        tl, sl = tl_ref[block(p, b), :], sl_ref[block(p, b), :]
        delta = (jnp.exp2(sl - row[:, 1:2]) - jnp.exp2(tl - row[:, 0:1])) + (
            jnp.exp2(sl - col_s) - jnp.exp2(tl - col_t)
        )
        high = delta.astype(BF16)
        high_ref[block(p, b), :] = high
        low_ref[block(p, b), :] = (delta - high.astype(F32)).astype(BF16)
    image_share[...] = jnp.broadcast_to(col_share, image_share.shape)
    text_share[...] = jnp.broadcast_to(row_share, text_share.shape)
    quarter = nr // 4
    for n in (3, 2, 1, 0):
        rows = slice(n * quarter * b, (n + 1) * quarter * b)
        part = matmul(high_ref[rows, :], text[...], 1, 0) + matmul(low_ref[rows, :], text[...], 1, 0)
        image_parts[n][...] = part * image_scale
    half = nc // 2
    for n in (1, 0):
        cols = slice(n * half * b, (n + 1) * half * b)
        part = matmul(high_ref[:, cols], image[...], 0, 0) + matmul(low_ref[:, cols], image[...], 0, 0)
        text_parts[n][...] = part * text_scale


def call(kernel, outs, args, scratch=(), flops=0, transcendentals=0):
    shapes = [jax.ShapeDtypeStruct(s, d) for s, d in outs]
    size = sum(x.size * x.dtype.itemsize for x in list(args) + shapes)
    return pl.pallas_call(
        kernel,
        out_shape=shapes,
        in_specs=[SMEM if x.dtype == jnp.int32 else VMEM for x in args],
        out_specs=[VMEM] * len(shapes),
        scratch_shapes=[pltpu.VMEM(s, d) for s, d in scratch],
        compiler_params=PARAMS,
        cost_estimate=pl.CostEstimate(flops=flops, bytes_accessed=size, transcendentals=transcendentals),
    )(*args)


def swap(bits, x):
    perm = [(i, i ^ ((1 << len(bits)) - 1)) for i in range(1 << len(bits))]
    return lax.ppermute(x, bits, perm)


def subset(bits, q):
    return tuple(b for k, b in enumerate(bits) if q >> k & 1)


def together(*groups):
    return lax.optimization_barrier(groups)


def gather(bits, x):
    blocks = [x]
    for bit in bits:
        blocks = blocks + [swap((bit,), y) for y in blocks]
    return blocks


def halves(x):
    return x[: x.shape[0] // 2], x[x.shape[0] // 2 :]


def local(image_bits, text_bits, teacher_image, teacher_text, student_image, student_text):
    b, tw = teacher_image.shape
    sw = student_image.shape[1]
    nr, nc = 1 << len(image_bits), 1 << len(text_bits)
    r, c = nr * b, nc * b
    pair, others = image_bits[-1:], image_bits[:-1]
    images = gather(image_bits, jnp.concatenate([teacher_image, student_image], 1))
    texts = gather(text_bits, jnp.concatenate([teacher_text, student_text], 1))
    core = lax.axis_index(pair).astype(jnp.int32).reshape(1)
    tl, sl, rows, rows_swapped, cols = call(
        functools.partial(stats_kernel, nr, nc, b, tw, tw**-0.5, sw**-0.5),
        [((r, c), F32), ((r, c), F32), ((LINES, r), F32), ((LINES, r), F32), ((LINES, c), F32)],
        [core] + images + texts, [((c, tw), BF16), ((c, sw), BF16)], 2 * r * c * (tw + sw), 4 * r * c,
    )
    other = swap(pair, rows_swapped)
    col_parts = [cols] + [swap(subset(text_bits, q), cols) for q in range(1, nc)]
    rows = rows + other
    row_parts = [rows] + [swap(subset(others, q), rows) for q in range(1, nr // 2)]
    pairs = b << (len(image_bits) + len(text_bits))
    lanes = ((8, 128), F32)
    near, far, other_near, other_far, text_keep, text_send, back, image_share, text_share = call(
        functools.partial(gradient_kernel, nr, nc, b, tw, pairs, sw**-0.5),
        [((r // 4, sw), F32)] * 4 + [((c // 2, sw), F32)] * 2 + [((8, sw), F32), lanes, lanes],
        images + texts + [tl, sl] + row_parts + col_parts,
        [((c, sw), BF16), ((r, sw), BF16), ((r, c), BF16), ((r, c), BF16), ((nr, r), F32), ((max(nc, 8), c), F32)],
        8 * r * c * sw, 4 * r * c,
    )
    image_send = far + swap(pair, other_far)
    image_keep = near + swap(pair, other_near)
    image_share = image_share + swap(pair, image_share)
    text_share = text_share + swap(text_bits[-1:], text_share)
    for k in reversed(range(max(len(text_bits), len(others)))):
        todo = {}
        if k < len(text_bits):
            todo["text"] = [text_send.astype(F16)]
        if 0 < k < len(text_bits):
            todo["text"].append(text_share)
        if k < len(others):
            todo["image"] = [image_send.astype(F16), image_share]
        (todo,) = together(todo)
        if k < len(text_bits):
            text_total = text_keep + swap(text_bits[k : k + 1], todo["text"][0]).astype(F32)
            text_keep, text_send = halves(text_total)
        if 0 < k < len(text_bits):
            text_share = todo["text"][1] + swap(text_bits[k - 1 : k], todo["text"][1])
        if k < len(others):
            image_total = image_keep + swap(others[k : k + 1], todo["image"][0]).astype(F32)
            image_keep, image_send = halves(image_total)
            image_share = todo["image"][1] + swap(others[k : k + 1], todo["image"][1])
    loss = (image_share[0, 0] + text_share[0, 0]) / (2.0 * pairs)
    return (loss, image_total * back[0:1], text_total * back[1:2])


def solution(mesh):
    bits = {axis: [f"{axis}{k}" for k in reversed(range(mesh.shape[axis].bit_length() - 1))] for axis in ("img", "txt")}
    names = bits["img"] + bits["txt"]
    cube = Mesh(np.asarray(mesh.devices).reshape((2,) * len(names)), names)
    image_bits = bits["img"][:-1] + [x for x in bits["txt"] if int(x[3:]) % 2 == 0]
    text_bits = [x for x in names if x not in image_bits]
    image, text = P(tuple(names), None), P(tuple(bits["txt"] + bits["img"]), None)
    return jax.shard_map(
        functools.partial(local, tuple(image_bits), tuple(text_bits)),
        mesh=cube,
        in_specs=(image, text, image, text),
        out_specs=(P(), image, text),
        check_vma=False,
    )
```

```python
import functools
import math

import jax
import jax.numpy as jnp
import numpy as np
from jax import lax
from jax.experimental import pallas as pl
from jax.experimental.pallas import tpu as pltpu
from jax.sharding import Mesh, PartitionSpec as P

F32 = jnp.float32
BF16 = jnp.bfloat16
F16 = jnp.float16
LOG2E = 1.4426950408889634
LN2 = 0.6931471805599453
LINES = 8
KINDS = 3
EXTRA = 16
DIGITS = (64.0, 2.0**-4, 2.0**-14, 2.0**-24, 2.0**-34)
ROOM = 12 * 2**20
VMEM = pl.BlockSpec(memory_space=pltpu.VMEM)
SMEM = pl.BlockSpec(memory_space=pltpu.SMEM)


def matmul(a, b, da, db):
    return lax.dot_general(a, b, (((da,), (db,)), ((), ())), preferred_element_type=F32)


def block(k, b):
    return slice(k * b, (k + 1) * b)


def stack_rows(values, shape, axis, first=0):
    index = lax.broadcasted_iota(jnp.int32, shape, axis) - first
    out = jnp.zeros(shape, F32)
    for k, value in enumerate(values):
        out = jnp.where(index == k, value, out)
    return out


def tree(op, items):
    while len(items) > 1:
        items = [op(x, y) for x, y in zip(items[::2], items[1::2])]
    return items[0]


def stats_kernel(nr, nc, b, tw, scale_t, scale_s, core, *refs):
    images, texts, refs = refs[:nr], refs[nr : nr + nc], refs[nr + nc :]
    tl_ref, sl_ref, row_ref, swap_ref, col_ref, image_s, text_s, text_t = refs
    for p in range(nc):
        text_t[block(p, b), :] = texts[p][:, :tw]
        text_s[block(p, b), :] = texts[p][:, tw:]
    for p in range(nr):
        image_s[block(p, b), :] = images[p][:, tw:]
    largest = [
        functools.reduce(jnp.maximum, [jnp.max(jnp.abs(x[block(p, b), :].astype(F32)), 0, keepdims=True) for p in range(n)])
        for x, n in ((image_s, nr), (text_s, nc))
    ]
    width = largest[0].shape[1]

    def with_largest(flat, k):
        if (k + 1) * b > width:
            return flat
        return flat + stack_rows((largest[1][:, block(k, b)],), flat.shape, 0, 2 * KINDS + core[0])

    step = 2 if nr % 2 == 0 else 1
    count = step * b
    peak_t = peak_s = None
    for p in range(0, nr, step):
        rows = slice(p * b, p * b + count)
        tl = matmul(jnp.concatenate([x[:, :tw] for x in images[p : p + step]], 0), text_t[...], 1, 1) * (scale_t * LOG2E)
        sl = matmul(image_s[rows, :], text_s[...], 1, 1) * (scale_s * LOG2E)
        tl_ref[rows, :] = tl
        sl_ref[rows, :] = sl
        top_t, top_s = jnp.max(tl, 0, keepdims=True), jnp.max(sl, 0, keepdims=True)
        peak_t = top_t if peak_t is None else jnp.maximum(peak_t, top_t)
        peak_s = top_s if peak_s is None else jnp.maximum(peak_s, top_s)
        mt, ms = jnp.max(tl, 1, keepdims=True), jnp.max(sl, 1, keepdims=True)
        et = jnp.exp2(tl - mt)
        sum_t = jnp.sum(et, 1, keepdims=True)
        gap = jnp.sum(et * (tl - sl), 1, keepdims=True)
        sum_s = jnp.sum(jnp.exp2(sl - ms), 1, keepdims=True)
        lines = (mt + jnp.log2(sum_t), ms + jnp.log2(sum_s), gap / sum_t)
        lines = stack_rows(lines, (count, 128), 1, core[0] * KINDS)
        for k in range(step):
            flat = jnp.transpose(lines[block(k, b)])[:LINES]
            other = (p + k) ^ (nr // 2)
            row_ref[:, block(p + k, b)] = with_largest(flat, p + k)
            swap_ref[:, block(other, b)] = with_largest(flat, other)
    sum_t = sum_s = gap = None
    for p in range(0, nr, step):
        tl, sl = tl_ref[p * b : p * b + count, :], sl_ref[p * b : p * b + count, :]
        et = jnp.exp2(tl - peak_t)
        parts = [
            jnp.sum(et, 0, keepdims=True),
            jnp.sum(jnp.exp2(sl - peak_s), 0, keepdims=True),
            jnp.sum(et * (tl - sl), 0, keepdims=True),
        ]
        sum_t, sum_s, gap = parts if p == 0 else [x + y for x, y in zip((sum_t, sum_s, gap), parts)]
    lines = (peak_t + jnp.log2(sum_t), peak_s + jnp.log2(sum_s), gap / sum_t)
    most = largest[0]
    if col_ref.shape[1] > width:
        most = jnp.concatenate([most, jnp.zeros((1, col_ref.shape[1] - width), F32)], 1)
    col_ref[...] = stack_rows(lines + (most,), col_ref.shape, 0)


def join_kernel(teacher_image, student_image, teacher_text, student_text, image, text):
    tw = teacher_image.shape[1]
    image[:, :tw] = teacher_image[...]
    image[:, tw:] = student_image[...]
    text[:, :tw] = teacher_text[...]
    text[:, tw:] = student_text[...]


def digits(share, rank, slots, width):
    rows = []
    for unit in DIGITS:
        digit = jnp.floor(share * (1.0 / unit))
        share = share - digit * unit
        rows.append(digit)
    lane = lax.broadcasted_iota(jnp.int32, (EXTRA, width), 1)
    return jnp.where(lane // (width // slots) == rank, stack_rows(rows, (EXTRA, width), 0), 0.0)


def combine(tiles, terms):
    lses = []
    for kind in (1, 0):
        peak = tree(jnp.maximum, [x[kind] for x in tiles])
        weights = [jnp.exp2(x[kind] - peak) for x in tiles]
        total = tree(jnp.add, weights)
        lses.append(peak + jnp.log2(total))
    for k, (w, x) in enumerate(zip(weights, tiles)):
        terms[k : k + 1, :] = w * x[2]
    gap = tree(jnp.add, [terms[k : k + 1, :] for k in range(len(tiles))])
    return lses[1], lses[0], gap / total + (lses[0] - lses[1])


def sum_blocks(x, b):
    parts = [jnp.sum(x[:, block(p, b)], axis=(0, 1), keepdims=True) for p in range(x.shape[1] // b)]
    return tree(jnp.add, parts) * LN2


def powers(largest, pairs, scale):
    bound = functools.reduce(jnp.maximum, largest) * ((1 + pairs) * scale)
    power = jnp.ceil(jnp.log2(jnp.maximum(bound, 1e-30)))
    return jnp.exp2(15.0 - power) * scale, jnp.exp2(power - 15.0)


def gradient_kernel(nr, nc, b, pairs, scale, place, *refs):
    image, text, tl_ref, sl_ref, refs = *refs[:4], refs[4:]
    row_parts, refs = refs[: nr // 2], refs[nr // 2 :]
    col_parts, refs = refs[:nc], refs[nc:]
    image_parts, text_parts, refs = refs[:4], refs[4:6], refs[6:]
    image_back_ref, text_back_ref, refs = refs[0], refs[1], refs[2:]
    width = image_back_ref.shape[1]
    lines = [x[2 * KINDS + core : 2 * KINDS + core + 1, :width] for x in row_parts for core in range(2)]
    image_scale, image_back = powers(lines, pairs, scale)
    text_scale, text_back = powers([x[KINDS : KINDS + 1, :width] for x in col_parts], pairs, scale)
    image_back_ref[...] = image_back
    text_back_ref[...] = text_back
    high_ref, low_ref, row_terms, col_terms = refs
    tiles = []
    for q in range(nr // 2):
        x = jnp.concatenate([row_parts[q][:, block(p ^ q, b)] for p in range(nr)], 1)
        for core in range(2):
            tiles.append([x[core * KINDS + k : core * KINDS + k + 1, :] for k in range(KINDS)])
    row_t, row_s, terms = combine(tiles, row_terms)
    row_share = sum_blocks(terms, b)
    rows = stack_rows((row_t, row_s), (LINES, nr * b), 0)
    tiles = []
    for q in range(nc):
        x = jnp.concatenate([col_parts[q][:, block(p ^ q, b)] for p in range(nc)], 1)
        tiles.append([x[k : k + 1, :] for k in range(KINDS)])
    col_t, col_s, terms = combine(tiles, col_terms)
    col_share = sum_blocks(terms, b)
    for p in range(nr):
        row = jnp.transpose(rows[:, block(p, b)])
        tl, sl = tl_ref[block(p, b), :], sl_ref[block(p, b), :]
        delta = (jnp.exp2(sl - row[:, 1:2]) - jnp.exp2(tl - row[:, 0:1])) + (
            jnp.exp2(sl - col_s) - jnp.exp2(tl - col_t)
        )
        high = delta.astype(BF16)
        high_ref[block(p, b), :] = high
        low_ref[block(p, b), :] = (delta - high.astype(F32)).astype(BF16)
    image_extra = digits(col_share * (1.0 / (nc * b)), place[1], nr, width)
    text_extra = digits(row_share * (1.0 / (nr * b)), place[2], nc, width)
    quarter = nr // 4
    for n in (3, 2, 1, 0):
        rows = slice(n * quarter * b, (n + 1) * quarter * b)
        part = matmul(high_ref[rows, :], text[...], 1, 0) + matmul(low_ref[rows, :], text[...], 1, 0)
        image_parts[n][: quarter * b, :] = part * image_scale
        image_parts[n][quarter * b :, :] = image_extra
    half = nc // 2
    for n in (1, 0):
        cols = slice(n * half * b, (n + 1) * half * b)
        part = matmul(high_ref[:, cols], image[...], 0, 0) + matmul(low_ref[:, cols], image[...], 0, 0)
        text_parts[n][: half * b, :] = part * text_scale
        text_parts[n][half * b :, :] = text_extra


def call(kernel, outs, args, scratch=(), flops=0, transcendentals=0):
    shapes = [jax.ShapeDtypeStruct(s, d) for s, d in outs]
    size = sum(x.size * x.dtype.itemsize for x in list(args) + shapes)
    held = sum(math.prod(s) * jnp.dtype(d).itemsize for s, d in scratch)
    return pl.pallas_call(
        kernel,
        out_shape=shapes,
        in_specs=[SMEM if x.dtype == jnp.int32 else VMEM for x in args],
        out_specs=[VMEM] * len(shapes),
        scratch_shapes=[pltpu.VMEM(s, d) for s, d in scratch],
        compiler_params=pltpu.CompilerParams(vmem_limit_bytes=size + held + ROOM),
        cost_estimate=pl.CostEstimate(flops=flops, bytes_accessed=size, transcendentals=transcendentals),
    )(*args)


def swap(bits, x):
    perm = [(i, i ^ ((1 << len(bits)) - 1)) for i in range(1 << len(bits))]
    return lax.ppermute(x, bits, perm)


def subset(bits, q):
    return tuple(b for k, b in enumerate(bits) if q >> k & 1)


def together(*groups):
    return lax.optimization_barrier(groups)


def gather(bits, x):
    blocks = [x]
    for k, bit in enumerate(bits):
        own = together(x, blocks[2])[0] if k > 1 else x
        blocks = blocks + [swap((bit,), y) for y in [own] + blocks[1:]]
    return blocks


def add_message(keep, come):
    rows = keep[0].shape[0]
    come = come.astype(F32)
    return keep[0] + come[:rows], keep[1] + come[rows:]


def local(image_bits, text_bits, teacher_image, teacher_text, student_image, student_text):
    b, tw = teacher_image.shape
    sw = student_image.shape[1]
    nr, nc = 1 << len(image_bits), 1 << len(text_bits)
    r, c = nr * b, nc * b
    pair, others = image_bits[-1:], image_bits[:-1]
    whole = ((b, tw + sw), BF16)
    image, text = call(join_kernel, [whole, whole], [teacher_image, student_image, teacher_text, student_text])
    images, texts = gather(image_bits, image), gather(text_bits, text)
    place = jnp.stack([lax.axis_index(x) for x in (pair, image_bits, text_bits)]).astype(jnp.int32)
    tl, sl, rows, rows_swapped, cols, image, text = call(
        functools.partial(stats_kernel, nr, nc, b, tw, tw**-0.5, sw**-0.5),
        [((r, c), F32), ((r, c), F32), ((LINES, r), F32), ((LINES, r), F32), ((LINES, c), F32), ((r, sw), BF16), ((c, sw), BF16)],
        [place] + images + texts, [((c, tw), BF16)], 2 * r * c * (tw + sw), 4 * r * c,
    )
    other = swap(pair, rows_swapped)
    col_parts = [cols] + [swap(subset(text_bits, q), cols) for q in range(1, nc)]
    rows = rows + other
    row_parts = [rows] + [swap(subset(others, q), rows) for q in range(1, nr // 2)]
    pairs = b << (len(image_bits) + len(text_bits))
    near, far, other_near, other_far, text_keep, text_send, image_back, text_back = call(
        functools.partial(gradient_kernel, nr, nc, b, pairs, sw**-0.5),
        [((r // 4 + EXTRA, sw), F32)] * 4 + [((c // 2 + EXTRA, sw), F32)] * 2 + [((1, sw), F32)] * 2,
        [place, image, text, tl, sl] + row_parts + col_parts,
        [((r, c), BF16), ((r, c), BF16), ((nr, r), F32), ((max(nc, 8), c), F32)],
        8 * r * c * sw, 4 * r * c,
    )
    image_send = far + swap(pair, other_far)
    image_keep = near + swap(pair, other_near)
    image_keep, text_keep = [(x[:-EXTRA], x[-EXTRA:]) for x in (image_keep, text_keep)]
    for k in reversed(range(max(len(text_bits), len(others)))):
        todo = {}
        if k < len(text_bits):
            todo["text"] = text_send.astype(F16)
        if k < len(others):
            todo["image"] = image_send.astype(F16)
        (todo,) = together(todo)
        half = b << k >> 1
        if k < len(text_bits):
            body, extra = text_keep = add_message(text_keep, swap(text_bits[k : k + 1], todo["text"]))
            if k:
                text_keep, text_send = (body[:half], extra), jnp.concatenate([body[half:], extra])
        if k < len(others):
            body, extra = image_keep = add_message(image_keep, swap(others[k : k + 1], todo["image"]))
            if k:
                image_keep, image_send = (body[:half], extra), jnp.concatenate([body[half:], extra])
    units = stack_rows(DIGITS, (EXTRA, sw), 0)
    loss = jnp.sum((image_keep[1] + text_keep[1]) * units) * (0.5 / sw)
    return (loss, image_keep[0] * image_back, text_keep[0] * text_back)


def solution(mesh):
    bits = {axis: [f"{axis}{k}" for k in reversed(range(mesh.shape[axis].bit_length() - 1))] for axis in ("img", "txt")}
    names = bits["img"] + bits["txt"]
    cube = Mesh(np.asarray(mesh.devices).reshape((2,) * len(names)), names)
    image_bits = bits["img"][:-1] + [x for x in bits["txt"] if int(x[3:]) % 2 == 0]
    text_bits = [x for x in names if x not in image_bits]
    image, text = P(tuple(names), None), P(tuple(bits["txt"] + bits["img"]), None)
    return jax.shard_map(
        functools.partial(local, tuple(image_bits), tuple(text_bits)),
        mesh=cube,
        in_specs=(image, text, image, text),
        out_specs=(P(), image, text),
        check_vma=False,
    )
```

```python
import functools
import math

import jax
import jax.numpy as jnp
import numpy as np
from jax import lax
from jax.experimental import pallas as pl
from jax.experimental.pallas import tpu as pltpu
from jax.sharding import Mesh, PartitionSpec as P

F32 = jnp.float32
BF16 = jnp.bfloat16
F16 = jnp.float16
LOG2E = 1.4426950408889634
LN2 = 0.6931471805599453
LINES = 8
KINDS = 3
EXTRA = 16
DIGITS = (64.0, 2.0**-4, 2.0**-14, 2.0**-24, 2.0**-34)
MOST = 60 * 2**20
ROOM = 12 * 2**20
VMEM = pl.BlockSpec(memory_space=pltpu.VMEM)
SMEM = pl.BlockSpec(memory_space=pltpu.SMEM)


def matmul(a, b, da, db):
    return lax.dot_general(a, b, (((da,), (db,)), ((), ())), preferred_element_type=F32)


def block(k, b):
    return slice(k * b, (k + 1) * b)


def stack_rows(values, shape, axis, first=0):
    index = lax.broadcasted_iota(jnp.int32, shape, axis) - first
    out = jnp.zeros(shape, F32)
    for k, value in enumerate(values):
        out = jnp.where(index == k, value, out)
    return out


def tree(op, items):
    while len(items) > 1:
        items = [op(x, y) for x, y in zip(items[::2], items[1::2])]
    return items[0]


def stats_kernel(nr, nc, b, tw, scale_t, scale_s, core, *refs):
    images, texts, refs = refs[:nr], refs[nr : nr + nc], refs[nr + nc :]
    tl_ref, sl_ref, row_ref, swap_ref, col_ref, image_s, text_s, text_t = refs
    for p in range(nc):
        text_t[block(p, b), :] = texts[p][:, :tw]
        text_s[block(p, b), :] = texts[p][:, tw:]
    for p in range(nr):
        image_s[block(p, b), :] = images[p][:, tw:]
    largest = [
        functools.reduce(jnp.maximum, [jnp.max(jnp.abs(x[block(p, b), :].astype(F32)), 0, keepdims=True) for p in range(n)])
        for x, n in ((image_s, nr), (text_s, nc))
    ]
    width = largest[0].shape[1]

    def with_largest(flat, k):
        if (k + 1) * b > width:
            return flat
        return flat + stack_rows((largest[1][:, block(k, b)],), flat.shape, 0, 2 * KINDS + core[0])

    step = 2 if nr % 2 == 0 else 1
    count = step * b
    peak_t = peak_s = None
    for p in range(0, nr, step):
        rows = slice(p * b, p * b + count)
        tl = matmul(jnp.concatenate([x[:, :tw] for x in images[p : p + step]], 0), text_t[...], 1, 1) * (scale_t * LOG2E)
        sl = matmul(image_s[rows, :], text_s[...], 1, 1) * (scale_s * LOG2E)
        tl_ref[rows, :] = tl
        sl_ref[rows, :] = sl
        top_t, top_s = jnp.max(tl, 0, keepdims=True), jnp.max(sl, 0, keepdims=True)
        peak_t = top_t if peak_t is None else jnp.maximum(peak_t, top_t)
        peak_s = top_s if peak_s is None else jnp.maximum(peak_s, top_s)
        mt, ms = jnp.max(tl, 1, keepdims=True), jnp.max(sl, 1, keepdims=True)
        et = jnp.exp2(tl - mt)
        sum_t = jnp.sum(et, 1, keepdims=True)
        gap = jnp.sum(et * (tl - sl), 1, keepdims=True)
        sum_s = jnp.sum(jnp.exp2(sl - ms), 1, keepdims=True)
        lines = (mt + jnp.log2(sum_t), ms + jnp.log2(sum_s), gap / sum_t)
        lines = stack_rows(lines, (count, 128), 1, core[0] * KINDS)
        for k in range(step):
            flat = jnp.transpose(lines[block(k, b)])[:LINES]
            other = (p + k) ^ (nr // 2)
            row_ref[:, block(p + k, b)] = with_largest(flat, p + k)
            swap_ref[:, block(other, b)] = with_largest(flat, other)
    sum_t = sum_s = gap = None
    for p in range(0, nr, step):
        tl, sl = tl_ref[p * b : p * b + count, :], sl_ref[p * b : p * b + count, :]
        et = jnp.exp2(tl - peak_t)
        parts = [
            jnp.sum(et, 0, keepdims=True),
            jnp.sum(jnp.exp2(sl - peak_s), 0, keepdims=True),
            jnp.sum(et * (tl - sl), 0, keepdims=True),
        ]
        sum_t, sum_s, gap = parts if p == 0 else [x + y for x, y in zip((sum_t, sum_s, gap), parts)]
    lines = (peak_t + jnp.log2(sum_t), peak_s + jnp.log2(sum_s), gap / sum_t)
    most = largest[0]
    if col_ref.shape[1] > width:
        most = jnp.concatenate([most, jnp.zeros((1, col_ref.shape[1] - width), F32)], 1)
    col_ref[...] = stack_rows(lines + (most,), col_ref.shape, 0)


def join_kernel(teacher_image, student_image, teacher_text, student_text, image, text, sems):
    tw = teacher_image.shape[1]
    copies = [
        pltpu.make_async_copy(teacher_image, image.at[:, :tw], sems.at[0]),
        pltpu.make_async_copy(student_image, image.at[:, tw:], sems.at[1]),
        pltpu.make_async_copy(teacher_text, text.at[:, :tw], sems.at[2]),
        pltpu.make_async_copy(student_text, text.at[:, tw:], sems.at[3]),
    ]
    for copy in copies:
        copy.start()
    for copy in copies:
        copy.wait()


def digits(share, rank, slots, width):
    rows = []
    for unit in DIGITS:
        digit = jnp.floor(share * (1.0 / unit))
        share = share - digit * unit
        rows.append(digit)
    lane = lax.broadcasted_iota(jnp.int32, (EXTRA, width), 1)
    return jnp.where(lane // (width // slots) == rank, stack_rows(rows, (EXTRA, width), 0), 0.0)


def combine(tiles, terms):
    lses = []
    for kind in (1, 0):
        peak = tree(jnp.maximum, [x[kind] for x in tiles])
        weights = [jnp.exp2(x[kind] - peak) for x in tiles]
        total = tree(jnp.add, weights)
        lses.append(peak + jnp.log2(total))
    for k, (w, x) in enumerate(zip(weights, tiles)):
        terms[k : k + 1, :] = w * x[2]
    gap = tree(jnp.add, [terms[k : k + 1, :] for k in range(len(tiles))])
    return lses[1], lses[0], gap / total + (lses[0] - lses[1])


def sum_blocks(x, b):
    parts = [jnp.sum(x[:, block(p, b)], axis=(0, 1), keepdims=True) for p in range(x.shape[1] // b)]
    return tree(jnp.add, parts) * LN2


def powers(largest, pairs, scale):
    bound = functools.reduce(jnp.maximum, largest) * ((1 + pairs) * scale)
    power = jnp.ceil(jnp.log2(jnp.maximum(bound, 1e-30)))
    return jnp.exp2(15.0 - power) * scale, jnp.exp2(power - 15.0)


def split_lines(refs, n):
    views = []
    while len(views) < n:
        views += [refs[0].at[block(k, LINES), :] for k in range(refs[0].shape[0] // LINES)]
        refs = refs[1:]
    return views, refs


def gradient_kernel(nr, nc, b, pairs, scale, place, *refs):
    image, text, tl_ref, sl_ref, refs = *refs[:4], refs[4:]
    row_parts, refs = split_lines(refs, nr // 2)
    col_parts, refs = split_lines(refs, nc)
    image_parts, text_parts, refs = refs[:4], refs[4:6], refs[6:]
    image_back_ref, text_back_ref, refs = refs[0], refs[1], refs[2:]
    width = image_back_ref.shape[1]
    lines = [x[2 * KINDS + core : 2 * KINDS + core + 1, :width] for x in row_parts for core in range(2)]
    image_scale, image_back = powers(lines, pairs, scale)
    text_scale, text_back = powers([x[KINDS : KINDS + 1, :width] for x in col_parts], pairs, scale)
    image_back_ref[...] = image_back
    text_back_ref[...] = text_back
    high_ref, low_ref, row_terms, col_terms = refs
    tiles = []
    for q in range(nr // 2):
        x = jnp.concatenate([row_parts[q][:, block(p ^ q, b)] for p in range(nr)], 1)
        for core in range(2):
            tiles.append([x[core * KINDS + k : core * KINDS + k + 1, :] for k in range(KINDS)])
    row_t, row_s, terms = combine(tiles, row_terms)
    row_share = sum_blocks(terms, b)
    rows = stack_rows((row_t, row_s), (LINES, nr * b), 0)
    tiles = []
    for q in range(nc):
        x = jnp.concatenate([col_parts[q][:, block(p ^ q, b)] for p in range(nc)], 1)
        tiles.append([x[k : k + 1, :] for k in range(KINDS)])
    col_t, col_s, terms = combine(tiles, col_terms)
    col_share = sum_blocks(terms, b)
    for p in range(nr):
        row = jnp.transpose(rows[:, block(p, b)])
        tl, sl = tl_ref[block(p, b), :], sl_ref[block(p, b), :]
        delta = (jnp.exp2(sl - row[:, 1:2]) - jnp.exp2(tl - row[:, 0:1])) + (
            jnp.exp2(sl - col_s) - jnp.exp2(tl - col_t)
        )
        high = delta.astype(BF16)
        high_ref[block(p, b), :] = high
        low_ref[block(p, b), :] = (delta - high.astype(F32)).astype(BF16)
    image_extra = digits(col_share * (1.0 / (nc * b)), place[1], nr, width)
    text_extra = digits(row_share * (1.0 / (nr * b)), place[2], nc, width)
    quarter = nr // 4
    for n in (3, 2, 1, 0):
        rows = slice(n * quarter * b, (n + 1) * quarter * b)
        part = matmul(high_ref[rows, :], text[...], 1, 0) + matmul(low_ref[rows, :], text[...], 1, 0)
        image_parts[n][: quarter * b, :] = part * image_scale
        image_parts[n][quarter * b :, :] = image_extra
    half = nc // 2
    for n in (1, 0):
        cols = slice(n * half * b, (n + 1) * half * b)
        part = matmul(high_ref[:, cols], image[...], 0, 0) + matmul(low_ref[:, cols], image[...], 0, 0)
        text_parts[n][: half * b, :] = part * text_scale
        text_parts[n][half * b :, :] = text_extra


def call(kernel, outs, args, scratch=(), flops=0, transcendentals=0):
    shapes = [jax.ShapeDtypeStruct(s, d) for s, d in outs]
    size = sum(x.size * x.dtype.itemsize for x in list(args) + shapes)
    held = sum(math.prod(s) * jnp.dtype(d).itemsize for s, d in scratch)
    return pl.pallas_call(
        kernel,
        out_shape=shapes,
        in_specs=[SMEM if x.dtype == jnp.int32 else VMEM for x in args],
        out_specs=[VMEM] * len(shapes),
        scratch_shapes=[pltpu.VMEM(s, d) for s, d in scratch],
        compiler_params=pltpu.CompilerParams(vmem_limit_bytes=size + held + ROOM),
        cost_estimate=pl.CostEstimate(flops=flops, bytes_accessed=size, transcendentals=transcendentals),
    )(*args)


def swap(bits, x):
    perm = [(i, i ^ ((1 << len(bits)) - 1)) for i in range(1 << len(bits))]
    return lax.ppermute(x, bits, perm)


def subset(bits, q):
    return tuple(b for k, b in enumerate(bits) if q >> k & 1)


def together(*groups):
    return lax.optimization_barrier(groups)


def gather(bits, x):
    blocks = [x]
    for k, bit in enumerate(bits):
        own = together(x, blocks[2])[0] if k > 1 else x
        blocks = blocks + [swap((bit,), y) for y in [own] + blocks[1:]]
    return blocks


def exchange(bits, x):
    parts = [x]
    for bit in bits:
        parts.append(swap((bit,), jnp.concatenate(parts) if len(parts) > 1 else x))
    return parts


def start_step(send, b, gate):
    half = 0 if send.shape[0] - EXTRA == b else (send.shape[0] - EXTRA) // 2
    if not half:
        return [send.astype(F16)]
    return [send[half:].astype(F16), together(send[:half].astype(F16), gate)[0]]


def end_step(keep, come, b):
    if len(come) == 1:
        return (keep[0] + come[0][:b].astype(F32), keep[1] + come[0][b:].astype(F32)), None
    half = come[1].shape[0]
    on = keep[half:] + come[0].astype(F32)
    keep = keep[:half] + come[1].astype(F32), on[half:]
    return keep if half == b else jnp.concatenate(keep), on


def local(image_bits, text_bits, teacher_image, teacher_text, student_image, student_text):
    b, tw = teacher_image.shape
    sw = student_image.shape[1]
    nr, nc = 1 << len(image_bits), 1 << len(text_bits)
    r, c = nr * b, nc * b
    pair, others = image_bits[-1:], image_bits[:-1]
    whole = jax.ShapeDtypeStruct((b, tw + sw), BF16)
    image, text = pl.pallas_call(
        join_kernel,
        out_shape=[whole, whole],
        in_specs=[pl.BlockSpec(memory_space=pltpu.HBM)] * 4,
        out_specs=[VMEM] * 2,
        scratch_shapes=[pltpu.SemaphoreType.DMA((4,))],
        compiler_params=pltpu.CompilerParams(vmem_limit_bytes=MOST),
    )(teacher_image, student_image, teacher_text, student_text)
    images, texts = gather(image_bits, image), gather(text_bits, text)
    place = jnp.stack([lax.axis_index(x) for x in (pair, image_bits, text_bits)]).astype(jnp.int32)
    tl, sl, rows, rows_swapped, cols, image, text = call(
        functools.partial(stats_kernel, nr, nc, b, tw, tw**-0.5, sw**-0.5),
        [((r, c), F32), ((r, c), F32), ((LINES, r), F32), ((LINES, r), F32), ((LINES, c), F32), ((r, sw), BF16), ((c, sw), BF16)],
        [place] + images + texts, [((c, tw), BF16)], 2 * r * c * (tw + sw), 4 * r * c,
    )
    other = swap(pair, rows_swapped)
    row_parts, col_parts = exchange(others, rows + other), exchange(text_bits, cols)
    pairs = b << (len(image_bits) + len(text_bits))
    near, far, other_near, other_far, text_keep, text_send, image_back, text_back = call(
        functools.partial(gradient_kernel, nr, nc, b, pairs, sw**-0.5),
        [((r // 4 + EXTRA, sw), F32)] * 4 + [((c // 2 + EXTRA, sw), F32)] * 2 + [((1, sw), F32)] * 2,
        [place, image, text, tl, sl] + row_parts + col_parts,
        [((r, c), BF16), ((r, c), BF16), ((nr, r), F32), ((max(nc, 8), c), F32)],
        8 * r * c * sw, 4 * r * c,
    )
    image_send = far + swap(pair, other_far)
    image_keep = near + swap(pair, other_near)
    for k in reversed(range(max(len(text_bits), len(others)))):
        todo = {}
        if k < len(text_bits):
            todo["text"] = start_step(text_send, b, image_keep)
        if k < len(others):
            todo["image"] = start_step(image_send, b, image_keep)
        first = {name: x[0] for name, x in todo.items()}
        (first,) = together(first)
        todo = {name: [first[name]] + x[1:] for name, x in todo.items()}
        if k < len(text_bits):
            text_keep, text_send = end_step(text_keep, [swap(text_bits[k : k + 1], x) for x in todo["text"]], b)
        if k < len(others):
            image_keep, image_send = end_step(image_keep, [swap(others[k : k + 1], x) for x in todo["image"]], b)
    units = stack_rows(DIGITS, (EXTRA, sw), 0)
    loss = jnp.sum((image_keep[1] + text_keep[1]) * units) * (0.5 / sw)
    return (loss, image_keep[0] * image_back, text_keep[0] * text_back)


def solution(mesh):
    bits = {axis: [f"{axis}{k}" for k in reversed(range(mesh.shape[axis].bit_length() - 1))] for axis in ("img", "txt")}
    names = bits["img"] + bits["txt"]
    cube = Mesh(np.asarray(mesh.devices).reshape((2,) * len(names)), names)
    image_bits = bits["img"][:-1] + [x for x in bits["txt"] if int(x[3:]) % 2 == 0]
    text_bits = [x for x in names if x not in image_bits]
    image, text = P(tuple(names), None), P(tuple(bits["txt"] + bits["img"]), None)
    return jax.shard_map(
        functools.partial(local, tuple(image_bits), tuple(text_bits)),
        mesh=cube,
        in_specs=(image, text, image, text),
        out_specs=(P(), image, text),
        check_vma=False,
    )
```

```python
import functools
import math

import jax
import jax.numpy as jnp
import numpy as np
from jax import lax
from jax.experimental import pallas as pl
from jax.experimental.pallas import tpu as pltpu
from jax.sharding import Mesh, PartitionSpec as P

F32 = jnp.float32
BF16 = jnp.bfloat16
F16 = jnp.float16
LOG2E = 1.4426950408889634
LN2 = 0.6931471805599453
LINES = 8
KINDS = 3
EXTRA = 16
DIGITS = (64.0, 2.0**-4, 2.0**-14, 2.0**-24, 2.0**-34)
ROOM = 12 * 2**20
VMEM = pl.BlockSpec(memory_space=pltpu.VMEM)
SMEM = pl.BlockSpec(memory_space=pltpu.SMEM)


def matmul(a, b, da, db):
    return lax.dot_general(a, b, (((da,), (db,)), ((), ())), preferred_element_type=F32)


def block(k, b):
    return slice(k * b, (k + 1) * b)


def stack_rows(values, shape, axis, first=0):
    index = lax.broadcasted_iota(jnp.int32, shape, axis) - first
    out = jnp.zeros(shape, F32)
    for k, value in enumerate(values):
        out = jnp.where(index == k, value, out)
    return out


def tree(op, items):
    while len(items) > 1:
        items = [op(x, y) for x, y in zip(items[::2], items[1::2])]
    return items[0]


def stats_kernel(nr, nc, b, tw, scale_t, scale_s, core, *refs):
    images, texts, refs = refs[:nr], refs[nr : nr + nc], refs[nr + nc :]
    tl_ref, sl_ref, row_ref, swap_ref, peak_ref, image_s, text_s, text_t = refs
    for p in range(nc):
        text_t[block(p, b), :] = texts[p][:, :tw]
        text_s[block(p, b), :] = texts[p][:, tw:]
    for p in range(nr):
        image_s[block(p, b), :] = images[p][:, tw:]
    largest = jnp.max(jnp.abs(text_s[...].astype(F32)), 0, keepdims=True)
    width = largest.shape[1]

    def with_largest(flat, k):
        if (k + 1) * b > width:
            return flat
        return flat + stack_rows((largest[:, block(k, b)],), flat.shape, 0, 2 * KINDS + core[0])

    step = 2 if nr % 2 == 0 else 1
    count = step * b
    peak_t = peak_s = None
    for p in range(0, nr, step):
        rows = slice(p * b, p * b + count)
        tl = matmul(jnp.concatenate([x[:, :tw] for x in images[p : p + step]], 0), text_t[...], 1, 1) * (scale_t * LOG2E)
        sl = matmul(image_s[rows, :], text_s[...], 1, 1) * (scale_s * LOG2E)
        tl_ref[rows, :] = tl
        sl_ref[rows, :] = sl
        top_t, top_s = jnp.max(tl, 0, keepdims=True), jnp.max(sl, 0, keepdims=True)
        peak_t = top_t if peak_t is None else jnp.maximum(peak_t, top_t)
        peak_s = top_s if peak_s is None else jnp.maximum(peak_s, top_s)
        mt, ms = jnp.max(tl, 1, keepdims=True), jnp.max(sl, 1, keepdims=True)
        et = jnp.exp2(tl - mt)
        sum_t = jnp.sum(et, 1, keepdims=True)
        gap = jnp.sum(et * (tl - sl), 1, keepdims=True)
        sum_s = jnp.sum(jnp.exp2(sl - ms), 1, keepdims=True)
        lines = (mt + jnp.log2(sum_t), ms + jnp.log2(sum_s), gap / sum_t)
        lines = stack_rows(lines, (count, 128), 1, core[0] * KINDS)
        for k in range(step):
            flat = jnp.transpose(lines[block(k, b)])[:LINES]
            other = (p + k) ^ (nr // 2)
            row_ref[:, block(p + k, b)] = with_largest(flat, p + k)
            swap_ref[:, block(other, b)] = with_largest(flat, other)
    peak_ref[...] = stack_rows((peak_t, peak_s), peak_ref.shape, 0)


def column_kernel(step, tl_ref, sl_ref, peaks, image, col_ref):
    peak_t, peak_s = peaks[0:1, :], peaks[1:2, :]
    sums = None
    for k in range(0, tl_ref.shape[0], step):
        tl, sl = tl_ref[k : k + step, :], sl_ref[k : k + step, :]
        et = jnp.exp2(tl - peak_t)
        parts = [jnp.sum(x, 0, keepdims=True) for x in (et, jnp.exp2(sl - peak_s), et * (tl - sl))]
        sums = parts if sums is None else [x + y for x, y in zip(sums, parts)]
    most = jnp.max(jnp.abs(image[...].astype(F32)), 0, keepdims=True)
    if col_ref.shape[1] > most.shape[1]:
        most = jnp.concatenate([most, jnp.zeros((1, col_ref.shape[1] - most.shape[1]), F32)], 1)
    lines = (peak_t + jnp.log2(sums[0]), peak_s + jnp.log2(sums[1]), sums[2] / sums[0], most)
    col_ref[...] = stack_rows(lines, col_ref.shape, 0)


def join_kernel(teacher, student, both):
    tw = teacher.shape[1]
    both[:, :tw] = teacher[...]
    both[:, tw:] = student[...]


def digits(share, rank, slots, width):
    rows = []
    for unit in DIGITS:
        digit = jnp.floor(share * (1.0 / unit))
        share = share - digit * unit
        rows.append(digit)
    lane = lax.broadcasted_iota(jnp.int32, (EXTRA, width), 1)
    return jnp.where(lane // (width // slots) == rank, stack_rows(rows, (EXTRA, width), 0), 0.0)


def combine(tiles, terms):
    lses = []
    for kind in (1, 0):
        peak = tree(jnp.maximum, [x[kind] for x in tiles])
        weights = [jnp.exp2(x[kind] - peak) for x in tiles]
        total = tree(jnp.add, weights)
        lses.append(peak + jnp.log2(total))
    for k, (w, x) in enumerate(zip(weights, tiles)):
        terms[k : k + 1, :] = w * x[2]
    gap = tree(jnp.add, [terms[k : k + 1, :] for k in range(len(tiles))])
    return lses[1], lses[0], gap / total + (lses[0] - lses[1])


def sum_blocks(x, b):
    parts = [jnp.sum(x[:, block(p, b)], axis=(0, 1), keepdims=True) for p in range(x.shape[1] // b)]
    return tree(jnp.add, parts) * LN2


def powers(largest, pairs, scale):
    bound = functools.reduce(jnp.maximum, largest) * ((1 + pairs) * scale)
    power = jnp.ceil(jnp.log2(jnp.maximum(bound, 1e-30)))
    return jnp.exp2(15.0 - power) * scale, jnp.exp2(power - 15.0)


def split_lines(refs, n):
    views = []
    while len(views) < n:
        views += [refs[0].at[block(k, LINES), :] for k in range(refs[0].shape[0] // LINES)]
        refs = refs[1:]
    return views, refs


def delta_kernel(nr, nc, b, pairs, scale, place, *refs):
    text, tl_ref, sl_ref, refs = *refs[:3], refs[3:]
    row_parts, refs = split_lines(refs, nr // 2)
    col_parts, refs = split_lines(refs, nc)
    other_near, other_far, high_ref, low_ref, refs = *refs[:4], refs[4:]
    image_back_ref, text_back_ref, scale_ref, image_extra, text_extra, row_terms, col_terms = refs
    width = image_back_ref.shape[1]
    lines = [x[2 * KINDS + core : 2 * KINDS + core + 1, :width] for x in row_parts for core in range(2)]
    image_scale, image_back = powers(lines, pairs, scale)
    text_scale, text_back = powers([x[KINDS : KINDS + 1, :width] for x in col_parts], pairs, scale)
    image_back_ref[...] = image_back
    text_back_ref[...] = text_back
    scale_ref[...] = stack_rows((image_scale, text_scale), scale_ref.shape, 0)
    tiles = []
    for q in range(nr // 2):
        x = jnp.concatenate([row_parts[q][:, block(p ^ q, b)] for p in range(nr)], 1)
        for core in range(2):
            tiles.append([x[core * KINDS + k : core * KINDS + k + 1, :] for k in range(KINDS)])
    row_t, row_s, terms = combine(tiles, row_terms)
    row_share = sum_blocks(terms, b)
    rows = stack_rows((row_t, row_s), (LINES, nr * b), 0)
    tiles = []
    for q in range(nc):
        x = jnp.concatenate([col_parts[q][:, block(p ^ q, b)] for p in range(nc)], 1)
        tiles.append([x[k : k + 1, :] for k in range(KINDS)])
    col_t, col_s, terms = combine(tiles, col_terms)
    col_share = sum_blocks(terms, b)
    for p in range(nr):
        row = jnp.transpose(rows[:, block(p, b)])
        tl, sl = tl_ref[block(p, b), :], sl_ref[block(p, b), :]
        delta = (jnp.exp2(sl - row[:, 1:2]) - jnp.exp2(tl - row[:, 0:1])) + (
            jnp.exp2(sl - col_s) - jnp.exp2(tl - col_t)
        )
        high = delta.astype(BF16)
        high_ref[block(p, b), :] = high
        low_ref[block(p, b), :] = (delta - high.astype(F32)).astype(BF16)
    image_extra[...] = digits(col_share * (1.0 / (nc * b)), place[1], nr, width)
    text_extra[...] = digits(row_share * (1.0 / (nr * b)), place[2], nc, width)
    rows = nr * b // 4
    for n, ref in ((3, other_far), (2, other_near)):
        ref[:rows, :] = product(high_ref, low_ref, (block(n, rows), slice(None)), text, 1) * image_scale
        ref[rows:, :] = image_extra[...]


def product(high_ref, low_ref, place, other, dim):
    return matmul(high_ref[place], other[...], dim, 0) + matmul(low_ref[place], other[...], dim, 0)


def gradient_kernel(image, text, high_ref, low_ref, scale_ref, image_extra, text_extra, near, far, keep, send):
    rows, cols = near.shape[0] - EXTRA, keep.shape[0] - EXTRA
    for n, ref in ((1, far), (0, near)):
        ref[:rows, :] = product(high_ref, low_ref, (block(n, rows), slice(None)), text, 1) * scale_ref[0:1, :]
        ref[rows:, :] = image_extra[...]
    for n, ref in ((1, send), (0, keep)):
        ref[:cols, :] = product(high_ref, low_ref, (slice(None), block(n, cols)), image, 0) * scale_ref[1:2, :]
        ref[cols:, :] = text_extra[...]


def call(kernel, outs, args, scratch=(), flops=0, transcendentals=0):
    shapes = [jax.ShapeDtypeStruct(s, d) for s, d in outs]
    size = sum(x.size * x.dtype.itemsize for x in list(args) + shapes)
    held = sum(math.prod(s) * jnp.dtype(d).itemsize for s, d in scratch)
    return pl.pallas_call(
        kernel,
        out_shape=shapes,
        in_specs=[SMEM if x.dtype == jnp.int32 else VMEM for x in args],
        out_specs=[VMEM] * len(shapes),
        scratch_shapes=[pltpu.VMEM(s, d) for s, d in scratch],
        compiler_params=pltpu.CompilerParams(vmem_limit_bytes=size + held + ROOM),
        cost_estimate=pl.CostEstimate(flops=flops, bytes_accessed=size, transcendentals=transcendentals),
    )(*args)


def swap(bits, x):
    perm = [(i, i ^ ((1 << len(bits)) - 1)) for i in range(1 << len(bits))]
    return lax.ppermute(x, bits, perm)


def subset(bits, q):
    return tuple(b for k, b in enumerate(bits) if q >> k & 1)


def together(*groups):
    return lax.optimization_barrier(groups)


def gather(bits, x):
    blocks = [x]
    for k, bit in enumerate(bits):
        own = together(x, blocks[2])[0] if k > 1 else x
        blocks = blocks + [swap((bit,), y) for y in [own] + blocks[1:]]
    return blocks


def exchange(bits, x):
    parts = [x]
    for bit in bits:
        parts.append(swap((bit,), jnp.concatenate(parts) if len(parts) > 1 else x))
    return parts


def add_message(keep, come):
    rows = keep[0].shape[0]
    come = come.astype(F32)
    return keep[0] + come[:rows], keep[1] + come[rows:]


def local(image_bits, text_bits, teacher_image, teacher_text, student_image, student_text):
    b, tw = teacher_image.shape
    sw = student_image.shape[1]
    nr, nc = 1 << len(image_bits), 1 << len(text_bits)
    r, c = nr * b, nc * b
    pair, others = image_bits[-1:], image_bits[:-1]
    (image,) = call(join_kernel, [((b, tw + sw), BF16)], [teacher_image, student_image])
    (text,) = call(join_kernel, [((b, tw + sw), BF16)], [teacher_text, student_text])
    images, texts = gather(image_bits, image), gather(text_bits, text)
    place = jnp.stack([lax.axis_index(x) for x in (pair, image_bits, text_bits)]).astype(jnp.int32)
    tl, sl, rows, rows_swapped, peaks, image, text = call(
        functools.partial(stats_kernel, nr, nc, b, tw, tw**-0.5, sw**-0.5),
        [((r, c), F32), ((r, c), F32), ((LINES, r), F32), ((LINES, r), F32), ((LINES, c), F32), ((r, sw), BF16), ((c, sw), BF16)],
        [place] + images + texts, [((c, tw), BF16)], 2 * r * c * (tw + sw), 4 * r * c,
    )
    other = swap(pair, rows_swapped)
    (cols,) = call(
        functools.partial(column_kernel, 2 * b), [((LINES, c), F32)], [tl, sl, peaks, image], (), 0, 2 * r * c
    )
    row_parts, col_parts = exchange(others, rows + other), exchange(text_bits, cols)
    pairs = b << (len(image_bits) + len(text_bits))
    row, extra = ((1, sw), F32), ((EXTRA, sw), F32)
    near_shape, keep_shape = ((r // 4 + EXTRA, sw), F32), ((c // 2 + EXTRA, sw), F32)
    other_near, other_far, high, low, image_back, text_back, *more = call(
        functools.partial(delta_kernel, nr, nc, b, pairs, sw**-0.5),
        [near_shape, near_shape, ((r, c), BF16), ((r, c), BF16), row, row, ((8, sw), F32), extra, extra],
        [place, text, tl, sl] + row_parts + col_parts,
        [((nr, r), F32), ((max(nc, 8), c), F32)], 2 * r * c * sw, 4 * r * c,
    )
    other_far, other_near = swap(pair, other_far), swap(pair, other_near)
    near, far, text_keep, text_send = call(
        gradient_kernel, [near_shape, near_shape, keep_shape, keep_shape], [image, text, high, low] + more, (), 6 * r * c * sw
    )
    image_send = far + other_far
    image_keep = near + other_near
    image_keep, text_keep = [(x[:-EXTRA], x[-EXTRA:]) for x in (image_keep, text_keep)]
    for k in reversed(range(max(len(text_bits), len(others)))):
        todo = {}
        if k < len(text_bits):
            todo["text"] = text_send.astype(F16)
        if k < len(others):
            todo["image"] = image_send.astype(F16)
        (todo,) = together(todo)
        half = b << k >> 1
        if k < len(text_bits):
            body, extra = text_keep = add_message(text_keep, swap(text_bits[k : k + 1], todo["text"]))
            if k:
                text_keep, text_send = (body[:half], extra), jnp.concatenate([body[half:], extra])
        if k < len(others):
            body, extra = image_keep = add_message(image_keep, swap(others[k : k + 1], todo["image"]))
            if k:
                image_keep, image_send = (body[:half], extra), jnp.concatenate([body[half:], extra])
    units = stack_rows(DIGITS, (EXTRA, sw), 0)
    loss = jnp.sum((image_keep[1] + text_keep[1]) * units) * (0.5 / sw)
    return (loss, image_keep[0] * image_back, text_keep[0] * text_back)


def solution(mesh):
    bits = {axis: [f"{axis}{k}" for k in reversed(range(mesh.shape[axis].bit_length() - 1))] for axis in ("img", "txt")}
    names = bits["img"] + bits["txt"]
    cube = Mesh(np.asarray(mesh.devices).reshape((2,) * len(names)), names)
    image_bits = bits["img"][:-1] + [x for x in bits["txt"] if int(x[3:]) % 2 == 0]
    text_bits = [x for x in names if x not in image_bits]
    image, text = P(tuple(names), None), P(tuple(bits["txt"] + bits["img"]), None)
    return jax.shard_map(
        functools.partial(local, tuple(image_bits), tuple(text_bits)),
        mesh=cube,
        in_specs=(image, text, image, text),
        out_specs=(P(), image, text),
        check_vma=False,
    )
```

```python
import functools
import math

import jax
import jax.numpy as jnp
import numpy as np
from jax import lax
from jax.experimental import pallas as pl
from jax.experimental.pallas import tpu as pltpu
from jax.sharding import Mesh, PartitionSpec as P

F32 = jnp.float32
BF16 = jnp.bfloat16
F16 = jnp.float16
LOG2E = 1.4426950408889634
LN2 = 0.6931471805599453
LINES = 8
KINDS = 3
EXTRA = 16
DIGITS = (64.0, 2.0**-4, 2.0**-14, 2.0**-24, 2.0**-34)
ROOM = 12 * 2**20
VMEM = pl.BlockSpec(memory_space=pltpu.VMEM)
SMEM = pl.BlockSpec(memory_space=pltpu.SMEM)


def matmul(a, b, da, db):
    return lax.dot_general(a, b, (((da,), (db,)), ((), ())), preferred_element_type=F32)


def block(k, b):
    return slice(k * b, (k + 1) * b)


def stack_rows(values, shape, axis, first=0):
    index = lax.broadcasted_iota(jnp.int32, shape, axis) - first
    out = jnp.zeros(shape, F32)
    for k, value in enumerate(values):
        out = jnp.where(index == k, value, out)
    return out


def tree(op, items):
    while len(items) > 1:
        items = [op(x, y) for x, y in zip(items[::2], items[1::2])]
    return items[0]


def stats_kernel(image_forms, text_forms, b, tw, scale_t, scale_s, core, *refs):
    nr, nc = len(image_forms), len(text_forms)
    images, texts = [], []
    for forms, blocks in ((image_forms, images), (text_forms, texts)):
        for form in forms:
            blocks.append(refs[:form])
            refs = refs[form:]
    tl_ref, sl_ref, row_ref, swap_ref, peak_ref, image_s, text_s, text_t = refs
    for p in range(nc):
        for k, x in enumerate(texts[p]):
            rows = slice(p * b + k * x.shape[0], p * b + (k + 1) * x.shape[0])
            text_t[rows, :] = x[:, :tw]
            text_s[rows, :] = x[:, tw:]
    for p in range(nr):
        for k, x in enumerate(images[p]):
            image_s[p * b + k * x.shape[0] : p * b + (k + 1) * x.shape[0], :] = x[:, tw:]
    largest = jnp.max(jnp.abs(text_s[...].astype(F32)), 0, keepdims=True)
    width = largest.shape[1]

    def with_largest(flat, k):
        if (k + 1) * b > width:
            return flat
        return flat + stack_rows((largest[:, block(k, b)],), flat.shape, 0, 2 * KINDS + core[0])

    step = 2 if nr % 2 == 0 else 1
    count = step * b
    peak_t = peak_s = None
    for p in range(0, nr, step):
        rows = slice(p * b, p * b + count)
        tl = matmul(jnp.concatenate([x[:, :tw] for pieces in images[p : p + step] for x in pieces], 0), text_t[...], 1, 1) * (scale_t * LOG2E)
        sl = matmul(image_s[rows, :], text_s[...], 1, 1) * (scale_s * LOG2E)
        tl_ref[rows, :] = tl
        sl_ref[rows, :] = sl
        top_t, top_s = jnp.max(tl, 0, keepdims=True), jnp.max(sl, 0, keepdims=True)
        peak_t = top_t if peak_t is None else jnp.maximum(peak_t, top_t)
        peak_s = top_s if peak_s is None else jnp.maximum(peak_s, top_s)
        mt, ms = jnp.max(tl, 1, keepdims=True), jnp.max(sl, 1, keepdims=True)
        et = jnp.exp2(tl - mt)
        sum_t = jnp.sum(et, 1, keepdims=True)
        gap = jnp.sum(et * (tl - sl), 1, keepdims=True)
        sum_s = jnp.sum(jnp.exp2(sl - ms), 1, keepdims=True)
        lines = (mt + jnp.log2(sum_t), ms + jnp.log2(sum_s), gap / sum_t)
        lines = stack_rows(lines, (count, 128), 1, core[0] * KINDS)
        for k in range(step):
            flat = jnp.transpose(lines[block(k, b)])[:LINES]
            other = (p + k) ^ (nr // 2)
            row_ref[:, block(p + k, b)] = with_largest(flat, p + k)
            swap_ref[:, block(other, b)] = with_largest(flat, other)
    peak_ref[...] = stack_rows((peak_t, peak_s), peak_ref.shape, 0)


def column_kernel(step, tl_ref, sl_ref, peaks, image, col_ref):
    peak_t, peak_s = peaks[0:1, :], peaks[1:2, :]
    sums = None
    for k in range(0, tl_ref.shape[0], step):
        tl, sl = tl_ref[k : k + step, :], sl_ref[k : k + step, :]
        et = jnp.exp2(tl - peak_t)
        parts = [jnp.sum(x, 0, keepdims=True) for x in (et, jnp.exp2(sl - peak_s), et * (tl - sl))]
        sums = parts if sums is None else [x + y for x, y in zip(sums, parts)]
    most = jnp.max(jnp.abs(image[...].astype(F32)), 0, keepdims=True)
    if col_ref.shape[1] > most.shape[1]:
        most = jnp.concatenate([most, jnp.zeros((1, col_ref.shape[1] - most.shape[1]), F32)], 1)
    lines = (peak_t + jnp.log2(sums[0]), peak_s + jnp.log2(sums[1]), sums[2] / sums[0], most)
    col_ref[...] = stack_rows(lines, col_ref.shape, 0)


def join_kernel(teacher, student, both):
    tw = teacher.shape[1]
    both[:, :tw] = teacher[...]
    both[:, tw:] = student[...]


def digits(share, rank, slots, width):
    rows = []
    for unit in DIGITS:
        digit = jnp.floor(share * (1.0 / unit))
        share = share - digit * unit
        rows.append(digit)
    lane = lax.broadcasted_iota(jnp.int32, (EXTRA, width), 1)
    return jnp.where(lane // (width // slots) == rank, stack_rows(rows, (EXTRA, width), 0), 0.0)


def combine(tiles, terms):
    lses = []
    for kind in (1, 0):
        peak = tree(jnp.maximum, [x[kind] for x in tiles])
        weights = [jnp.exp2(x[kind] - peak) for x in tiles]
        total = tree(jnp.add, weights)
        lses.append(peak + jnp.log2(total))
    for k, (w, x) in enumerate(zip(weights, tiles)):
        terms[k : k + 1, :] = w * x[2]
    gap = tree(jnp.add, [terms[k : k + 1, :] for k in range(len(tiles))])
    return lses[1], lses[0], gap / total + (lses[0] - lses[1])


def sum_blocks(x, b):
    parts = [jnp.sum(x[:, block(p, b)], axis=(0, 1), keepdims=True) for p in range(x.shape[1] // b)]
    return tree(jnp.add, parts) * LN2


def powers(largest, pairs, scale):
    bound = functools.reduce(jnp.maximum, largest) * ((1 + pairs) * scale)
    power = jnp.ceil(jnp.log2(jnp.maximum(bound, 1e-30)))
    return jnp.exp2(15.0 - power) * scale, jnp.exp2(power - 15.0)


def split_lines(refs, n):
    views = []
    while len(views) < n:
        views += [refs[0].at[block(k, LINES), :] for k in range(refs[0].shape[0] // LINES)]
        refs = refs[1:]
    return views, refs


def delta_kernel(nr, nc, b, pairs, scale, place, *refs):
    text, tl_ref, sl_ref, refs = *refs[:3], refs[3:]
    row_parts, refs = split_lines(refs, nr // 2)
    col_parts, refs = split_lines(refs, nc)
    other_near, other_far, high_ref, low_ref, refs = *refs[:4], refs[4:]
    image_back_ref, text_back_ref, scale_ref, image_extra, text_extra, row_terms, col_terms = refs
    width = image_back_ref.shape[1]
    lines = [x[2 * KINDS + core : 2 * KINDS + core + 1, :width] for x in row_parts for core in range(2)]
    image_scale, image_back = powers(lines, pairs, scale)
    text_scale, text_back = powers([x[KINDS : KINDS + 1, :width] for x in col_parts], pairs, scale)
    image_back_ref[...] = image_back
    text_back_ref[...] = text_back
    scale_ref[...] = stack_rows((image_scale, text_scale), scale_ref.shape, 0)
    tiles = []
    for q in range(nr // 2):
        x = jnp.concatenate([row_parts[q][:, block(p ^ q, b)] for p in range(nr)], 1)
        for core in range(2):
            tiles.append([x[core * KINDS + k : core * KINDS + k + 1, :] for k in range(KINDS)])
    row_t, row_s, terms = combine(tiles, row_terms)
    row_share = sum_blocks(terms, b)
    rows = stack_rows((row_t, row_s), (LINES, nr * b), 0)
    tiles = []
    for q in range(nc):
        x = jnp.concatenate([col_parts[q][:, block(p ^ q, b)] for p in range(nc)], 1)
        tiles.append([x[k : k + 1, :] for k in range(KINDS)])
    col_t, col_s, terms = combine(tiles, col_terms)
    col_share = sum_blocks(terms, b)
    for p in range(nr):
        row = jnp.transpose(rows[:, block(p, b)])
        tl, sl = tl_ref[block(p, b), :], sl_ref[block(p, b), :]
        delta = (jnp.exp2(sl - row[:, 1:2]) - jnp.exp2(tl - row[:, 0:1])) + (
            jnp.exp2(sl - col_s) - jnp.exp2(tl - col_t)
        )
        high = delta.astype(BF16)
        high_ref[block(p, b), :] = high
        low_ref[block(p, b), :] = (delta - high.astype(F32)).astype(BF16)
    image_extra[...] = digits(col_share * (1.0 / (nc * b)), place[1], nr, width)
    text_extra[...] = digits(row_share * (1.0 / (nr * b)), place[2], nc, width)
    rows = nr * b // 4
    for n, ref in ((3, other_far), (2, other_near)):
        ref[:rows, :] = product(high_ref, low_ref, (block(n, rows), slice(None)), text, 1) * image_scale
        ref[rows:, :] = image_extra[...]


def product(high_ref, low_ref, place, other, dim):
    return matmul(high_ref[place], other[...], dim, 0) + matmul(low_ref[place], other[...], dim, 0)


def gradient_kernel(image, text, high_ref, low_ref, scale_ref, image_extra, text_extra, near, far, keep, send):
    rows, cols = near.shape[0] - EXTRA, keep.shape[0] - EXTRA
    for n, ref in ((1, far), (0, near)):
        ref[:rows, :] = product(high_ref, low_ref, (block(n, rows), slice(None)), text, 1) * scale_ref[0:1, :]
        ref[rows:, :] = image_extra[...]
    for n, ref in ((1, send), (0, keep)):
        ref[:cols, :] = product(high_ref, low_ref, (slice(None), block(n, cols)), image, 0) * scale_ref[1:2, :]
        ref[cols:, :] = text_extra[...]


def call(kernel, outs, args, scratch=(), flops=0, transcendentals=0):
    shapes = [jax.ShapeDtypeStruct(s, d) for s, d in outs]
    size = sum(x.size * x.dtype.itemsize for x in list(args) + shapes)
    held = sum(math.prod(s) * jnp.dtype(d).itemsize for s, d in scratch)
    return pl.pallas_call(
        kernel,
        out_shape=shapes,
        in_specs=[SMEM if x.dtype == jnp.int32 else VMEM for x in args],
        out_specs=[VMEM] * len(shapes),
        scratch_shapes=[pltpu.VMEM(s, d) for s, d in scratch],
        compiler_params=pltpu.CompilerParams(vmem_limit_bytes=size + held + ROOM),
        cost_estimate=pl.CostEstimate(flops=flops, bytes_accessed=size, transcendentals=transcendentals),
    )(*args)


def swap(bits, x):
    perm = [(i, i ^ ((1 << len(bits)) - 1)) for i in range(1 << len(bits))]
    return lax.ppermute(x, bits, perm)


def subset(bits, q):
    return tuple(b for k, b in enumerate(bits) if q >> k & 1)


def together(*groups):
    return lax.optimization_barrier(groups)


def gather(image_bits, text_bits, image, text):
    groups = [(image_bits, image), (text_bits, text)]
    own = [[swap(bits[k : k + 1], x) for k in range(1, len(bits))] for bits, x in groups]
    half = image.shape[0] // 2
    first = [swap(bits[:1], x[:half]) for bits, x in groups]
    second = [swap(bits[:1], together(x[half:], own[0][-1])[0]) for bits, x in groups]
    result = []
    for n, (bits, x) in enumerate(groups):
        blocks = [[x], [first[n], second[n]]]
        for k in range(1, len(bits)):
            ways = [[swap(bits[k : k + 1], together(y, own[n][k - 1])[0]) for y in pieces] for pieces in blocks[1:]]
            blocks = blocks + [[own[n][k - 1]]] + ways
        result.append(blocks)
    return result


def exchange(bits, x):
    parts = [x]
    for bit in bits:
        parts.append(swap((bit,), jnp.concatenate(parts) if len(parts) > 1 else x))
    return parts


def add_message(keep, come):
    rows = keep[0].shape[0]
    come = come.astype(F32)
    return keep[0] + come[:rows], keep[1] + come[rows:]


def local(image_bits, text_bits, teacher_image, teacher_text, student_image, student_text):
    b, tw = teacher_image.shape
    sw = student_image.shape[1]
    nr, nc = 1 << len(image_bits), 1 << len(text_bits)
    r, c = nr * b, nc * b
    pair, others = image_bits[-1:], image_bits[:-1]
    (image,) = call(join_kernel, [((b, tw + sw), BF16)], [teacher_image, student_image])
    (text,) = call(join_kernel, [((b, tw + sw), BF16)], [teacher_text, student_text])
    images, texts = gather(image_bits, text_bits, image, text)
    forms = [[len(x) for x in blocks] for blocks in (images, texts)]
    place = jnp.stack([lax.axis_index(x) for x in (pair, image_bits, text_bits)]).astype(jnp.int32)
    tl, sl, rows, rows_swapped, peaks, image, text = call(
        functools.partial(stats_kernel, *forms, b, tw, tw**-0.5, sw**-0.5),
        [((r, c), F32), ((r, c), F32), ((LINES, r), F32), ((LINES, r), F32), ((LINES, c), F32), ((r, sw), BF16), ((c, sw), BF16)],
        [place] + [x for pieces in images + texts for x in pieces], [((c, tw), BF16)], 2 * r * c * (tw + sw), 4 * r * c,
    )
    other = swap(pair, rows_swapped)
    (cols,) = call(
        functools.partial(column_kernel, 2 * b), [((LINES, c), F32)], [tl, sl, peaks, image], (), 0, 2 * r * c
    )
    row_parts, col_parts = exchange(others, together(rows, cols)[0] + other), exchange(text_bits, cols)
    pairs = b << (len(image_bits) + len(text_bits))
    row, extra = ((1, sw), F32), ((EXTRA, sw), F32)
    near_shape, keep_shape = ((r // 4 + EXTRA, sw), F32), ((c // 2 + EXTRA, sw), F32)
    other_near, other_far, high, low, image_back, text_back, *more = call(
        functools.partial(delta_kernel, nr, nc, b, pairs, sw**-0.5),
        [near_shape, near_shape, ((r, c), BF16), ((r, c), BF16), row, row, ((8, sw), F32), extra, extra],
        [place, text, tl, sl] + row_parts + col_parts,
        [((nr, r), F32), ((max(nc, 8), c), F32)], 2 * r * c * sw, 4 * r * c,
    )
    other_far, other_near = swap(pair, other_far), swap(pair, other_near)
    near, far, text_keep, text_send = call(
        gradient_kernel, [near_shape, near_shape, keep_shape, keep_shape], [image, text, high, low] + more, (), 6 * r * c * sw
    )
    image_send = far + other_far
    image_keep = near + other_near
    image_keep, text_keep = [(x[:-EXTRA], x[-EXTRA:]) for x in (image_keep, text_keep)]
    for k in reversed(range(max(len(text_bits), len(others)))):
        todo = {}
        if k < len(text_bits):
            todo["text"] = text_send.astype(F16)
        if k < len(others):
            todo["image"] = image_send.astype(F16)
        (todo,) = together(todo)
        half = b << k >> 1
        if k < len(text_bits):
            body, extra = text_keep = add_message(text_keep, swap(text_bits[k : k + 1], todo["text"]))
            if k:
                text_keep, text_send = (body[:half], extra), jnp.concatenate([body[half:], extra])
        if k < len(others):
            body, extra = image_keep = add_message(image_keep, swap(others[k : k + 1], todo["image"]))
            if k:
                image_keep, image_send = (body[:half], extra), jnp.concatenate([body[half:], extra])
    units = stack_rows(DIGITS, (EXTRA, sw), 0)
    loss = jnp.sum((image_keep[1] + text_keep[1]) * units) * (0.5 / sw)
    return (loss, image_keep[0] * image_back, text_keep[0] * text_back)


def solution(mesh):
    bits = {axis: [f"{axis}{k}" for k in reversed(range(mesh.shape[axis].bit_length() - 1))] for axis in ("img", "txt")}
    names = bits["img"] + bits["txt"]
    cube = Mesh(np.asarray(mesh.devices).reshape((2,) * len(names)), names)
    image_bits = bits["img"][:-1] + [x for x in bits["txt"] if int(x[3:]) % 2 == 0]
    text_bits = [x for x in names if x not in image_bits]
    image, text = P(tuple(names), None), P(tuple(bits["txt"] + bits["img"]), None)
    return jax.shard_map(
        functools.partial(local, tuple(image_bits), tuple(text_bits)),
        mesh=cube,
        in_specs=(image, text, image, text),
        out_specs=(P(), image, text),
        check_vma=False,
    )
```

```python
import functools
import math

import jax
import jax.numpy as jnp
import numpy as np
from jax import lax
from jax.experimental import pallas as pl
from jax.experimental.pallas import tpu as pltpu
from jax.sharding import Mesh, PartitionSpec as P

F32 = jnp.float32
BF16 = jnp.bfloat16
F16 = jnp.float16
LOG2E = 1.4426950408889634
LN2 = 0.6931471805599453
LINES = 8
KINDS = 3
EXTRA = 16
DIGITS = (64.0, 2.0**-4, 2.0**-14, 2.0**-24, 2.0**-34)
ROOM = 12 * 2**20
VMEM = pl.BlockSpec(memory_space=pltpu.VMEM)
SMEM = pl.BlockSpec(memory_space=pltpu.SMEM)


def matmul(a, b, da, db):
    return lax.dot_general(a, b, (((da,), (db,)), ((), ())), preferred_element_type=F32)


def block(k, b):
    return slice(k * b, (k + 1) * b)


def stack_rows(values, shape, axis, first=0):
    index = lax.broadcasted_iota(jnp.int32, shape, axis) - first
    out = jnp.zeros(shape, F32)
    for k, value in enumerate(values):
        out = jnp.where(index == k, value, out)
    return out


def tree(op, items):
    while len(items) > 1:
        items = [op(x, y) for x, y in zip(items[::2], items[1::2])]
    return items[0]


def views(refs, forms, tw):
    teachers, students = [], []
    for form in forms:
        teachers.append(refs[0].at[:, :tw] if form == 1 else refs[0])
        students.append(refs[0].at[:, tw:] if form == 1 else refs[1])
        refs = refs[form:]
    return teachers, students, refs


def stats_kernel(image_forms, text_forms, b, tw, scale_t, scale_s, core, *refs):
    nr, nc = len(image_forms), len(text_forms)
    ti, si, refs = views(refs, image_forms, tw)
    tt, st, refs = views(refs, text_forms, tw)
    tl_ref, sl_ref, row_ref, swap_ref, peak_ref, image_s, text_s, text_t = refs
    for p in range(nc):
        text_t[block(p, b), :] = tt[p][...]
        text_s[block(p, b), :] = st[p][...]
    for p in range(nr):
        image_s[block(p, b), :] = si[p][...]
    largest = jnp.max(jnp.abs(text_s[...].astype(F32)), 0, keepdims=True)
    width = largest.shape[1]

    def with_largest(flat, k):
        if (k + 1) * b > width:
            return flat
        return flat + stack_rows((largest[:, block(k, b)],), flat.shape, 0, 2 * KINDS + core[0])

    step = 2 if nr % 2 == 0 else 1
    count = step * b
    peak_t = peak_s = None
    for p in range(0, nr, step):
        rows = slice(p * b, p * b + count)
        tl = matmul(jnp.concatenate([x[...] for x in ti[p : p + step]], 0), text_t[...], 1, 1) * (scale_t * LOG2E)
        sl = matmul(image_s[rows, :], text_s[...], 1, 1) * (scale_s * LOG2E)
        tl_ref[rows, :] = tl
        sl_ref[rows, :] = sl
        top_t, top_s = jnp.max(tl, 0, keepdims=True), jnp.max(sl, 0, keepdims=True)
        peak_t = top_t if peak_t is None else jnp.maximum(peak_t, top_t)
        peak_s = top_s if peak_s is None else jnp.maximum(peak_s, top_s)
        mt, ms = jnp.max(tl, 1, keepdims=True), jnp.max(sl, 1, keepdims=True)
        et = jnp.exp2(tl - mt)
        sum_t = jnp.sum(et, 1, keepdims=True)
        gap = jnp.sum(et * (tl - sl), 1, keepdims=True)
        sum_s = jnp.sum(jnp.exp2(sl - ms), 1, keepdims=True)
        lines = (mt + jnp.log2(sum_t), ms + jnp.log2(sum_s), gap / sum_t)
        lines = stack_rows(lines, (count, 128), 1, core[0] * KINDS)
        for k in range(step):
            flat = jnp.transpose(lines[block(k, b)])[:LINES]
            other = (p + k) ^ (nr // 2)
            row_ref[:, block(p + k, b)] = with_largest(flat, p + k)
            swap_ref[:, block(other, b)] = with_largest(flat, other)
    peak_ref[...] = stack_rows((peak_t, peak_s), peak_ref.shape, 0)


def column_kernel(step, tl_ref, sl_ref, peaks, image, col_ref):
    peak_t, peak_s = peaks[0:1, :], peaks[1:2, :]
    sums = None
    for k in range(0, tl_ref.shape[0], step):
        tl, sl = tl_ref[k : k + step, :], sl_ref[k : k + step, :]
        et = jnp.exp2(tl - peak_t)
        parts = [jnp.sum(x, 0, keepdims=True) for x in (et, jnp.exp2(sl - peak_s), et * (tl - sl))]
        sums = parts if sums is None else [x + y for x, y in zip(sums, parts)]
    most = jnp.max(jnp.abs(image[...].astype(F32)), 0, keepdims=True)
    if col_ref.shape[1] > most.shape[1]:
        most = jnp.concatenate([most, jnp.zeros((1, col_ref.shape[1] - most.shape[1]), F32)], 1)
    lines = (peak_t + jnp.log2(sums[0]), peak_s + jnp.log2(sums[1]), sums[2] / sums[0], most)
    col_ref[...] = stack_rows(lines, col_ref.shape, 0)


def join_kernel(teacher, student, both):
    tw = teacher.shape[1]
    both[:, :tw] = teacher[...]
    both[:, tw:] = student[...]


def digits(share, rank, slots, width):
    rows = []
    for unit in DIGITS:
        digit = jnp.floor(share * (1.0 / unit))
        share = share - digit * unit
        rows.append(digit)
    lane = lax.broadcasted_iota(jnp.int32, (EXTRA, width), 1)
    return jnp.where(lane // (width // slots) == rank, stack_rows(rows, (EXTRA, width), 0), 0.0)


def combine(tiles, terms):
    lses = []
    for kind in (1, 0):
        peak = tree(jnp.maximum, [x[kind] for x in tiles])
        weights = [jnp.exp2(x[kind] - peak) for x in tiles]
        total = tree(jnp.add, weights)
        lses.append(peak + jnp.log2(total))
    for k, (w, x) in enumerate(zip(weights, tiles)):
        terms[k : k + 1, :] = w * x[2]
    gap = tree(jnp.add, [terms[k : k + 1, :] for k in range(len(tiles))])
    return lses[1], lses[0], gap / total + (lses[0] - lses[1])


def sum_blocks(x, b):
    parts = [jnp.sum(x[:, block(p, b)], axis=(0, 1), keepdims=True) for p in range(x.shape[1] // b)]
    return tree(jnp.add, parts) * LN2


def powers(largest, pairs, scale):
    bound = functools.reduce(jnp.maximum, largest) * ((1 + pairs) * scale)
    power = jnp.ceil(jnp.log2(jnp.maximum(bound, 1e-30)))
    return jnp.exp2(15.0 - power) * scale, jnp.exp2(power - 15.0)


def split_lines(refs, n):
    views = []
    while len(views) < n:
        views += [refs[0].at[block(k, LINES), :] for k in range(refs[0].shape[0] // LINES)]
        refs = refs[1:]
    return views, refs


def delta_kernel(nr, nc, b, pairs, scale, place, *refs):
    text, tl_ref, sl_ref, refs = *refs[:3], refs[3:]
    row_parts, refs = split_lines(refs, nr // 2)
    col_parts, refs = split_lines(refs, nc)
    other_near, other_far, high_ref, low_ref, refs = *refs[:4], refs[4:]
    image_back_ref, text_back_ref, scale_ref, image_extra, text_extra, row_terms, col_terms = refs
    width = image_back_ref.shape[1]
    lines = [x[2 * KINDS + core : 2 * KINDS + core + 1, :width] for x in row_parts for core in range(2)]
    image_scale, image_back = powers(lines, pairs, scale)
    text_scale, text_back = powers([x[KINDS : KINDS + 1, :width] for x in col_parts], pairs, scale)
    image_back_ref[...] = image_back
    text_back_ref[...] = text_back
    scale_ref[...] = stack_rows((image_scale, text_scale), scale_ref.shape, 0)
    tiles = []
    for q in range(nr // 2):
        x = jnp.concatenate([row_parts[q][:, block(p ^ q, b)] for p in range(nr)], 1)
        for core in range(2):
            tiles.append([x[core * KINDS + k : core * KINDS + k + 1, :] for k in range(KINDS)])
    row_t, row_s, terms = combine(tiles, row_terms)
    row_share = sum_blocks(terms, b)
    rows = stack_rows((row_t, row_s), (LINES, nr * b), 0)
    tiles = []
    for q in range(nc):
        x = jnp.concatenate([col_parts[q][:, block(p ^ q, b)] for p in range(nc)], 1)
        tiles.append([x[k : k + 1, :] for k in range(KINDS)])
    col_t, col_s, terms = combine(tiles, col_terms)
    col_share = sum_blocks(terms, b)
    for p in range(nr):
        row = jnp.transpose(rows[:, block(p, b)])
        tl, sl = tl_ref[block(p, b), :], sl_ref[block(p, b), :]
        delta = (jnp.exp2(sl - row[:, 1:2]) - jnp.exp2(tl - row[:, 0:1])) + (
            jnp.exp2(sl - col_s) - jnp.exp2(tl - col_t)
        )
        high = delta.astype(BF16)
        high_ref[block(p, b), :] = high
        low_ref[block(p, b), :] = (delta - high.astype(F32)).astype(BF16)
    image_extra[...] = digits(col_share * (1.0 / (nc * b)), place[1], nr, width)
    text_extra[...] = digits(row_share * (1.0 / (nr * b)), place[2], nc, width)
    rows = nr * b // 4
    for n, ref in ((3, other_far), (2, other_near)):
        ref[:rows, :] = product(high_ref, low_ref, (block(n, rows), slice(None)), text, 1) * image_scale
        ref[rows:, :] = image_extra[...]


def product(high_ref, low_ref, place, other, dim):
    return matmul(high_ref[place], other[...], dim, 0) + matmul(low_ref[place], other[...], dim, 0)


def gradient_kernel(image, text, high_ref, low_ref, scale_ref, image_extra, text_extra, near, far, keep, send):
    rows, cols = near.shape[0] - EXTRA, keep.shape[0] - EXTRA
    for n, ref in ((1, far), (0, near)):
        ref[:rows, :] = product(high_ref, low_ref, (block(n, rows), slice(None)), text, 1) * scale_ref[0:1, :]
        ref[rows:, :] = image_extra[...]
    for n, ref in ((1, send), (0, keep)):
        ref[:cols, :] = product(high_ref, low_ref, (slice(None), block(n, cols)), image, 0) * scale_ref[1:2, :]
        ref[cols:, :] = text_extra[...]


def call(kernel, outs, args, scratch=(), flops=0, transcendentals=0):
    shapes = [jax.ShapeDtypeStruct(s, d) for s, d in outs]
    size = sum(x.size * x.dtype.itemsize for x in list(args) + shapes)
    held = sum(math.prod(s) * jnp.dtype(d).itemsize for s, d in scratch)
    return pl.pallas_call(
        kernel,
        out_shape=shapes,
        in_specs=[SMEM if x.dtype == jnp.int32 else VMEM for x in args],
        out_specs=[VMEM] * len(shapes),
        scratch_shapes=[pltpu.VMEM(s, d) for s, d in scratch],
        compiler_params=pltpu.CompilerParams(vmem_limit_bytes=size + held + ROOM),
        cost_estimate=pl.CostEstimate(flops=flops, bytes_accessed=size, transcendentals=transcendentals),
    )(*args)


def swap(bits, x):
    perm = [(i, i ^ ((1 << len(bits)) - 1)) for i in range(1 << len(bits))]
    return lax.ppermute(x, bits, perm)


def subset(bits, q):
    return tuple(b for k, b in enumerate(bits) if q >> k & 1)


def together(*groups):
    return lax.optimization_barrier(groups)


def gather(bits, both, apart=None, gates=(None, None)):
    blocks = [(both,)]
    for k, bit in enumerate(bits):
        own = apart if k == 0 and apart else (both,)
        if k > 1:
            own = together(own, blocks[2])[0]
        if k == 1 and gates[0] is not None:
            own = together(own, gates[0])[0]
        ways = blocks[1:]
        if k and gates[1] is not None:
            ways = together(ways, gates[1])[0]
        blocks = blocks + [tuple(swap((bit,), y) for y in parts) for parts in [own] + list(ways)]
    return blocks


def exchange(bits, x):
    parts = [x]
    for bit in bits:
        parts.append(swap((bit,), jnp.concatenate(parts) if len(parts) > 1 else x))
    return parts


def add_message(keep, come):
    rows = keep[0].shape[0]
    come = come.astype(F32)
    return keep[0] + come[:rows], keep[1] + come[rows:]


def local(image_bits, text_bits, teacher_image, teacher_text, student_image, student_text):
    b, tw = teacher_image.shape
    sw = student_image.shape[1]
    nr, nc = 1 << len(image_bits), 1 << len(text_bits)
    r, c = nr * b, nc * b
    pair, others = image_bits[-1:], image_bits[:-1]
    (image,) = call(join_kernel, [((b, tw + sw), BF16)], [teacher_image, student_image])
    (text,) = call(join_kernel, [((b, tw + sw), BF16)], [teacher_text, student_text])
    texts = gather(text_bits, text)
    images = gather(image_bits, image, None, (text, texts[1:3]))
    forms = [[len(x) for x in blocks] for blocks in (images, texts)]
    place = jnp.stack([lax.axis_index(x) for x in (pair, image_bits, text_bits)]).astype(jnp.int32)
    tl, sl, rows, rows_swapped, peaks, image, text = call(
        functools.partial(stats_kernel, *forms, b, tw, tw**-0.5, sw**-0.5),
        [((r, c), F32), ((r, c), F32), ((LINES, r), F32), ((LINES, r), F32), ((LINES, c), F32), ((r, sw), BF16), ((c, sw), BF16)],
        [place] + [x for parts in images + texts for x in parts], [((c, tw), BF16)], 2 * r * c * (tw + sw), 4 * r * c,
    )
    other = swap(pair, rows_swapped)
    (cols,) = call(
        functools.partial(column_kernel, 2 * b), [((LINES, c), F32)], [tl, sl, peaks, image], (), 0, 2 * r * c
    )
    row_parts, col_parts = exchange(others, rows + other), exchange(text_bits, cols)
    pairs = b << (len(image_bits) + len(text_bits))
    row, extra = ((1, sw), F32), ((EXTRA, sw), F32)
    near_shape, keep_shape = ((r // 4 + EXTRA, sw), F32), ((c // 2 + EXTRA, sw), F32)
    other_near, other_far, high, low, image_back, text_back, *more = call(
        functools.partial(delta_kernel, nr, nc, b, pairs, sw**-0.5),
        [near_shape, near_shape, ((r, c), BF16), ((r, c), BF16), row, row, ((8, sw), F32), extra, extra],
        [place, text, tl, sl] + row_parts + col_parts,
        [((nr, r), F32), ((max(nc, 8), c), F32)], 2 * r * c * sw, 4 * r * c,
    )
    other_far, other_near = swap(pair, other_far), swap(pair, other_near)
    near, far, text_keep, text_send = call(
        gradient_kernel, [near_shape, near_shape, keep_shape, keep_shape], [image, text, high, low] + more, (), 6 * r * c * sw
    )
    image_send = far + other_far
    image_keep = near + other_near
    image_keep, text_keep = [(x[:-EXTRA], x[-EXTRA:]) for x in (image_keep, text_keep)]
    for k in reversed(range(max(len(text_bits), len(others)))):
        todo = {}
        if k < len(text_bits):
            todo["text"] = text_send.astype(F16)
        if k < len(others):
            todo["image"] = image_send.astype(F16)
        (todo,) = together(todo)
        half = b << k >> 1
        if k < len(text_bits):
            body, extra = text_keep = add_message(text_keep, swap(text_bits[k : k + 1], todo["text"]))
            if k:
                text_keep, text_send = (body[:half], extra), jnp.concatenate([body[half:], extra])
        if k < len(others):
            body, extra = image_keep = add_message(image_keep, swap(others[k : k + 1], todo["image"]))
            if k:
                image_keep, image_send = (body[:half], extra), jnp.concatenate([body[half:], extra])
    units = stack_rows(DIGITS, (EXTRA, sw), 0)
    loss = jnp.sum((image_keep[1] + text_keep[1]) * units) * (0.5 / sw)
    return (loss, image_keep[0] * image_back, text_keep[0] * text_back)


def solution(mesh):
    bits = {axis: [f"{axis}{k}" for k in reversed(range(mesh.shape[axis].bit_length() - 1))] for axis in ("img", "txt")}
    names = bits["img"] + bits["txt"]
    cube = Mesh(np.asarray(mesh.devices).reshape((2,) * len(names)), names)
    image_bits = bits["img"][:-1] + [x for x in bits["txt"] if int(x[3:]) % 2 == 0]
    text_bits = [x for x in names if x not in image_bits]
    image, text = P(tuple(names), None), P(tuple(bits["txt"] + bits["img"]), None)
    return jax.shard_map(
        functools.partial(local, tuple(image_bits), tuple(text_bits)),
        mesh=cube,
        in_specs=(image, text, image, text),
        out_specs=(P(), image, text),
        check_vma=False,
    )
```

```python
import functools
import math

import jax
import jax.numpy as jnp
import numpy as np
from jax import lax
from jax.experimental import pallas as pl
from jax.experimental.pallas import tpu as pltpu
from jax.sharding import Mesh, PartitionSpec as P

F32 = jnp.float32
BF16 = jnp.bfloat16
F16 = jnp.float16
LOG2E = 1.4426950408889634
LN2 = 0.6931471805599453
LINES = 8
KINDS = 3
EXTRA = 16
DIGITS = (64.0, 2.0**-4, 2.0**-14, 2.0**-24, 2.0**-34)
ROOM = 12 * 2**20
VMEM = pl.BlockSpec(memory_space=pltpu.VMEM)
SMEM = pl.BlockSpec(memory_space=pltpu.SMEM)


def matmul(a, b, da, db):
    return lax.dot_general(a, b, (((da,), (db,)), ((), ())), preferred_element_type=F32)


def block(k, b):
    return slice(k * b, (k + 1) * b)


def stack_rows(values, shape, axis, first=0):
    index = lax.broadcasted_iota(jnp.int32, shape, axis) - first
    out = jnp.zeros(shape, F32)
    for k, value in enumerate(values):
        out = jnp.where(index == k, value, out)
    return out


def tree(op, items):
    while len(items) > 1:
        items = [op(x, y) for x, y in zip(items[::2], items[1::2])]
    return items[0]


def views(refs, forms, tw):
    teachers, students = [], []
    for form in forms:
        teachers.append(refs[0].at[:, :tw] if form == 1 else refs[0])
        students.append(refs[0].at[:, tw:] if form == 1 else refs[1])
        refs = refs[form:]
    return teachers, students, refs


def stats_kernel(image_forms, text_forms, b, tw, scale_t, scale_s, core, *refs):
    nr, nc = len(image_forms), len(text_forms)
    ti, si, refs = views(refs, image_forms, tw)
    tt, st, refs = views(refs, text_forms, tw)
    tl_ref, sl_ref, row_ref, swap_ref, peak_ref, image_s, text_s, text_t = refs
    for p in range(nc):
        text_t[block(p, b), :] = tt[p][...]
        text_s[block(p, b), :] = st[p][...]
    for p in range(nr):
        image_s[block(p, b), :] = si[p][...]
    largest = jnp.max(jnp.abs(text_s[...].astype(F32)), 0, keepdims=True)
    width = largest.shape[1]

    def with_largest(flat, k):
        if (k + 1) * b > width:
            return flat
        return flat + stack_rows((largest[:, block(k, b)],), flat.shape, 0, 2 * KINDS + core[0])

    step = 2 if nr % 2 == 0 else 1
    count = step * b
    peak_t = peak_s = None
    for p in range(0, nr, step):
        rows = slice(p * b, p * b + count)
        tl = matmul(jnp.concatenate([x[...] for x in ti[p : p + step]], 0), text_t[...], 1, 1) * (scale_t * LOG2E)
        sl = matmul(image_s[rows, :], text_s[...], 1, 1) * (scale_s * LOG2E)
        tl_ref[rows, :] = tl
        sl_ref[rows, :] = sl
        top_t, top_s = jnp.max(tl, 0, keepdims=True), jnp.max(sl, 0, keepdims=True)
        peak_t = top_t if peak_t is None else jnp.maximum(peak_t, top_t)
        peak_s = top_s if peak_s is None else jnp.maximum(peak_s, top_s)
        mt, ms = jnp.max(tl, 1, keepdims=True), jnp.max(sl, 1, keepdims=True)
        et = jnp.exp2(tl - mt)
        sum_t = jnp.sum(et, 1, keepdims=True)
        gap = jnp.sum(et * (tl - sl), 1, keepdims=True)
        sum_s = jnp.sum(jnp.exp2(sl - ms), 1, keepdims=True)
        lines = (mt + jnp.log2(sum_t), ms + jnp.log2(sum_s), gap / sum_t)
        lines = stack_rows(lines, (count, 128), 1, core[0] * KINDS)
        for k in range(step):
            flat = jnp.transpose(lines[block(k, b)])[:LINES]
            other = (p + k) ^ (nr // 2)
            row_ref[:, block(p + k, b)] = with_largest(flat, p + k)
            swap_ref[:, block(other, b)] = with_largest(flat, other)
    peak_ref[...] = stack_rows((peak_t, peak_s), peak_ref.shape, 0)


def column_kernel(step, tl_ref, sl_ref, peaks, image, col_ref):
    peak_t, peak_s = peaks[0:1, :], peaks[1:2, :]
    sums = None
    for k in range(0, tl_ref.shape[0], step):
        tl, sl = tl_ref[k : k + step, :], sl_ref[k : k + step, :]
        et = jnp.exp2(tl - peak_t)
        parts = [jnp.sum(x, 0, keepdims=True) for x in (et, jnp.exp2(sl - peak_s), et * (tl - sl))]
        sums = parts if sums is None else [x + y for x, y in zip(sums, parts)]
    most = jnp.max(jnp.abs(image[...].astype(F32)), 0, keepdims=True)
    if col_ref.shape[1] > most.shape[1]:
        most = jnp.concatenate([most, jnp.zeros((1, col_ref.shape[1] - most.shape[1]), F32)], 1)
    lines = (peak_t + jnp.log2(sums[0]), peak_s + jnp.log2(sums[1]), sums[2] / sums[0], most)
    col_ref[...] = stack_rows(lines, col_ref.shape, 0)


def join_kernel(teacher, student, both):
    tw = teacher.shape[1]
    both[:, :tw] = teacher[...]
    both[:, tw:] = student[...]


def digits(share, rank, slots, width):
    rows = []
    for unit in DIGITS:
        digit = jnp.floor(share * (1.0 / unit))
        share = share - digit * unit
        rows.append(digit)
    lane = lax.broadcasted_iota(jnp.int32, (EXTRA, width), 1)
    return jnp.where(lane // (width // slots) == rank, stack_rows(rows, (EXTRA, width), 0), 0.0)


def combine(tiles, terms):
    lses = []
    for kind in (1, 0):
        peak = tree(jnp.maximum, [x[kind] for x in tiles])
        weights = [jnp.exp2(x[kind] - peak) for x in tiles]
        total = tree(jnp.add, weights)
        lses.append(peak + jnp.log2(total))
    for k, (w, x) in enumerate(zip(weights, tiles)):
        terms[k : k + 1, :] = w * x[2]
    gap = tree(jnp.add, [terms[k : k + 1, :] for k in range(len(tiles))])
    return lses[1], lses[0], gap / total + (lses[0] - lses[1])


def sum_blocks(x, b):
    parts = [jnp.sum(x[:, block(p, b)], axis=(0, 1), keepdims=True) for p in range(x.shape[1] // b)]
    return tree(jnp.add, parts) * LN2


def powers(largest, pairs, scale):
    bound = functools.reduce(jnp.maximum, largest) * ((1 + pairs) * scale)
    power = jnp.ceil(jnp.log2(jnp.maximum(bound, 1e-30)))
    return jnp.exp2(15.0 - power) * scale, jnp.exp2(power - 15.0)


def split_lines(refs, n):
    views = []
    while len(views) < n:
        views += [refs[0].at[block(k, LINES), :] for k in range(refs[0].shape[0] // LINES)]
        refs = refs[1:]
    return views, refs


def delta_kernel(nr, nc, b, pairs, scale, place, *refs):
    text, tl_ref, sl_ref, refs = *refs[:3], refs[3:]
    row_parts, refs = split_lines(refs, nr // 2)
    col_parts, refs = split_lines(refs, nc)
    other_near, other_far, high_ref, low_ref, refs = *refs[:4], refs[4:]
    image_back_ref, text_back_ref, scale_ref, image_extra, text_extra, row_terms, col_terms = refs
    width = image_back_ref.shape[1]
    lines = [x[2 * KINDS + core : 2 * KINDS + core + 1, :width] for x in row_parts for core in range(2)]
    image_scale, image_back = powers(lines, pairs, scale)
    text_scale, text_back = powers([x[KINDS : KINDS + 1, :width] for x in col_parts], pairs, scale)
    image_back_ref[...] = image_back
    text_back_ref[...] = text_back
    scale_ref[...] = stack_rows((image_scale, text_scale), scale_ref.shape, 0)
    tiles = []
    for q in range(nr // 2):
        x = jnp.concatenate([row_parts[q][:, block(p ^ q, b)] for p in range(nr)], 1)
        for core in range(2):
            tiles.append([x[core * KINDS + k : core * KINDS + k + 1, :] for k in range(KINDS)])
    row_t, row_s, terms = combine(tiles, row_terms)
    row_share = sum_blocks(terms, b)
    rows = stack_rows((row_t, row_s), (LINES, nr * b), 0)
    tiles = []
    for q in range(nc):
        x = jnp.concatenate([col_parts[q][:, block(p ^ q, b)] for p in range(nc)], 1)
        tiles.append([x[k : k + 1, :] for k in range(KINDS)])
    col_t, col_s, terms = combine(tiles, col_terms)
    col_share = sum_blocks(terms, b)
    for p in range(nr):
        row = jnp.transpose(rows[:, block(p, b)])
        tl, sl = tl_ref[block(p, b), :], sl_ref[block(p, b), :]
        delta = (jnp.exp2(sl - row[:, 1:2]) - jnp.exp2(tl - row[:, 0:1])) + (
            jnp.exp2(sl - col_s) - jnp.exp2(tl - col_t)
        )
        high = delta.astype(BF16)
        high_ref[block(p, b), :] = high
        low_ref[block(p, b), :] = (delta - high.astype(F32)).astype(BF16)
    image_extra[...] = digits(col_share * (1.0 / (nc * b)), place[1], nr, width)
    text_extra[...] = digits(row_share * (1.0 / (nr * b)), place[2], nc, width)
    rows = nr * b // 4
    for n, ref in ((3, other_far), (2, other_near)):
        ref[:rows, :] = product(high_ref, low_ref, (block(n, rows), slice(None)), text, 1) * image_scale
        ref[rows:, :] = image_extra[...]


def product(high_ref, low_ref, place, other, dim):
    return matmul(high_ref[place], other[...], dim, 0) + matmul(low_ref[place], other[...], dim, 0)


def gradient_kernel(image, text, high_ref, low_ref, scale_ref, image_extra, text_extra, near, far, keep, send):
    rows, cols = near.shape[0] - EXTRA, keep.shape[0] - EXTRA
    for n, ref in ((1, far), (0, near)):
        ref[:rows, :] = product(high_ref, low_ref, (block(n, rows), slice(None)), text, 1) * scale_ref[0:1, :]
        ref[rows:, :] = image_extra[...]
    for n, ref in ((1, send), (0, keep)):
        ref[:cols, :] = product(high_ref, low_ref, (slice(None), block(n, cols)), image, 0) * scale_ref[1:2, :]
        ref[cols:, :] = text_extra[...]


def call(kernel, outs, args, scratch=(), flops=0, transcendentals=0):
    shapes = [jax.ShapeDtypeStruct(s, d) for s, d in outs]
    size = sum(x.size * x.dtype.itemsize for x in list(args) + shapes)
    held = sum(math.prod(s) * jnp.dtype(d).itemsize for s, d in scratch)
    return pl.pallas_call(
        kernel,
        out_shape=shapes,
        in_specs=[SMEM if x.dtype == jnp.int32 else VMEM for x in args],
        out_specs=[VMEM] * len(shapes),
        scratch_shapes=[pltpu.VMEM(s, d) for s, d in scratch],
        compiler_params=pltpu.CompilerParams(vmem_limit_bytes=size + held + ROOM),
        cost_estimate=pl.CostEstimate(flops=flops, bytes_accessed=size, transcendentals=transcendentals),
    )(*args)


def swap(bits, x):
    perm = [(i, i ^ ((1 << len(bits)) - 1)) for i in range(1 << len(bits))]
    return lax.ppermute(x, bits, perm)


def subset(bits, q):
    return tuple(b for k, b in enumerate(bits) if q >> k & 1)


def together(*groups):
    return lax.optimization_barrier(groups)


def gather(groups):
    blocks, own = [], []
    for bits, both, apart in groups:
        first = swap(bits[:1], apart[0])
        own.append(swap(bits[1:2], both))
        second = swap(bits[:1], together(apart[1], first)[0])
        blocks.append([(both,), (first, second)])
    late = [x[1][1] for x in blocks]
    for n, (bits, both, _) in enumerate(groups):
        for k in range(1, len(bits)):
            if k == 1:
                first, second = blocks[n][1]
                ways = [(together(first, own[n])[0], second)]
                new = [(own[n],)]
            else:
                ways = together(blocks[n][1:], late)[0]
                new = [(swap(bits[k : k + 1], together(both, own[n])[0]),)]
            blocks[n] = blocks[n] + new + [tuple(swap(bits[k : k + 1], y) for y in parts) for parts in ways]
    return blocks


def exchange(bits, x):
    parts = [x]
    for bit in bits:
        parts.append(swap((bit,), jnp.concatenate(parts) if len(parts) > 1 else x))
    return parts


def add_message(keep, come):
    rows = keep[0].shape[0]
    come = come.astype(F32)
    return keep[0] + come[:rows], keep[1] + come[rows:]


def local(image_bits, text_bits, teacher_image, teacher_text, student_image, student_text):
    b, tw = teacher_image.shape
    sw = student_image.shape[1]
    nr, nc = 1 << len(image_bits), 1 << len(text_bits)
    r, c = nr * b, nc * b
    pair, others = image_bits[-1:], image_bits[:-1]
    (image,) = call(join_kernel, [((b, tw + sw), BF16)], [teacher_image, student_image])
    (text,) = call(join_kernel, [((b, tw + sw), BF16)], [teacher_text, student_text])
    images, texts = gather(
        [(image_bits, image, (teacher_image, student_image)), (text_bits, text, (teacher_text, student_text))]
    )
    forms = [[len(x) for x in blocks] for blocks in (images, texts)]
    place = jnp.stack([lax.axis_index(x) for x in (pair, image_bits, text_bits)]).astype(jnp.int32)
    tl, sl, rows, rows_swapped, peaks, image, text = call(
        functools.partial(stats_kernel, *forms, b, tw, tw**-0.5, sw**-0.5),
        [((r, c), F32), ((r, c), F32), ((LINES, r), F32), ((LINES, r), F32), ((LINES, c), F32), ((r, sw), BF16), ((c, sw), BF16)],
        [place] + [x for parts in images + texts for x in parts], [((c, tw), BF16)], 2 * r * c * (tw + sw), 4 * r * c,
    )
    other = swap(pair, rows_swapped)
    (cols,) = call(
        functools.partial(column_kernel, 2 * b), [((LINES, c), F32)], [tl, sl, peaks, image], (), 0, 2 * r * c
    )
    row_parts, col_parts = exchange(others, rows + other), exchange(text_bits, cols)
    pairs = b << (len(image_bits) + len(text_bits))
    row, extra = ((1, sw), F32), ((EXTRA, sw), F32)
    near_shape, keep_shape = ((r // 4 + EXTRA, sw), F32), ((c // 2 + EXTRA, sw), F32)
    other_near, other_far, high, low, image_back, text_back, *more = call(
        functools.partial(delta_kernel, nr, nc, b, pairs, sw**-0.5),
        [near_shape, near_shape, ((r, c), BF16), ((r, c), BF16), row, row, ((8, sw), F32), extra, extra],
        [place, text, tl, sl] + row_parts + col_parts,
        [((nr, r), F32), ((max(nc, 8), c), F32)], 2 * r * c * sw, 4 * r * c,
    )
    other_far, other_near = swap(pair, other_far), swap(pair, other_near)
    near, far, text_keep, text_send = call(
        gradient_kernel, [near_shape, near_shape, keep_shape, keep_shape], [image, text, high, low] + more, (), 6 * r * c * sw
    )
    image_send = far + other_far
    image_keep = near + other_near
    image_keep, text_keep = [(x[:-EXTRA], x[-EXTRA:]) for x in (image_keep, text_keep)]
    for k in reversed(range(max(len(text_bits), len(others)))):
        todo = {}
        if k < len(text_bits):
            todo["text"] = text_send.astype(F16)
        if k < len(others):
            todo["image"] = image_send.astype(F16)
        (todo,) = together(todo)
        half = b << k >> 1
        if k < len(text_bits):
            body, extra = text_keep = add_message(text_keep, swap(text_bits[k : k + 1], todo["text"]))
            if k:
                text_keep, text_send = (body[:half], extra), jnp.concatenate([body[half:], extra])
        if k < len(others):
            body, extra = image_keep = add_message(image_keep, swap(others[k : k + 1], todo["image"]))
            if k:
                image_keep, image_send = (body[:half], extra), jnp.concatenate([body[half:], extra])
    units = stack_rows(DIGITS, (EXTRA, sw), 0)
    loss = jnp.sum((image_keep[1] + text_keep[1]) * units) * (0.5 / sw)
    return (loss, image_keep[0] * image_back, text_keep[0] * text_back)


def solution(mesh):
    bits = {axis: [f"{axis}{k}" for k in reversed(range(mesh.shape[axis].bit_length() - 1))] for axis in ("img", "txt")}
    names = bits["img"] + bits["txt"]
    cube = Mesh(np.asarray(mesh.devices).reshape((2,) * len(names)), names)
    image_bits = bits["img"][:-1] + [x for x in bits["txt"] if int(x[3:]) % 2 == 0]
    text_bits = [x for x in names if x not in image_bits]
    image, text = P(tuple(names), None), P(tuple(bits["txt"] + bits["img"]), None)
    return jax.shard_map(
        functools.partial(local, tuple(image_bits), tuple(text_bits)),
        mesh=cube,
        in_specs=(image, text, image, text),
        out_specs=(P(), image, text),
        check_vma=False,
    )
```

```python
import functools
import math

import jax
import jax.numpy as jnp
import numpy as np
from jax import lax
from jax.experimental import pallas as pl
from jax.experimental.pallas import tpu as pltpu
from jax.sharding import Mesh, PartitionSpec as P

F32 = jnp.float32
BF16 = jnp.bfloat16
F16 = jnp.float16
LOG2E = 1.4426950408889634
LN2 = 0.6931471805599453
LINES = 8
KINDS = 3
EXTRA = 16
DIGITS = (64.0, 2.0**-4, 2.0**-14, 2.0**-24, 2.0**-34)
MOST = 60 * 2**20
ROOM = 12 * 2**20
VMEM = pl.BlockSpec(memory_space=pltpu.VMEM)
SMEM = pl.BlockSpec(memory_space=pltpu.SMEM)


def matmul(a, b, da, db):
    return lax.dot_general(a, b, (((da,), (db,)), ((), ())), preferred_element_type=F32)


def block(k, b):
    return slice(k * b, (k + 1) * b)


def stack_rows(values, shape, axis, first=0):
    index = lax.broadcasted_iota(jnp.int32, shape, axis) - first
    out = jnp.zeros(shape, F32)
    for k, value in enumerate(values):
        out = jnp.where(index == k, value, out)
    return out


def tree(op, items):
    while len(items) > 1:
        items = [op(x, y) for x, y in zip(items[::2], items[1::2])]
    return items[0]


def stats_kernel(nr, nc, b, tw, scale_t, scale_s, core, *refs):
    images, texts, refs = refs[:nr], refs[nr : nr + nc], refs[nr + nc :]
    tl_ref, sl_ref, row_ref, swap_ref, peak_ref, image_s, text_s, text_t = refs
    for p in range(nc):
        text_t[block(p, b), :] = texts[p][:, :tw]
        text_s[block(p, b), :] = texts[p][:, tw:]
    for p in range(nr):
        image_s[block(p, b), :] = images[p][:, tw:]
    largest = jnp.max(jnp.abs(text_s[...].astype(F32)), 0, keepdims=True)
    width = largest.shape[1]

    def with_largest(flat, k):
        if (k + 1) * b > width:
            return flat
        return flat + stack_rows((largest[:, block(k, b)],), flat.shape, 0, 2 * KINDS + core[0])

    step = 2 if nr % 2 == 0 else 1
    count = step * b
    peak_t = peak_s = None
    for p in range(0, nr, step):
        rows = slice(p * b, p * b + count)
        tl = matmul(jnp.concatenate([x[:, :tw] for x in images[p : p + step]], 0), text_t[...], 1, 1) * (scale_t * LOG2E)
        sl = matmul(image_s[rows, :], text_s[...], 1, 1) * (scale_s * LOG2E)
        tl_ref[rows, :] = tl
        sl_ref[rows, :] = sl
        top_t, top_s = jnp.max(tl, 0, keepdims=True), jnp.max(sl, 0, keepdims=True)
        peak_t = top_t if peak_t is None else jnp.maximum(peak_t, top_t)
        peak_s = top_s if peak_s is None else jnp.maximum(peak_s, top_s)
        mt, ms = jnp.max(tl, 1, keepdims=True), jnp.max(sl, 1, keepdims=True)
        et = jnp.exp2(tl - mt)
        sum_t = jnp.sum(et, 1, keepdims=True)
        gap = jnp.sum(et * (tl - sl), 1, keepdims=True)
        sum_s = jnp.sum(jnp.exp2(sl - ms), 1, keepdims=True)
        lines = (mt + jnp.log2(sum_t), ms + jnp.log2(sum_s), gap / sum_t)
        lines = stack_rows(lines, (count, 128), 1, core[0] * KINDS)
        for k in range(step):
            flat = jnp.transpose(lines[block(k, b)])[:LINES]
            other = (p + k) ^ (nr // 2)
            row_ref[:, block(p + k, b)] = with_largest(flat, p + k)
            swap_ref[:, block(other, b)] = with_largest(flat, other)
    peak_ref[...] = stack_rows((peak_t, peak_s), peak_ref.shape, 0)


def column_kernel(step, tl_ref, sl_ref, peaks, image, col_ref):
    peak_t, peak_s = peaks[0:1, :], peaks[1:2, :]
    sums = None
    for k in range(0, tl_ref.shape[0], step):
        tl, sl = tl_ref[k : k + step, :], sl_ref[k : k + step, :]
        et = jnp.exp2(tl - peak_t)
        parts = [jnp.sum(x, 0, keepdims=True) for x in (et, jnp.exp2(sl - peak_s), et * (tl - sl))]
        sums = parts if sums is None else [x + y for x, y in zip(sums, parts)]
    most = jnp.max(jnp.abs(image[...].astype(F32)), 0, keepdims=True)
    if col_ref.shape[1] > most.shape[1]:
        most = jnp.concatenate([most, jnp.zeros((1, col_ref.shape[1] - most.shape[1]), F32)], 1)
    lines = (peak_t + jnp.log2(sums[0]), peak_s + jnp.log2(sums[1]), sums[2] / sums[0], most)
    col_ref[...] = stack_rows(lines, col_ref.shape, 0)


def join_kernel(teacher, student, both):
    tw = teacher.shape[1]
    both[:, :tw] = teacher[...]
    both[:, tw:] = student[...]


def send_kernel(teacher_image, student_image, teacher_text, student_text, image, text, sems):
    tw = teacher_image.shape[1]
    copies = [
        pltpu.make_async_copy(teacher_image, image.at[:, :tw], sems.at[0]),
        pltpu.make_async_copy(student_image, image.at[:, tw:], sems.at[1]),
        pltpu.make_async_copy(teacher_text, text.at[:, :tw], sems.at[2]),
        pltpu.make_async_copy(student_text, text.at[:, tw:], sems.at[3]),
    ]
    for copy in copies:
        copy.start()
    for copy in copies:
        copy.wait()


def digits(share, rank, slots, width):
    rows = []
    for unit in DIGITS:
        digit = jnp.floor(share * (1.0 / unit))
        share = share - digit * unit
        rows.append(digit)
    lane = lax.broadcasted_iota(jnp.int32, (EXTRA, width), 1)
    return jnp.where(lane // (width // slots) == rank, stack_rows(rows, (EXTRA, width), 0), 0.0)


def combine(tiles, terms):
    lses = []
    for kind in (1, 0):
        peak = tree(jnp.maximum, [x[kind] for x in tiles])
        weights = [jnp.exp2(x[kind] - peak) for x in tiles]
        total = tree(jnp.add, weights)
        lses.append(peak + jnp.log2(total))
    for k, (w, x) in enumerate(zip(weights, tiles)):
        terms[k : k + 1, :] = w * x[2]
    gap = tree(jnp.add, [terms[k : k + 1, :] for k in range(len(tiles))])
    return lses[1], lses[0], gap / total + (lses[0] - lses[1])


def sum_blocks(x, b):
    parts = [jnp.sum(x[:, block(p, b)], axis=(0, 1), keepdims=True) for p in range(x.shape[1] // b)]
    return tree(jnp.add, parts) * LN2


def powers(largest, pairs, scale):
    bound = functools.reduce(jnp.maximum, largest) * ((1 + pairs) * scale)
    power = jnp.ceil(jnp.log2(jnp.maximum(bound, 1e-30)))
    return jnp.exp2(15.0 - power) * scale, jnp.exp2(power - 15.0)


def split_lines(refs, n):
    views = []
    while len(views) < n:
        views += [refs[0].at[block(k, LINES), :] for k in range(refs[0].shape[0] // LINES)]
        refs = refs[1:]
    return views, refs


def delta_kernel(nr, nc, b, pairs, scale, place, *refs):
    text, tl_ref, sl_ref, refs = *refs[:3], refs[3:]
    row_parts, refs = split_lines(refs, nr // 2)
    col_parts, refs = split_lines(refs, nc)
    other_near, other_far, high_ref, low_ref, refs = *refs[:4], refs[4:]
    image_back_ref, text_back_ref, scale_ref, image_extra, text_extra, row_terms, col_terms = refs
    width = image_back_ref.shape[1]
    lines = [x[2 * KINDS + core : 2 * KINDS + core + 1, :width] for x in row_parts for core in range(2)]
    image_scale, image_back = powers(lines, pairs, scale)
    text_scale, text_back = powers([x[KINDS : KINDS + 1, :width] for x in col_parts], pairs, scale)
    image_back_ref[...] = image_back
    text_back_ref[...] = text_back
    scale_ref[...] = stack_rows((image_scale, text_scale), scale_ref.shape, 0)
    tiles = []
    for q in range(nr // 2):
        x = jnp.concatenate([row_parts[q][:, block(p ^ q, b)] for p in range(nr)], 1)
        for core in range(2):
            tiles.append([x[core * KINDS + k : core * KINDS + k + 1, :] for k in range(KINDS)])
    row_t, row_s, terms = combine(tiles, row_terms)
    row_share = sum_blocks(terms, b)
    rows = stack_rows((row_t, row_s), (LINES, nr * b), 0)
    tiles = []
    for q in range(nc):
        x = jnp.concatenate([col_parts[q][:, block(p ^ q, b)] for p in range(nc)], 1)
        tiles.append([x[k : k + 1, :] for k in range(KINDS)])
    col_t, col_s, terms = combine(tiles, col_terms)
    col_share = sum_blocks(terms, b)
    for p in range(nr):
        row = jnp.transpose(rows[:, block(p, b)])
        tl, sl = tl_ref[block(p, b), :], sl_ref[block(p, b), :]
        delta = (jnp.exp2(sl - row[:, 1:2]) - jnp.exp2(tl - row[:, 0:1])) + (
            jnp.exp2(sl - col_s) - jnp.exp2(tl - col_t)
        )
        high = delta.astype(BF16)
        high_ref[block(p, b), :] = high
        low_ref[block(p, b), :] = (delta - high.astype(F32)).astype(BF16)
    image_extra[...] = digits(col_share * (1.0 / (nc * b)), place[1], nr, width)
    text_extra[...] = digits(row_share * (1.0 / (nr * b)), place[2], nc, width)
    rows = nr * b // 4
    for n, ref in ((3, other_far), (2, other_near)):
        ref[:rows, :] = product(high_ref, low_ref, (block(n, rows), slice(None)), text, 1) * image_scale
        ref[rows:, :] = image_extra[...]


def product(high_ref, low_ref, place, other, dim):
    return matmul(high_ref[place], other[...], dim, 0) + matmul(low_ref[place], other[...], dim, 0)


def gradient_kernel(image, text, high_ref, low_ref, scale_ref, image_extra, text_extra, near, far, keep, send):
    rows, cols = near.shape[0] - EXTRA, keep.shape[0] - EXTRA
    for n, ref in ((1, far), (0, near)):
        ref[:rows, :] = product(high_ref, low_ref, (block(n, rows), slice(None)), text, 1) * scale_ref[0:1, :]
        ref[rows:, :] = image_extra[...]
    for n, ref in ((1, send), (0, keep)):
        ref[:cols, :] = product(high_ref, low_ref, (slice(None), block(n, cols)), image, 0) * scale_ref[1:2, :]
        ref[cols:, :] = text_extra[...]


def last_kernel(*refs):
    (image, image_extra, image_come, image_back), (text, text_extra, text_come, text_back) = refs[:4], refs[4:8]
    image_grad, text_grad, loss = refs[8:]
    rows, width = image.shape
    image_grad[...] = (image[...] + image_come[:rows, :]) * image_back[...]
    text_grad[...] = (text[...] + text_come[:rows, :]) * text_back[...]
    counts = (image_extra[...] + image_come[rows:, :]) + (text_extra[...] + text_come[rows:, :])
    counts = counts * stack_rows(DIGITS, counts.shape, 0)
    loss[...] = jnp.sum(counts, axis=(0, 1), keepdims=True) * (0.5 / width)


def call(kernel, outs, args, scratch=(), flops=0, transcendentals=0):
    shapes = [jax.ShapeDtypeStruct(s, d) for s, d in outs]
    size = sum(x.size * x.dtype.itemsize for x in list(args) + shapes)
    held = sum(math.prod(s) * jnp.dtype(d).itemsize for s, d in scratch)
    return pl.pallas_call(
        kernel,
        out_shape=shapes,
        in_specs=[SMEM if x.dtype == jnp.int32 else VMEM for x in args],
        out_specs=[VMEM] * len(shapes),
        scratch_shapes=[pltpu.VMEM(s, d) for s, d in scratch],
        compiler_params=pltpu.CompilerParams(vmem_limit_bytes=size + held + ROOM),
        cost_estimate=pl.CostEstimate(flops=flops, bytes_accessed=size, transcendentals=transcendentals),
    )(*args)


def swap(bits, x):
    perm = [(i, i ^ ((1 << len(bits)) - 1)) for i in range(1 << len(bits))]
    return lax.ppermute(x, bits, perm)


def subset(bits, q):
    return tuple(b for k, b in enumerate(bits) if q >> k & 1)


def together(*groups):
    return lax.optimization_barrier(groups)


def gather(bits, x):
    blocks = [x]
    for k, bit in enumerate(bits):
        own = together(x, blocks[2])[0] if k > 1 else x
        blocks = blocks + [swap((bit,), y) for y in [own] + blocks[1:]]
    return blocks


def exchange(bits, x):
    parts = [x]
    for bit in bits:
        parts.append(swap((bit,), jnp.concatenate(parts) if len(parts) > 1 else x))
    return parts


def add_message(keep, come):
    rows = keep[0].shape[0]
    come = come.astype(F32)
    return keep[0] + come[:rows], keep[1] + come[rows:]


def local(image_bits, text_bits, teacher_image, teacher_text, student_image, student_text):
    b, tw = teacher_image.shape
    sw = student_image.shape[1]
    nr, nc = 1 << len(image_bits), 1 << len(text_bits)
    r, c = nr * b, nc * b
    pair, others = image_bits[-1:], image_bits[:-1]
    whole = jax.ShapeDtypeStruct((b, tw + sw), BF16)
    image, text = pl.pallas_call(
        send_kernel,
        out_shape=[whole, whole],
        in_specs=[pl.BlockSpec(memory_space=pltpu.HBM)] * 4,
        out_specs=[VMEM] * 2,
        scratch_shapes=[pltpu.SemaphoreType.DMA((4,))],
        compiler_params=pltpu.CompilerParams(vmem_limit_bytes=MOST),
    )(teacher_image, student_image, teacher_text, student_text)
    images, texts = gather(image_bits, image), gather(text_bits, text)
    own = together([teacher_image, student_image, teacher_text, student_text], [images[2], texts[2]])[0]
    (images[0],) = call(join_kernel, [((b, tw + sw), BF16)], own[:2])
    (texts[0],) = call(join_kernel, [((b, tw + sw), BF16)], own[2:])
    place = jnp.stack([lax.axis_index(x) for x in (pair, image_bits, text_bits)]).astype(jnp.int32)
    tl, sl, rows, rows_swapped, peaks, image, text = call(
        functools.partial(stats_kernel, nr, nc, b, tw, tw**-0.5, sw**-0.5),
        [((r, c), F32), ((r, c), F32), ((LINES, r), F32), ((LINES, r), F32), ((LINES, c), F32), ((r, sw), BF16), ((c, sw), BF16)],
        [place] + images + texts, [((c, tw), BF16)], 2 * r * c * (tw + sw), 4 * r * c,
    )
    other = swap(pair, rows_swapped)
    (cols,) = call(
        functools.partial(column_kernel, 2 * b), [((LINES, c), F32)], [tl, sl, peaks, image], (), 0, 2 * r * c
    )
    row_parts, col_parts = exchange(others, rows + other), exchange(text_bits, cols)
    pairs = b << (len(image_bits) + len(text_bits))
    row, extra = ((1, sw), F32), ((EXTRA, sw), F32)
    near_shape, keep_shape = ((r // 4 + EXTRA, sw), F32), ((c // 2 + EXTRA, sw), F32)
    other_near, other_far, high, low, image_back, text_back, *more = call(
        functools.partial(delta_kernel, nr, nc, b, pairs, sw**-0.5),
        [near_shape, near_shape, ((r, c), BF16), ((r, c), BF16), row, row, ((8, sw), F32), extra, extra],
        [place, text, tl, sl] + row_parts + col_parts,
        [((nr, r), F32), ((max(nc, 8), c), F32)], 2 * r * c * sw, 4 * r * c,
    )
    other_far, other_near = swap(pair, other_far), swap(pair, other_near)
    near, far, text_keep, text_send = call(
        gradient_kernel, [near_shape, near_shape, keep_shape, keep_shape], [image, text, high, low] + more, (), 6 * r * c * sw
    )
    image_send = far + other_far
    image_keep = near + other_near
    image_keep, text_keep = [(x[:-EXTRA], x[-EXTRA:]) for x in (image_keep, text_keep)]
    for k in reversed(range(max(len(text_bits), len(others)))):
        todo = {}
        if k < len(text_bits):
            todo["text"] = text_send.astype(F16)
        if k < len(others):
            todo["image"] = image_send.astype(F16)
        (todo,) = together(todo)
        half = b << k >> 1
        if k < len(text_bits):
            text_come = swap(text_bits[k : k + 1], todo["text"])
            if k:
                body, extra = add_message(text_keep, text_come)
                text_keep, text_send = (body[:half], extra), jnp.concatenate([body[half:], extra])
        if k < len(others):
            image_come = swap(others[k : k + 1], todo["image"])
            if k:
                body, extra = add_message(image_keep, image_come)
                image_keep, image_send = (body[:half], extra), jnp.concatenate([body[half:], extra])
    image_grad, text_grad, loss = call(
        last_kernel, [((b, sw), F32), ((b, sw), F32), ((1, 1), F32)],
        [*image_keep, image_come.astype(F32), image_back, *text_keep, text_come.astype(F32), text_back],
    )
    return (loss.reshape(()), image_grad, text_grad)


def solution(mesh):
    bits = {axis: [f"{axis}{k}" for k in reversed(range(mesh.shape[axis].bit_length() - 1))] for axis in ("img", "txt")}
    names = bits["img"] + bits["txt"]
    cube = Mesh(np.asarray(mesh.devices).reshape((2,) * len(names)), names)
    image_bits = bits["img"][:-1] + [x for x in bits["txt"] if int(x[3:]) % 2 == 0]
    text_bits = [x for x in names if x not in image_bits]
    image, text = P(tuple(names), None), P(tuple(bits["txt"] + bits["img"]), None)
    return jax.shard_map(
        functools.partial(local, tuple(image_bits), tuple(text_bits)),
        mesh=cube,
        in_specs=(image, text, image, text),
        out_specs=(P(), image, text),
        check_vma=False,
    )
```

```python
import functools
import math

import jax
import jax.numpy as jnp
import numpy as np
from jax import lax
from jax.experimental import pallas as pl
from jax.experimental.pallas import tpu as pltpu
from jax.sharding import Mesh, PartitionSpec as P

F32 = jnp.float32
BF16 = jnp.bfloat16
F16 = jnp.float16
LOG2E = 1.4426950408889634
LN2 = 0.6931471805599453
LINES = 8
KINDS = 3
EXTRA = 16
DIGITS = (64.0, 2.0**-4, 2.0**-14, 2.0**-24, 2.0**-34)
MOST = 60 * 2**20
ROOM = 12 * 2**20
VMEM = pl.BlockSpec(memory_space=pltpu.VMEM)
SMEM = pl.BlockSpec(memory_space=pltpu.SMEM)


def matmul(a, b, da, db):
    return lax.dot_general(a, b, (((da,), (db,)), ((), ())), preferred_element_type=F32)


def block(k, b):
    return slice(k * b, (k + 1) * b)


def stack_rows(values, shape, axis, first=0):
    index = lax.broadcasted_iota(jnp.int32, shape, axis) - first
    out = jnp.zeros(shape, F32)
    for k, value in enumerate(values):
        out = jnp.where(index == k, value, out)
    return out


def tree(op, items):
    while len(items) > 1:
        items = [op(x, y) for x, y in zip(items[::2], items[1::2])]
    return items[0]


def stats_kernel(nr, nc, b, tw, scale_t, scale_s, core, *refs):
    images, texts, refs = refs[:nr], refs[nr : nr + nc], refs[nr + nc :]
    tl_ref, sl_ref, row_ref, swap_ref, peak_ref, image_s, text_s, text_t = refs
    for p in range(nc):
        text_t[block(p, b), :] = texts[p][:, :tw]
        text_s[block(p, b), :] = texts[p][:, tw:]
    for p in range(nr):
        image_s[block(p, b), :] = images[p][:, tw:]
    largest = jnp.max(jnp.abs(text_s[...].astype(F32)), 0, keepdims=True)
    width = largest.shape[1]

    def with_largest(flat, k):
        if (k + 1) * b > width:
            return flat
        return flat + stack_rows((largest[:, block(k, b)],), flat.shape, 0, 2 * KINDS + core[0])

    step = math.gcd(nr, 4)
    count = step * b
    peak_t = peak_s = None
    for p in range(0, nr, step):
        rows = slice(p * b, p * b + count)
        tl = matmul(jnp.concatenate([x[:, :tw] for x in images[p : p + step]], 0), text_t[...], 1, 1) * (scale_t * LOG2E)
        sl = matmul(image_s[rows, :], text_s[...], 1, 1) * (scale_s * LOG2E)
        tl_ref[rows, :] = tl
        sl_ref[rows, :] = sl
        top_t, top_s = jnp.max(tl, 0, keepdims=True), jnp.max(sl, 0, keepdims=True)
        peak_t = top_t if peak_t is None else jnp.maximum(peak_t, top_t)
        peak_s = top_s if peak_s is None else jnp.maximum(peak_s, top_s)
        mt, ms = jnp.max(tl, 1, keepdims=True), jnp.max(sl, 1, keepdims=True)
        et = jnp.exp2(tl - mt)
        sum_t = jnp.sum(et, 1, keepdims=True)
        gap = jnp.sum(et * (tl - sl), 1, keepdims=True)
        sum_s = jnp.sum(jnp.exp2(sl - ms), 1, keepdims=True)
        lines = (mt + jnp.log2(sum_t), ms + jnp.log2(sum_s), gap / sum_t)
        lines = stack_rows(lines, (count, 128), 1, core[0] * KINDS)
        for k in range(step):
            flat = jnp.transpose(lines[block(k, b)])[:LINES]
            other = (p + k) ^ (nr // 2)
            row_ref[:, block(p + k, b)] = with_largest(flat, p + k)
            swap_ref[:, block(other, b)] = with_largest(flat, other)
    peak_ref[...] = stack_rows((peak_t, peak_s), peak_ref.shape, 0)


def column_kernel(step, tl_ref, sl_ref, peaks, image, col_ref):
    peak_t, peak_s = peaks[0:1, :], peaks[1:2, :]
    sums = None
    for k in range(0, tl_ref.shape[0], step):
        tl, sl = tl_ref[k : k + step, :], sl_ref[k : k + step, :]
        et = jnp.exp2(tl - peak_t)
        parts = [jnp.sum(x, 0, keepdims=True) for x in (et, jnp.exp2(sl - peak_s), et * (tl - sl))]
        sums = parts if sums is None else [x + y for x, y in zip(sums, parts)]
    most = jnp.max(jnp.abs(image[...].astype(F32)), 0, keepdims=True)
    if col_ref.shape[1] > most.shape[1]:
        most = jnp.concatenate([most, jnp.zeros((1, col_ref.shape[1] - most.shape[1]), F32)], 1)
    lines = (peak_t + jnp.log2(sums[0]), peak_s + jnp.log2(sums[1]), sums[2] / sums[0], most)
    col_ref[...] = stack_rows(lines, col_ref.shape, 0)


def join_kernel(teacher, student, both):
    tw = teacher.shape[1]
    both[:, :tw] = teacher[...]
    both[:, tw:] = student[...]


def send_kernel(teacher_image, student_image, teacher_text, student_text, image, text, sems):
    tw = teacher_image.shape[1]
    copies = [
        pltpu.make_async_copy(teacher_image, image.at[:, :tw], sems.at[0]),
        pltpu.make_async_copy(student_image, image.at[:, tw:], sems.at[1]),
        pltpu.make_async_copy(teacher_text, text.at[:, :tw], sems.at[2]),
        pltpu.make_async_copy(student_text, text.at[:, tw:], sems.at[3]),
    ]
    for copy in copies:
        copy.start()
    for copy in copies:
        copy.wait()


def digits(share, rank, slots, width):
    rows = []
    for unit in DIGITS:
        digit = jnp.floor(share * (1.0 / unit))
        share = share - digit * unit
        rows.append(digit)
    lane = lax.broadcasted_iota(jnp.int32, (EXTRA, width), 1)
    return jnp.where(lane // (width // slots) == rank, stack_rows(rows, (EXTRA, width), 0), 0.0)


def combine(tiles, terms):
    lses = []
    for kind in (1, 0):
        peak = tree(jnp.maximum, [x[kind] for x in tiles])
        weights = [jnp.exp2(x[kind] - peak) for x in tiles]
        total = tree(jnp.add, weights)
        lses.append(peak + jnp.log2(total))
    for k, (w, x) in enumerate(zip(weights, tiles)):
        terms[k : k + 1, :] = w * x[2]
    gap = tree(jnp.add, [terms[k : k + 1, :] for k in range(len(tiles))])
    return lses[1], lses[0], gap / total + (lses[0] - lses[1])


def sum_blocks(x, b):
    parts = [jnp.sum(x[:, block(p, b)], axis=(0, 1), keepdims=True) for p in range(x.shape[1] // b)]
    return tree(jnp.add, parts) * LN2


def powers(largest, pairs, scale):
    bound = functools.reduce(jnp.maximum, largest) * ((1 + pairs) * scale)
    power = jnp.ceil(jnp.log2(jnp.maximum(bound, 1e-30)))
    return jnp.exp2(15.0 - power) * scale, jnp.exp2(power - 15.0)


def split_lines(refs, n):
    views = []
    while len(views) < n:
        views += [refs[0].at[block(k, LINES), :] for k in range(refs[0].shape[0] // LINES)]
        refs = refs[1:]
    return views, refs


def delta_kernel(nr, nc, b, pairs, scale, place, *refs):
    text, tl_ref, sl_ref, refs = *refs[:3], refs[3:]
    row_parts, refs = split_lines(refs, nr // 2)
    col_parts, refs = split_lines(refs, nc)
    other_near, other_far, high_ref, low_ref, refs = *refs[:4], refs[4:]
    image_back_ref, text_back_ref, scale_ref, image_extra, text_extra, row_terms, col_terms = refs
    width = image_back_ref.shape[1]
    lines = [x[2 * KINDS + core : 2 * KINDS + core + 1, :width] for x in row_parts for core in range(2)]
    image_scale, image_back = powers(lines, pairs, scale)
    text_scale, text_back = powers([x[KINDS : KINDS + 1, :width] for x in col_parts], pairs, scale)
    image_back_ref[...] = image_back
    text_back_ref[...] = text_back
    scale_ref[...] = stack_rows((image_scale, text_scale), scale_ref.shape, 0)
    tiles = []
    for q in range(nr // 2):
        x = jnp.concatenate([row_parts[q][:, block(p ^ q, b)] for p in range(nr)], 1)
        for core in range(2):
            tiles.append([x[core * KINDS + k : core * KINDS + k + 1, :] for k in range(KINDS)])
    row_t, row_s, terms = combine(tiles, row_terms)
    row_share = sum_blocks(terms, b)
    rows = stack_rows((row_t, row_s), (LINES, nr * b), 0)
    tiles = []
    for q in range(nc):
        x = jnp.concatenate([col_parts[q][:, block(p ^ q, b)] for p in range(nc)], 1)
        tiles.append([x[k : k + 1, :] for k in range(KINDS)])
    col_t, col_s, terms = combine(tiles, col_terms)
    col_share = sum_blocks(terms, b)
    for p in range(nr):
        row = jnp.transpose(rows[:, block(p, b)])
        tl, sl = tl_ref[block(p, b), :], sl_ref[block(p, b), :]
        delta = (jnp.exp2(sl - row[:, 1:2]) - jnp.exp2(tl - row[:, 0:1])) + (
            jnp.exp2(sl - col_s) - jnp.exp2(tl - col_t)
        )
        high = delta.astype(BF16)
        high_ref[block(p, b), :] = high
        low_ref[block(p, b), :] = (delta - high.astype(F32)).astype(BF16)
    image_extra[...] = digits(col_share * (1.0 / (nc * b)), place[1], nr, width)
    text_extra[...] = digits(row_share * (1.0 / (nr * b)), place[2], nc, width)
    rows = nr * b // 4
    for n, ref in ((3, other_far), (2, other_near)):
        ref[:rows, :] = product(high_ref, low_ref, (block(n, rows), slice(None)), text, 1) * image_scale
        ref[rows:, :] = image_extra[...]


def product(high_ref, low_ref, place, other, dim):
    return matmul(high_ref[place], other[...], dim, 0) + matmul(low_ref[place], other[...], dim, 0)


def gradient_kernel(image, text, high_ref, low_ref, scale_ref, image_extra, text_extra, near, far, keep, send):
    rows, cols = near.shape[0] - EXTRA, keep.shape[0] - EXTRA
    for n, ref in ((1, far), (0, near)):
        ref[:rows, :] = product(high_ref, low_ref, (block(n, rows), slice(None)), text, 1) * scale_ref[0:1, :]
        ref[rows:, :] = image_extra[...]
    for n, ref in ((1, send), (0, keep)):
        ref[:cols, :] = product(high_ref, low_ref, (slice(None), block(n, cols)), image, 0) * scale_ref[1:2, :]
        ref[cols:, :] = text_extra[...]


def last_kernel(*refs):
    (image, image_extra, image_come, image_back), (text, text_extra, text_come, text_back) = refs[:4], refs[4:8]
    image_grad, text_grad, loss = refs[8:]
    rows, width = image.shape
    image_grad[...] = (image[...] + image_come[:rows, :]) * image_back[...]
    text_grad[...] = (text[...] + text_come[:rows, :]) * text_back[...]
    counts = (image_extra[...] + image_come[rows:, :]) + (text_extra[...] + text_come[rows:, :])
    counts = counts * stack_rows(DIGITS, counts.shape, 0)
    loss[...] = jnp.sum(counts, axis=(0, 1), keepdims=True) * (0.5 / width)


def call(kernel, outs, args, scratch=(), flops=0, transcendentals=0):
    shapes = [jax.ShapeDtypeStruct(s, d) for s, d in outs]
    size = sum(x.size * x.dtype.itemsize for x in list(args) + shapes)
    held = sum(math.prod(s) * jnp.dtype(d).itemsize for s, d in scratch)
    return pl.pallas_call(
        kernel,
        out_shape=shapes,
        in_specs=[SMEM if x.dtype == jnp.int32 else VMEM for x in args],
        out_specs=[VMEM] * len(shapes),
        scratch_shapes=[pltpu.VMEM(s, d) for s, d in scratch],
        compiler_params=pltpu.CompilerParams(vmem_limit_bytes=size + held + ROOM),
        cost_estimate=pl.CostEstimate(flops=flops, bytes_accessed=size, transcendentals=transcendentals),
    )(*args)


def swap(bits, x):
    perm = [(i, i ^ ((1 << len(bits)) - 1)) for i in range(1 << len(bits))]
    return lax.ppermute(x, bits, perm)


def subset(bits, q):
    return tuple(b for k, b in enumerate(bits) if q >> k & 1)


def together(*groups):
    return lax.optimization_barrier(groups)


def gather(bits, x):
    blocks = [x]
    for k, bit in enumerate(bits):
        own = together(x, blocks[2])[0] if k > 1 else x
        blocks = blocks + [swap((bit,), y) for y in [own] + blocks[1:]]
    return blocks


def exchange(bits, x):
    parts = [x]
    for bit in bits:
        parts.append(swap((bit,), jnp.concatenate(parts) if len(parts) > 1 else x))
    return parts


def add_message(keep, come):
    rows = keep[0].shape[0]
    come = come.astype(F32)
    return keep[0] + come[:rows], keep[1] + come[rows:]


def local(image_bits, text_bits, teacher_image, teacher_text, student_image, student_text):
    b, tw = teacher_image.shape
    sw = student_image.shape[1]
    nr, nc = 1 << len(image_bits), 1 << len(text_bits)
    r, c = nr * b, nc * b
    pair, others = image_bits[-1:], image_bits[:-1]
    whole = jax.ShapeDtypeStruct((b, tw + sw), BF16)
    image, text = pl.pallas_call(
        send_kernel,
        out_shape=[whole, whole],
        in_specs=[pl.BlockSpec(memory_space=pltpu.HBM)] * 4,
        out_specs=[VMEM] * 2,
        scratch_shapes=[pltpu.SemaphoreType.DMA((4,))],
        compiler_params=pltpu.CompilerParams(vmem_limit_bytes=MOST),
    )(teacher_image, student_image, teacher_text, student_text)
    images, texts = gather(image_bits, image), gather(text_bits, text)
    own = together([teacher_image, student_image, teacher_text, student_text], [images[2], texts[2]])[0]
    (images[0],) = call(join_kernel, [((b, tw + sw), BF16)], own[:2])
    (texts[0],) = call(join_kernel, [((b, tw + sw), BF16)], own[2:])
    place = jnp.stack([lax.axis_index(x) for x in (pair, image_bits, text_bits)]).astype(jnp.int32)
    tl, sl, rows, rows_swapped, peaks, image, text = call(
        functools.partial(stats_kernel, nr, nc, b, tw, tw**-0.5, sw**-0.5),
        [((r, c), F32), ((r, c), F32), ((LINES, r), F32), ((LINES, r), F32), ((LINES, c), F32), ((r, sw), BF16), ((c, sw), BF16)],
        [place] + images + texts, [((c, tw), BF16)], 2 * r * c * (tw + sw), 4 * r * c,
    )
    other = swap(pair, rows_swapped)
    (cols,) = call(
        functools.partial(column_kernel, 2 * b), [((LINES, c), F32)], [tl, sl, peaks, image], (), 0, 2 * r * c
    )
    row_parts, col_parts = exchange(others, rows + other), exchange(text_bits, cols)
    pairs = b << (len(image_bits) + len(text_bits))
    row, extra = ((1, sw), F32), ((EXTRA, sw), F32)
    near_shape, keep_shape = ((r // 4 + EXTRA, sw), F32), ((c // 2 + EXTRA, sw), F32)
    other_near, other_far, high, low, image_back, text_back, *more = call(
        functools.partial(delta_kernel, nr, nc, b, pairs, sw**-0.5),
        [near_shape, near_shape, ((r, c), BF16), ((r, c), BF16), row, row, ((8, sw), F32), extra, extra],
        [place, text, tl, sl] + row_parts + col_parts,
        [((nr, r), F32), ((max(nc, 8), c), F32)], 2 * r * c * sw, 4 * r * c,
    )
    other_far, other_near = swap(pair, other_far), swap(pair, other_near)
    near, far, text_keep, text_send = call(
        gradient_kernel, [near_shape, near_shape, keep_shape, keep_shape], [image, text, high, low] + more, (), 6 * r * c * sw
    )
    image_send = far + other_far
    image_keep = near + other_near
    image_keep, text_keep = [(x[:-EXTRA], x[-EXTRA:]) for x in (image_keep, text_keep)]
    for k in reversed(range(max(len(text_bits), len(others)))):
        todo = {}
        if k < len(text_bits):
            todo["text"] = text_send.astype(F16)
        if k < len(others):
            todo["image"] = image_send.astype(F16)
        (todo,) = together(todo)
        half = b << k >> 1
        if k < len(text_bits):
            text_come = swap(text_bits[k : k + 1], todo["text"])
            if k:
                body, extra = add_message(text_keep, text_come)
                text_keep, text_send = (body[:half], extra), jnp.concatenate([body[half:], extra])
        if k < len(others):
            image_come = swap(others[k : k + 1], todo["image"])
            if k:
                body, extra = add_message(image_keep, image_come)
                image_keep, image_send = (body[:half], extra), jnp.concatenate([body[half:], extra])
    image_grad, text_grad, loss = call(
        last_kernel, [((b, sw), F32), ((b, sw), F32), ((1, 1), F32)],
        [*image_keep, image_come.astype(F32), image_back, *text_keep, text_come.astype(F32), text_back],
    )
    return (loss.reshape(()), image_grad, text_grad)


def solution(mesh):
    bits = {axis: [f"{axis}{k}" for k in reversed(range(mesh.shape[axis].bit_length() - 1))] for axis in ("img", "txt")}
    names = bits["img"] + bits["txt"]
    cube = Mesh(np.asarray(mesh.devices).reshape((2,) * len(names)), names)
    image_bits = bits["img"][:-1] + [x for x in bits["txt"] if int(x[3:]) % 2 == 0]
    text_bits = [x for x in names if x not in image_bits]
    image, text = P(tuple(names), None), P(tuple(bits["txt"] + bits["img"]), None)
    return jax.shard_map(
        functools.partial(local, tuple(image_bits), tuple(text_bits)),
        mesh=cube,
        in_specs=(image, text, image, text),
        out_specs=(P(), image, text),
        check_vma=False,
    )
```

```python
import functools
import math

import jax
import jax.numpy as jnp
import numpy as np
from jax import lax
from jax.experimental import pallas as pl
from jax.experimental.pallas import tpu as pltpu
from jax.sharding import Mesh, PartitionSpec as P

F32 = jnp.float32
BF16 = jnp.bfloat16
F16 = jnp.float16
LOG2E = 1.4426950408889634
LN2 = 0.6931471805599453
LINES = 8
KINDS = 3
EXTRA = 16
DIGITS = (64.0, 2.0**-4, 2.0**-14, 2.0**-24, 2.0**-34)
MOST = 60 * 2**20
ROOM = 12 * 2**20
VMEM = pl.BlockSpec(memory_space=pltpu.VMEM)
SMEM = pl.BlockSpec(memory_space=pltpu.SMEM)


def matmul(a, b, da, db):
    return lax.dot_general(a, b, (((da,), (db,)), ((), ())), preferred_element_type=F32)


def block(k, b):
    return slice(k * b, (k + 1) * b)


def stack_rows(values, shape, axis, first=0):
    index = lax.broadcasted_iota(jnp.int32, shape, axis) - first
    out = jnp.zeros(shape, F32)
    for k, value in enumerate(values):
        out = jnp.where(index == k, value, out)
    return out


def tree(op, items):
    while len(items) > 1:
        items = [op(x, y) for x, y in zip(items[::2], items[1::2])]
    return items[0]


def stats_kernel(nr, nc, b, tw, scale_t, scale_s, core, *refs):
    images, texts, refs = refs[:nr], refs[nr : nr + nc], refs[nr + nc :]
    tl_ref, sl_ref, row_ref, swap_ref, peak_ref, image_s, text_s, text_t = refs
    for p in range(nc):
        text_t[block(p, b), :] = texts[p][:, :tw]
        text_s[block(p, b), :] = texts[p][:, tw:]
    for p in range(nr):
        image_s[block(p, b), :] = images[p][:, tw:]
    largest = jnp.max(jnp.abs(text_s[...].astype(F32)), 0, keepdims=True)
    width = largest.shape[1]

    def with_largest(flat, k):
        if (k + 1) * b > width:
            return flat
        return flat + stack_rows((largest[:, block(k, b)],), flat.shape, 0, 2 * KINDS + core[0])

    step = 2 if nr % 2 == 0 else 1
    count = step * b
    peak_t = peak_s = None
    for p in range(0, nr, step):
        rows = slice(p * b, p * b + count)
        tl = matmul(jnp.concatenate([x[:, :tw] for x in images[p : p + step]], 0), text_t[...], 1, 1) * (scale_t * LOG2E)
        sl = matmul(image_s[rows, :], text_s[...], 1, 1) * (scale_s * LOG2E)
        tl_ref[rows, :] = tl
        sl_ref[rows, :] = sl
        top_t, top_s = jnp.max(tl, 0, keepdims=True), jnp.max(sl, 0, keepdims=True)
        peak_t = top_t if peak_t is None else jnp.maximum(peak_t, top_t)
        peak_s = top_s if peak_s is None else jnp.maximum(peak_s, top_s)
        mt, ms = jnp.max(tl, 1, keepdims=True), jnp.max(sl, 1, keepdims=True)
        et = jnp.exp2(tl - mt)
        sum_t = jnp.sum(et, 1, keepdims=True)
        gap = jnp.sum(et * (tl - sl), 1, keepdims=True)
        sum_s = jnp.sum(jnp.exp2(sl - ms), 1, keepdims=True)
        lines = (mt + jnp.log2(sum_t), ms + jnp.log2(sum_s), gap / sum_t)
        lines = stack_rows(lines, (count, 128), 1, core[0] * KINDS)
        for k in range(step):
            flat = jnp.transpose(lines[block(k, b)])[:LINES]
            other = (p + k) ^ (nr // 2)
            row_ref[:, block(p + k, b)] = with_largest(flat, p + k)
            swap_ref[:, block(other, b)] = with_largest(flat, other)
    peak_ref[...] = stack_rows((peak_t, peak_s), peak_ref.shape, 0)


def column_kernel(step, tl_ref, sl_ref, peaks, image, col_ref):
    peak_t, peak_s = peaks[0:1, :], peaks[1:2, :]
    sums = None
    for k in range(0, tl_ref.shape[0], step):
        tl, sl = tl_ref[k : k + step, :], sl_ref[k : k + step, :]
        et = jnp.exp2(tl - peak_t)
        parts = [jnp.sum(x, 0, keepdims=True) for x in (et, jnp.exp2(sl - peak_s), et * (tl - sl))]
        sums = parts if sums is None else [x + y for x, y in zip(sums, parts)]
    most = jnp.max(jnp.abs(image[...].astype(F32)), 0, keepdims=True)
    if col_ref.shape[1] > most.shape[1]:
        most = jnp.concatenate([most, jnp.zeros((1, col_ref.shape[1] - most.shape[1]), F32)], 1)
    lines = (peak_t + jnp.log2(sums[0]), peak_s + jnp.log2(sums[1]), sums[2] / sums[0], most)
    col_ref[...] = stack_rows(lines, col_ref.shape, 0)


def join_kernel(teacher, student, both):
    tw = teacher.shape[1]
    both[:, :tw] = teacher[...]
    both[:, tw:] = student[...]


def send_kernel(teacher_image, student_image, teacher_text, student_text, image, text, sems):
    tw = teacher_image.shape[1]
    copies = [
        pltpu.make_async_copy(teacher_image, image.at[:, :tw], sems.at[0]),
        pltpu.make_async_copy(student_image, image.at[:, tw:], sems.at[1]),
        pltpu.make_async_copy(teacher_text, text.at[:, :tw], sems.at[2]),
        pltpu.make_async_copy(student_text, text.at[:, tw:], sems.at[3]),
    ]
    for copy in copies:
        copy.start()
    for copy in copies:
        copy.wait()


def digits(share, rank, slots, width):
    rows = []
    for unit in DIGITS:
        digit = jnp.floor(share * (1.0 / unit))
        share = share - digit * unit
        rows.append(digit)
    lane = lax.broadcasted_iota(jnp.int32, (EXTRA, width), 1)
    return jnp.where(lane // (width // slots) == rank, stack_rows(rows, (EXTRA, width), 0), 0.0)


def combine(tiles, terms):
    lses = []
    for kind in (1, 0):
        peak = tree(jnp.maximum, [x[kind] for x in tiles])
        weights = [jnp.exp2(x[kind] - peak) for x in tiles]
        total = tree(jnp.add, weights)
        lses.append(peak + jnp.log2(total))
    for k, (w, x) in enumerate(zip(weights, tiles)):
        terms[k : k + 1, :] = w * x[2]
    gap = tree(jnp.add, [terms[k : k + 1, :] for k in range(len(tiles))])
    return lses[1], lses[0], gap / total + (lses[0] - lses[1])


def sum_blocks(x, b):
    parts = [jnp.sum(x[:, block(p, b)], axis=(0, 1), keepdims=True) for p in range(x.shape[1] // b)]
    return tree(jnp.add, parts) * LN2


def powers(largest, pairs, scale):
    bound = functools.reduce(jnp.maximum, largest) * ((1 + pairs) * scale)
    power = jnp.ceil(jnp.log2(jnp.maximum(bound, 1e-30)))
    return jnp.exp2(15.0 - power) * scale, jnp.exp2(power - 15.0)


def split_lines(refs, n):
    views = []
    while len(views) < n:
        views += [refs[0].at[block(k, LINES), :] for k in range(refs[0].shape[0] // LINES)]
        refs = refs[1:]
    return views, refs


def delta_kernel(nr, nc, b, pairs, scale, place, *refs):
    text, tl_ref, sl_ref, refs = *refs[:3], refs[3:]
    row_parts, refs = split_lines(refs, nr // 2)
    col_parts, refs = split_lines(refs, nc)
    other_near, other_far, high_ref, low_ref, refs = *refs[:4], refs[4:]
    image_back_ref, text_back_ref, scale_ref, image_extra, text_extra, row_terms, col_terms = refs
    width = image_back_ref.shape[1]
    lines = [x[2 * KINDS + core : 2 * KINDS + core + 1, :width] for x in row_parts for core in range(2)]
    image_scale, image_back = powers(lines, pairs, scale)
    text_scale, text_back = powers([x[KINDS : KINDS + 1, :width] for x in col_parts], pairs, scale)
    image_back_ref[...] = image_back
    text_back_ref[...] = text_back
    scale_ref[...] = stack_rows((image_scale, text_scale), scale_ref.shape, 0)
    tiles = []
    for q in range(nr // 2):
        x = jnp.concatenate([row_parts[q][:, block(p ^ q, b)] for p in range(nr)], 1)
        for core in range(2):
            tiles.append([x[core * KINDS + k : core * KINDS + k + 1, :] for k in range(KINDS)])
    row_t, row_s, terms = combine(tiles, row_terms)
    row_share = sum_blocks(terms, b)
    rows = stack_rows((row_t, row_s), (LINES, nr * b), 0)
    tiles = []
    for q in range(nc):
        x = jnp.concatenate([col_parts[q][:, block(p ^ q, b)] for p in range(nc)], 1)
        tiles.append([x[k : k + 1, :] for k in range(KINDS)])
    col_t, col_s, terms = combine(tiles, col_terms)
    col_share = sum_blocks(terms, b)
    for p in range(nr):
        row = jnp.transpose(rows[:, block(p, b)])
        tl, sl = tl_ref[block(p, b), :], sl_ref[block(p, b), :]
        delta = (jnp.exp2(sl - row[:, 1:2]) - jnp.exp2(tl - row[:, 0:1])) + (
            jnp.exp2(sl - col_s) - jnp.exp2(tl - col_t)
        )
        high = delta.astype(BF16)
        high_ref[block(p, b), :] = high
        low_ref[block(p, b), :] = (delta - high.astype(F32)).astype(BF16)
    image_extra[...] = digits(col_share * (1.0 / (nc * b)), place[1], nr, width)
    text_extra[...] = digits(row_share * (1.0 / (nr * b)), place[2], nc, width)
    rows = nr * b // 4
    for n, ref in ((3, other_far), (2, other_near)):
        ref[:rows, :] = product(high_ref, low_ref, (block(n, rows), slice(None)), text, 1) * image_scale
        ref[rows:, :] = image_extra[...]


def product(high_ref, low_ref, place, other, dim):
    return matmul(high_ref[place], other[...], dim, 0) + matmul(low_ref[place], other[...], dim, 0)


def gradient_kernel(image, text, high_ref, low_ref, scale_ref, image_extra, text_extra, near, far, keep, send):
    rows, cols = near.shape[0] - EXTRA, keep.shape[0] - EXTRA
    for n, ref in ((1, far), (0, near)):
        ref[:rows, :] = product(high_ref, low_ref, (block(n, rows), slice(None)), text, 1) * scale_ref[0:1, :]
        ref[rows:, :] = image_extra[...]
    for n, ref in ((1, send), (0, keep)):
        ref[:cols, :] = product(high_ref, low_ref, (slice(None), block(n, cols)), image, 0) * scale_ref[1:2, :]
        ref[cols:, :] = text_extra[...]


def last_kernel(*refs):
    (image, image_extra, image_come, image_back), (text, text_extra, text_come, text_back) = refs[:4], refs[4:8]
    image_grad, text_grad, loss = refs[8:]
    rows, width = image.shape
    image_grad[...] = (image[...] + image_come[:rows, :]) * image_back[...]
    text_grad[...] = (text[...] + text_come[:rows, :]) * text_back[...]
    counts = (image_extra[...] + image_come[rows:, :]) + (text_extra[...] + text_come[rows:, :])
    counts = counts * stack_rows(DIGITS, counts.shape, 0)
    loss[...] = jnp.sum(counts, axis=(0, 1), keepdims=True) * (0.5 / width)


def call(kernel, outs, args, scratch=(), flops=0, transcendentals=0):
    shapes = [jax.ShapeDtypeStruct(s, d) for s, d in outs]
    size = sum(x.size * x.dtype.itemsize for x in list(args) + shapes)
    held = sum(math.prod(s) * jnp.dtype(d).itemsize for s, d in scratch)
    return pl.pallas_call(
        kernel,
        out_shape=shapes,
        in_specs=[SMEM if x.dtype == jnp.int32 else VMEM for x in args],
        out_specs=[VMEM] * len(shapes),
        scratch_shapes=[pltpu.VMEM(s, d) for s, d in scratch],
        compiler_params=pltpu.CompilerParams(vmem_limit_bytes=size + held + ROOM),
        cost_estimate=pl.CostEstimate(flops=flops, bytes_accessed=size, transcendentals=transcendentals),
    )(*args)


def swap(bits, x):
    perm = [(i, i ^ ((1 << len(bits)) - 1)) for i in range(1 << len(bits))]
    return lax.ppermute(x, bits, perm)


def subset(bits, q):
    return tuple(b for k, b in enumerate(bits) if q >> k & 1)


def together(*groups):
    return lax.optimization_barrier(groups)


def gather(bits, x):
    blocks = [x]
    for k, bit in enumerate(bits):
        own = together(x, blocks[2])[0] if k > 1 else x
        blocks = blocks + [swap((bit,), y) for y in [own] + blocks[1:]]
    return blocks


def exchange(bits, x):
    parts = [x]
    for bit in bits:
        parts.append(swap((bit,), jnp.concatenate(parts) if len(parts) > 1 else x))
    return parts


def add_message(keep, come):
    rows = keep[0].shape[0]
    come = come.astype(F32)
    return keep[0] + come[:rows], keep[1] + come[rows:]


def local(image_bits, text_bits, teacher_image, teacher_text, student_image, student_text):
    b, tw = teacher_image.shape
    sw = student_image.shape[1]
    nr, nc = 1 << len(image_bits), 1 << len(text_bits)
    r, c = nr * b, nc * b
    pair, others = image_bits[-1:], image_bits[:-1]
    whole = jax.ShapeDtypeStruct((b, tw + sw), BF16)
    image, text = pl.pallas_call(
        send_kernel,
        out_shape=[whole, whole],
        in_specs=[pl.BlockSpec(memory_space=pltpu.HBM)] * 4,
        out_specs=[VMEM] * 2,
        scratch_shapes=[pltpu.SemaphoreType.DMA((4,))],
        compiler_params=pltpu.CompilerParams(vmem_limit_bytes=MOST),
    )(teacher_image, student_image, teacher_text, student_text)
    images, texts = gather(image_bits, image), gather(text_bits, text)
    own = together([teacher_image, student_image, teacher_text, student_text], [images[2], texts[2]])[0]
    (images[0],) = call(join_kernel, [((b, tw + sw), BF16)], own[:2])
    (texts[0],) = call(join_kernel, [((b, tw + sw), BF16)], own[2:])
    place = jnp.stack([lax.axis_index(x) for x in (pair, image_bits, text_bits)]).astype(jnp.int32)
    tl, sl, rows, rows_swapped, peaks, image, text = call(
        functools.partial(stats_kernel, nr, nc, b, tw, tw**-0.5, sw**-0.5),
        [((r, c), F32), ((r, c), F32), ((LINES, r), F32), ((LINES, r), F32), ((LINES, c), F32), ((r, sw), BF16), ((c, sw), BF16)],
        [place] + images + texts, [((c, tw), BF16)], 2 * r * c * (tw + sw), 4 * r * c,
    )
    other = swap(pair, rows_swapped)
    (cols,) = call(
        functools.partial(column_kernel, 2 * b), [((LINES, c), F32)], [tl, sl, peaks, image], (), 0, 2 * r * c
    )
    row_parts, col_parts = exchange(others, together(rows, cols)[0] + other), exchange(text_bits, cols)
    pairs = b << (len(image_bits) + len(text_bits))
    row, extra = ((1, sw), F32), ((EXTRA, sw), F32)
    near_shape, keep_shape = ((r // 4 + EXTRA, sw), F32), ((c // 2 + EXTRA, sw), F32)
    other_near, other_far, high, low, image_back, text_back, *more = call(
        functools.partial(delta_kernel, nr, nc, b, pairs, sw**-0.5),
        [near_shape, near_shape, ((r, c), BF16), ((r, c), BF16), row, row, ((8, sw), F32), extra, extra],
        [place, text, tl, sl] + row_parts + col_parts,
        [((nr, r), F32), ((max(nc, 8), c), F32)], 2 * r * c * sw, 4 * r * c,
    )
    other_far, other_near = swap(pair, other_far), swap(pair, other_near)
    near, far, text_keep, text_send = call(
        gradient_kernel, [near_shape, near_shape, keep_shape, keep_shape], [image, text, high, low] + more, (), 6 * r * c * sw
    )
    image_send = far + other_far
    image_keep = near + other_near
    image_keep, text_keep = [(x[:-EXTRA], x[-EXTRA:]) for x in (image_keep, text_keep)]
    for k in reversed(range(max(len(text_bits), len(others)))):
        todo = {}
        if k < len(text_bits):
            todo["text"] = text_send.astype(F16)
        if k < len(others):
            todo["image"] = image_send.astype(F16)
        (todo,) = together(todo)
        half = b << k >> 1
        if k < len(text_bits):
            text_come = swap(text_bits[k : k + 1], todo["text"])
            if k:
                body, extra = add_message(text_keep, text_come)
                text_keep, text_send = (body[:half], extra), jnp.concatenate([body[half:], extra])
        if k < len(others):
            image_come = swap(others[k : k + 1], todo["image"])
            if k:
                body, extra = add_message(image_keep, image_come)
                image_keep, image_send = (body[:half], extra), jnp.concatenate([body[half:], extra])
    image_grad, text_grad, loss = call(
        last_kernel, [((b, sw), F32), ((b, sw), F32), ((1, 1), F32)],
        [*image_keep, image_come.astype(F32), image_back, *text_keep, text_come.astype(F32), text_back],
    )
    return (loss.reshape(()), image_grad, text_grad)


def solution(mesh):
    bits = {axis: [f"{axis}{k}" for k in reversed(range(mesh.shape[axis].bit_length() - 1))] for axis in ("img", "txt")}
    names = bits["img"] + bits["txt"]
    cube = Mesh(np.asarray(mesh.devices).reshape((2,) * len(names)), names)
    image_bits = bits["img"][:-1] + [x for x in bits["txt"] if int(x[3:]) % 2 == 0]
    text_bits = [x for x in names if x not in image_bits]
    image, text = P(tuple(names), None), P(tuple(bits["txt"] + bits["img"]), None)
    return jax.shard_map(
        functools.partial(local, tuple(image_bits), tuple(text_bits)),
        mesh=cube,
        in_specs=(image, text, image, text),
        out_specs=(P(), image, text),
        check_vma=False,
    )
```
